32 devices in a mesh: clip: 8 (over z, x), band: 4 (over y, core).
Axes of the slice: x: 2, y: 2, z: 4, core: 2. Of those that a mesh axis runs over, the one named last changes fastest.
Arguments:
- visible: bfloat16 [128, 128, 768], P(('clip', 'band')), may hold values from -6 to 6
- keep_index: int32 [128, 128], P(('clip', 'band')), may hold values from 0 to 511, as said below
- visible_count: int32 [128], P(('clip', 'band')), may hold values from 52 to 128, as said below
- enc_gain1: bfloat16 [768], P(('clip', 'band')), may hold values from 0.5 to 1.5
- enc_shift1: bfloat16 [768], P(('clip', 'band')), may hold values from -4 to 4
- enc_qkv: bfloat16 [768, 2304], P(('clip', 'band')), may hold values from -0.21875 to 0.21875
- enc_out: bfloat16 [768, 768], P(('clip', 'band')), may hold values from -0.625 to 0.625
- enc_gain2: bfloat16 [768], P(('clip', 'band')), may hold values from 0.5 to 1.5
- enc_shift2: bfloat16 [768], P(('clip', 'band')), may hold values from -4 to 4
- enc_up: bfloat16 [768, 3072], P(('clip', 'band')), may hold values from -0.21875 to 0.21875
- enc_down: bfloat16 [3072, 768], P(('clip', 'band')), may hold values from -0.15625 to 0.15625
- proj: bfloat16 [768, 512], P(('clip', 'band')), may hold values from -0.4375 to 0.4375
- mask_token: bfloat16 [512], P(('clip', 'band')), may hold values from -6 to 6
- dec_gain1: bfloat16 [512], P(('clip', 'band')), may hold values from 0.5 to 1.5
- dec_shift1: bfloat16 [512], P(('clip', 'band')), may hold values from -4 to 4
- dec_qkv: bfloat16 [512, 1536], P(('clip', 'band')), may hold values from -0.25 to 0.25
- dec_out: bfloat16 [512, 512], P(('clip', 'band')), may hold values from -0.5 to 0.5
- dec_gain2: bfloat16 [512], P(('clip', 'band')), may hold values from 0.5 to 1.5
- dec_shift2: bfloat16 [512], P(('clip', 'band')), may hold values from -4 to 4
- dec_up: bfloat16 [512, 2048], P(('clip', 'band')), may hold values from -0.25 to 0.25
- dec_down: bfloat16 [2048, 512], P(('clip', 'band')), may hold values from -0.1875 to 0.1875
- cotangent: bfloat16 [32, 8, 64, 4, 512], P(('clip', 'band')), may hold values from -6 to 6
Outputs:
- decoded: bfloat16 [32, 8, 64, 4, 512], P(('clip', 'band'))
- visible_grad: bfloat16 [128, 128, 768], P(('clip', 'band'))
- enc_gain1_grad: float32 [768], replicated
- enc_shift1_grad: float32 [768], replicated
- enc_qkv_grad: float32 [768, 2304], replicated
- enc_out_grad: float32 [768, 768], replicated
- enc_gain2_grad: float32 [768], replicated
- enc_shift2_grad: float32 [768], replicated
- enc_up_grad: float32 [768, 3072], replicated
- enc_down_grad: float32 [3072, 768], replicated
- proj_grad: float32 [768, 512], replicated
- mask_token_grad: float32 [512], replicated
- dec_gain1_grad: float32 [512], replicated
- dec_shift1_grad: float32 [512], replicated
- dec_qkv_grad: float32 [512, 1536], replicated
- dec_out_grad: float32 [512, 512], replicated
- dec_gain2_grad: float32 [512], replicated
- dec_shift2_grad: float32 [512], replicated
- dec_up_grad: float32 [512, 2048], replicated
- dec_down_grad: float32 [2048, 512], replicated
The draws below stay inside these ranges and needn't reach their ends.
Inputs may be any that keep to these rules, and one draw needn't show every extreme that they name: `keep_index`: within a clip the 128 entries are distinct patch numbers; the first visible_count of them are the visible patches. `visible_count`: the 4 clips of each encoder device include one with exactly 128 visible patches.
All inputs are finite; a program needn't handle non-finite values.
Results may differ from the reference program's by a relative error of at most 0.02.
Values may be sent and summed in bfloat16 or wider, within the bound.
No kernel may reach another device: no remote copies, remote signals or barrier semaphores. Data moves between devices by JAX's collectives and lax.ppermute only.
A program may use at most 320 MiB of HBM per device.

```python
import math
import jax
import jax.numpy as jnp
from jax import lax

D_ENC = 768
HEADS_ENC = 12
FF_ENC = 3072
D_DEC = 512
HEADS_DEC = 16
FF_DEC = 2048
CLIPS_DEV = 4
TIME = 64
FREQ = 8
VIS = 128
MIN_VIS = 52
WINDOW = 4
SHIFT = 2
HALF = 8
CLIPS = 128
N_CLIP = 8
N_BAND = 4


def draw_keep_index(key, part):
    key = jax.random.fold_in(key, 11)
    clip_keys = jax.random.split(key, CLIPS)
    chosen = jax.vmap(lambda subkey: jax.random.permutation(subkey, TIME * FREQ)[:VIS])(clip_keys)
    return chosen.astype(jnp.int32)


def draw_visible_count(key, part):
    key = jax.random.fold_in(key, 12)
    first_key, second_key = jax.random.split(key)
    counts = jax.random.randint(first_key, (CLIPS,), MIN_VIS, VIS + 1)
    full_slot = jax.random.randint(second_key, (CLIPS // CLIPS_DEV, 1), 0, CLIPS_DEV)
    marked = (jnp.arange(CLIPS_DEV)[None, :] == full_slot).reshape(-1)
    return jnp.where(marked, VIS, counts).astype(jnp.int32)


def levels(stream_key, extent, cuts, least, high):
    gain, own = 1.0, jax.random.fold_in(stream_key, 6)
    for dim, blocks in cuts:
        draws = jnp.exp(jax.random.uniform(jax.random.fold_in(own, dim), (blocks,), jnp.float32, least / len(cuts), high / len(cuts)))
        gain = gain * jnp.repeat(draws, extent[dim] // blocks).reshape([-1 if axis == dim else 1 for axis in range(len(extent))])
    return gain


def gaussian(stream_key, dims, scale, bound, cuts=(), held_as=jnp.bfloat16):
    result = scale * jax.random.normal(stream_key, dims, jnp.float32)
    if cuts:
        result = result * levels(stream_key, dims, cuts, -0.22, 0.18)
    return jnp.clip(result, -bound, bound).astype(held_as)


def setup_inputs(seed: int = 0) -> dict:
    streams_of = jax.random.split(jax.random.key(seed), 23)
    visible = gaussian(streams_of[0], (CLIPS, VIS, D_ENC), 1.0, 6.0, ((0, 32),))
    keep_index = draw_keep_index(jax.random.fold_in(streams_of[22], 71), 0)
    visible_count = draw_visible_count(jax.random.fold_in(streams_of[22], 71), 0)
    enc_gain1 = jnp.clip(1.0 + 0.1 * jax.random.normal(streams_of[3], (D_ENC,), jnp.float32), 0.5, 1.5).astype(jnp.bfloat16)
    enc_shift1 = gaussian(streams_of[4], (D_ENC,), 0.3, 4.0, ((0, 32),))
    enc_qkv = gaussian(streams_of[5], (D_ENC, 3 * D_ENC), D_ENC ** -0.5, 0.21875, ((0, 32),))
    enc_out = gaussian(streams_of[6], (D_ENC, D_ENC), (D_ENC // 8) ** -0.5, 0.625, ((0, 32),))
    enc_gain2 = jnp.clip(1.0 + 0.1 * jax.random.normal(streams_of[7], (D_ENC,), jnp.float32), 0.5, 1.5).astype(jnp.bfloat16)
    enc_shift2 = gaussian(streams_of[8], (D_ENC,), 0.3, 4.0, ((0, 32),))
    enc_up = gaussian(streams_of[9], (D_ENC, FF_ENC), D_ENC ** -0.5, 0.21875, ((0, 32),))
    enc_down = gaussian(streams_of[10], (FF_ENC, D_ENC), (FF_ENC // 2) ** -0.5, 0.15625, ((0, 32),))
    proj = gaussian(streams_of[11], (D_ENC, D_DEC), (D_ENC // 4) ** -0.5, 0.4375, ((0, 32),))
    mask_token = gaussian(streams_of[12], (D_DEC,), 1.0, 6.0, ((0, 32),))
    dec_gain1 = jnp.clip(1.0 + 0.1 * jax.random.normal(streams_of[13], (D_DEC,), jnp.float32), 0.5, 1.5).astype(jnp.bfloat16)
    dec_shift1 = gaussian(streams_of[14], (D_DEC,), 0.3, 4.0, ((0, 32),))
    dec_qkv = gaussian(streams_of[15], (D_DEC, 3 * D_DEC), D_DEC ** -0.5, 0.25, ((0, 32),))
    dec_out = gaussian(streams_of[16], (D_DEC, D_DEC), (D_DEC // 4) ** -0.5, 0.5, ((0, 32),))
    dec_gain2 = jnp.clip(1.0 + 0.1 * jax.random.normal(streams_of[17], (D_DEC,), jnp.float32), 0.5, 1.5).astype(jnp.bfloat16)
    dec_shift2 = gaussian(streams_of[18], (D_DEC,), 0.3, 4.0, ((0, 32),))
    dec_up = gaussian(streams_of[19], (D_DEC, FF_DEC), D_DEC ** -0.5, 0.25, ((0, 32),))
    dec_down = gaussian(streams_of[20], (FF_DEC, D_DEC), (FF_DEC // 2) ** -0.5, 0.1875, ((0, 32),))
    cotangent = gaussian(streams_of[21], (N_CLIP * N_BAND, HALF, TIME, FREQ // 2, D_DEC), 1.0, 6.0, ((0, 32),))
    return {"visible": visible, "keep_index": keep_index, "visible_count": visible_count, "enc_gain1": enc_gain1, "enc_shift1": enc_shift1, "enc_qkv": enc_qkv, "enc_out": enc_out, "enc_gain2": enc_gain2, "enc_shift2": enc_shift2, "enc_up": enc_up, "enc_down": enc_down, "proj": proj, "mask_token": mask_token, "dec_gain1": dec_gain1, "dec_shift1": dec_shift1, "dec_qkv": dec_qkv, "dec_out": dec_out, "dec_gain2": dec_gain2, "dec_shift2": dec_shift2, "dec_up": dec_up, "dec_down": dec_down, "cotangent": cotangent}


exact_prec = lax.Precision.HIGHEST
norm_eps = 1e-06
neg_fill = -1e+30

@jax.custom_vjp
def low(v):
    return lax.optimization_barrier(v.astype(jnp.bfloat16)).astype(jnp.float32)

@jax.custom_vjp
def low_back(v):
    return v

def low_keep(v):
    return (low(v), None)

def low_pass(kept, grad):
    return (grad,)

def back_keep(v):
    return (v, None)

def back_low(kept, grad):
    return (low(grad),)
low.defvjp(low_keep, low_pass)
low_back.defvjp(back_keep, back_low)

def rounded_both(tensor):
    return low_back(low(tensor))

def layer_norm(inputs, gain_vec, shift_vec):
    centre = lax.optimization_barrier(jnp.mean(inputs, axis=-1, keepdims=True))
    centred = inputs - centre
    spread = lax.optimization_barrier(jnp.mean(centred * centred, axis=-1, keepdims=True))
    return centred * lax.rsqrt(spread + norm_eps) * gain_vec + shift_vec

def project(operand, weight):
    return jnp.einsum('...d,de->...e', operand, weight, precision=exact_prec)

def position_table(places):
    half_width = D_DEC // 2
    omega_vec = jnp.exp(jnp.arange(half_width, dtype=jnp.float32) * (-math.log(10000.0) / half_width))
    angles = places.astype(jnp.float32)[..., None] * omega_vec
    return jnp.concatenate([jnp.sin(angles), jnp.cos(angles)], axis=-1)

def window_allowed():
    time_wrap = (jnp.arange(TIME) >= TIME - SHIFT).astype(jnp.int32)
    freq_wrap = (jnp.arange(FREQ) >= FREQ - SHIFT).astype(jnp.int32)
    labels = time_wrap[:, None] * 2 + freq_wrap[None, :]
    labels = labels.reshape(TIME // WINDOW, WINDOW, FREQ // WINDOW, WINDOW).transpose(0, 2, 1, 3)
    labels = labels.reshape(-1, WINDOW * WINDOW)
    return labels[:, :, None] == labels[:, None, :]

def attention(normed, weight_qkv, weight_out, head_count, allowed):
    batch_size, length, model_width = normed.shape
    head_dim = model_width // head_count
    qkv_rows = rounded_both(project(normed, weight_qkv)).reshape(batch_size, length, 3, head_count, head_dim)
    queries, key_heads, values = (qkv_rows[:, :, 0], qkv_rows[:, :, 1], qkv_rows[:, :, 2])
    raw_scores = low_back(jnp.einsum('bqhd,bkhd->bhqk', queries, key_heads, precision=exact_prec))
    scores = jnp.where(allowed, raw_scores * head_dim ** (-0.5), neg_fill)
    row_top = lax.optimization_barrier(jnp.max(scores, axis=-1, keepdims=True))
    exp_scores = jnp.exp(scores - row_top)
    attn_prob = exp_scores / lax.optimization_barrier(jnp.sum(exp_scores, axis=-1, keepdims=True))
    mixed_heads = jnp.einsum('bhqk,bkhd->bqhd', low(attn_prob), values, precision=exact_prec)
    mixed_heads = rounded_both(mixed_heads.reshape(batch_size, length, model_width))
    return low_back(project(mixed_heads, weight_out))

def block(inputs, params, head_count, allowed):
    gain_one, shift_one, weight_qkv, weight_out, gain_two, shift_two, weight_up, weight_down = params
    normed = low(layer_norm(inputs, gain_one, shift_one))
    middle = inputs + attention(normed, weight_qkv, weight_out, head_count, allowed)
    normed_two = low(layer_norm(middle, gain_two, shift_two))
    hidden = low(jax.nn.gelu(low_back(project(normed_two, weight_up)), approximate=False))
    return middle + low_back(project(hidden, weight_down))

def clip_forward(weights, visible, keep_index, visible_count):
    enc_params, weight_proj, mask_vec, dec_params = weights
    clip_count = visible.shape[0]
    slot_ids = jnp.arange(VIS)
    valid_rows = slot_ids[None, :] < visible_count[:, None]
    encoded = block(visible, enc_params, HEADS_ENC, valid_rows[:, None, None, :])
    sent_rows = rounded_both(project(low(encoded), weight_proj))
    places = jnp.arange(TIME * FREQ)
    onehot = (keep_index[:, :, None] == places[None, None, :]).astype(jnp.float32)
    onehot = onehot * valid_rows.astype(jnp.float32)[:, :, None]
    grid_rows = jnp.einsum('cip,cid->cpd', onehot, sent_rows, precision=exact_prec)
    seen_mask = lax.optimization_barrier(jnp.sum(onehot, axis=1))[:, :, None]
    filled = seen_mask * grid_rows + (1.0 - seen_mask) * mask_vec + position_table(places)
    rolled = jnp.roll(filled.reshape(clip_count, TIME, FREQ, D_DEC), (-SHIFT, -SHIFT), (1, 2))
    windows = rolled.reshape(clip_count, TIME // WINDOW, WINDOW, FREQ // WINDOW, WINDOW, D_DEC)
    windows = windows.transpose(0, 1, 3, 2, 4, 5).reshape(-1, WINDOW * WINDOW, D_DEC)
    allowed = jnp.tile(window_allowed(), (clip_count, 1, 1))[:, None]
    decoded = block(windows, dec_params, HEADS_DEC, allowed)
    decoded = decoded.reshape(clip_count, TIME // WINDOW, FREQ // WINDOW, WINDOW, WINDOW, D_DEC)
    return decoded.transpose(0, 1, 3, 2, 4, 5).reshape(clip_count, TIME, FREQ, D_DEC)

def forward(weights, visible, keep_index, visible_count):
    group_size = 8
    block_count = CLIPS // group_size
    blocked = (visible.reshape(block_count, group_size, VIS, D_ENC), keep_index.reshape(block_count, group_size, VIS), visible_count.reshape(block_count, group_size))
    runner = jax.checkpoint(lambda batch_items: clip_forward(weights, batch_items[0], batch_items[1], batch_items[2]))
    decoded = lax.map(runner, blocked)
    decoded = decoded.reshape(N_CLIP, N_BAND, 2, CLIPS_DEV // 2, TIME, 2, FREQ // 2, D_DEC)
    decoded = decoded.transpose(0, 2, 5, 1, 3, 4, 6, 7)
    return decoded.reshape(N_CLIP * N_BAND, HALF, TIME, FREQ // 2, D_DEC)

def to_float(tensor):
    return tensor.astype(jnp.float32)

def reference(visible, keep_index, visible_count, enc_gain1, enc_shift1, enc_qkv, enc_out, enc_gain2, enc_shift2, enc_up, enc_down, proj, mask_token, dec_gain1, dec_shift1, dec_qkv, dec_out, dec_gain2, dec_shift2, dec_up, dec_down, cotangent):
    enc_params = tuple((to_float(tensor) for tensor in (enc_gain1, enc_shift1, enc_qkv, enc_out, enc_gain2, enc_shift2, enc_up, enc_down)))
    dec_params = tuple((to_float(tensor) for tensor in (dec_gain1, dec_shift1, dec_qkv, dec_out, dec_gain2, dec_shift2, dec_up, dec_down)))
    weights = (enc_params, to_float(proj), to_float(mask_token), dec_params)

    def run_layers(weights_in, visible_in):
        return forward(weights_in, visible_in, keep_index, visible_count)
    decoded, pull_back = jax.vjp(run_layers, weights, to_float(visible))
    weight_grads, visible_grad = pull_back(to_float(cotangent))
    enc_grads, proj_grad, mask_grad, dec_grads = weight_grads
    return (decoded.astype(jnp.bfloat16), visible_grad.astype(jnp.bfloat16), enc_grads[0], enc_grads[1], enc_grads[2], enc_grads[3], enc_grads[4], enc_grads[5], enc_grads[6], enc_grads[7], proj_grad, mask_grad, dec_grads[0], dec_grads[1], dec_grads[2], dec_grads[3], dec_grads[4], dec_grads[5], dec_grads[6], dec_grads[7])
```

```python
import math

import jax
import jax.numpy as jnp
from jax import lax
from jax.sharding import PartitionSpec as P

HEADS_ENC = 12
D_DEC = 512
HEADS_DEC = 16
TIME = 64
FREQ = 8
WINDOW = 4
SHIFT = 2


norm_eps = 1e-06
neg_fill = -1e30


def layer_norm(inputs, gain_vec, shift_vec):
    centre = jnp.mean(inputs, axis=-1, keepdims=True)
    centred = inputs - centre
    spread = jnp.mean(centred * centred, axis=-1, keepdims=True)
    return centred * lax.rsqrt(spread + norm_eps) * gain_vec + shift_vec


def position_table(places):
    half_width = D_DEC // 2
    omega_vec = jnp.exp(
        jnp.arange(half_width, dtype=jnp.float32) * (-math.log(10000.0) / half_width)
    )
    angles = places.astype(jnp.float32)[..., None] * omega_vec
    return jnp.concatenate([jnp.sin(angles), jnp.cos(angles)], axis=-1)


def forward_dot(operand, weight):
    return jnp.einsum("nd,de->ne", operand, weight, preferred_element_type=jnp.float32)


def backward_dot(gradient, weight):
    return jnp.einsum("ne,de->nd", gradient, weight, preferred_element_type=jnp.float32)


def weight_dot(operand, gradient):
    return jnp.einsum("nd,ne->de", operand, gradient, preferred_element_type=jnp.float32)


def exact_gelu(inputs):
    return jax.nn.gelu(inputs, approximate=False)


def block_forward(inputs, weights, head_count, allowed):
    batch_size, length, model_width = inputs.shape
    head_dim = model_width // head_count
    flat_rows = inputs.reshape(-1, model_width)
    normed, norm_back_one = jax.vjp(
        layer_norm, flat_rows, weights[0].astype(jnp.float32), weights[1].astype(jnp.float32)
    )
    normed = normed.astype(jnp.bfloat16)
    qkv_rows = (
        forward_dot(normed, weights[2])
        .astype(jnp.bfloat16)
        .reshape(batch_size, length, 3, head_count, head_dim)
    )
    queries, key_heads, values = (qkv_rows[:, :, 0], qkv_rows[:, :, 1], qkv_rows[:, :, 2])
    raw_scores = jnp.einsum(
        "bqhd,bkhd->bhqk", queries, key_heads, preferred_element_type=jnp.float32
    )
    scores = jnp.where(allowed, raw_scores * head_dim ** (-0.5), neg_fill)
    row_top = jnp.max(scores, axis=-1, keepdims=True)
    exp_scores = jnp.exp(scores - row_top)
    row_total = jnp.sum(exp_scores, axis=-1, keepdims=True)
    attn_prob = exp_scores / row_total
    log_total = row_top + jnp.log(row_total)
    mixed_heads = jnp.einsum(
        "bhqk,bkhd->bqhd",
        attn_prob.astype(jnp.bfloat16),
        values,
        preferred_element_type=jnp.float32,
    )
    mixed_heads = mixed_heads.astype(jnp.bfloat16).reshape(-1, model_width)
    middle = flat_rows + forward_dot(mixed_heads, weights[3])
    normed_two, norm_back_two = jax.vjp(
        layer_norm, middle, weights[4].astype(jnp.float32), weights[5].astype(jnp.float32)
    )
    normed_two = normed_two.astype(jnp.bfloat16)
    pre_gelu = forward_dot(normed_two, weights[6])
    hidden = exact_gelu(pre_gelu).astype(jnp.bfloat16)
    output = middle + forward_dot(hidden, weights[7])
    stored = (
        norm_back_one,
        normed,
        queries,
        key_heads,
        values,
        log_total,
        mixed_heads,
        norm_back_two,
        normed_two,
        pre_gelu,
        hidden,
    )
    return (output.reshape(inputs.shape), stored)


def block_backward(cotangent_in, stored, weights, head_count, allowed):
    (
        norm_back_one,
        normed,
        queries,
        key_heads,
        values,
        log_total,
        mixed_heads,
        norm_back_two,
        normed_two,
        pre_gelu,
        hidden,
    ) = stored
    batch_size, length, model_width = cotangent_in.shape
    head_dim = model_width // head_count
    upstream = cotangent_in.reshape(-1, model_width)
    upstream_low = upstream.astype(jnp.bfloat16)
    grad_down = weight_dot(hidden, upstream_low)
    grad_hidden = backward_dot(upstream_low, weights[7])
    gelu_back = jax.vjp(exact_gelu, pre_gelu)[1]
    grad_pre = gelu_back(grad_hidden)[0].astype(jnp.bfloat16)
    grad_up = weight_dot(normed_two, grad_pre)
    from_norm_two, grad_gain_two, grad_shift_two = norm_back_two(backward_dot(grad_pre, weights[6]))
    grad_middle = upstream + from_norm_two
    middle_low = grad_middle.astype(jnp.bfloat16)
    grad_out = weight_dot(mixed_heads, middle_low)
    grad_mixed = (
        backward_dot(middle_low, weights[3])
        .astype(jnp.bfloat16)
        .reshape(batch_size, length, head_count, head_dim)
    )
    raw_scores = jnp.einsum(
        "bqhd,bkhd->bhqk", queries, key_heads, preferred_element_type=jnp.float32
    )
    scores = jnp.where(allowed, raw_scores * head_dim ** (-0.5), neg_fill)
    attn_prob = jnp.exp(scores - log_total)
    grad_prob = jnp.einsum(
        "bqhd,bkhd->bhqk", grad_mixed, values, preferred_element_type=jnp.float32
    )
    grad_values = jnp.einsum(
        "bhqk,bqhd->bkhd",
        attn_prob.astype(jnp.bfloat16),
        grad_mixed,
        preferred_element_type=jnp.float32,
    )
    grad_scores = attn_prob * (grad_prob - jnp.sum(attn_prob * grad_prob, axis=-1, keepdims=True))
    grad_raw = (grad_scores * head_dim ** (-0.5)).astype(jnp.bfloat16)
    grad_queries = jnp.einsum(
        "bhqk,bkhd->bqhd", grad_raw, key_heads, preferred_element_type=jnp.float32
    )
    grad_keys = jnp.einsum("bhqk,bqhd->bkhd", grad_raw, queries, preferred_element_type=jnp.float32)
    grad_qkv_rows = (
        jnp.stack([grad_queries, grad_keys, grad_values], axis=2)
        .astype(jnp.bfloat16)
        .reshape(-1, 3 * model_width)
    )
    grad_qkv = weight_dot(normed, grad_qkv_rows)
    from_norm_one, grad_gain_one, grad_shift_one = norm_back_one(
        backward_dot(grad_qkv_rows, weights[2])
    )
    grad_inputs = grad_middle + from_norm_one
    return (
        grad_inputs.reshape(cotangent_in.shape),
        (
            grad_gain_one,
            grad_shift_one,
            grad_qkv,
            grad_out,
            grad_gain_two,
            grad_shift_two,
            grad_up,
            grad_down,
        ),
    )


AXES = ("clip", "band")


def split_bits(parts):
    return parts.bit_length() - 1


def bit_order(count):
    first = [0, 2, 1][: min(count, 3)]
    first = [b for b in first if b < count]
    rest = [b for b in range(count - 1, -1, -1) if b not in first]
    return first + rest


def swap_order(order):
    if len(order) < 3:
        return order
    return [order[0], order[2], order[1]] + order[3:]


def partner_pairs(total, bit):
    return [(i, i ^ (1 << bit)) for i in range(total)]


def scatter_sum(partial, total, order):
    me = lax.axis_index(AXES)
    left = list(range(split_bits(total) - 1, -1, -1))
    rows = partial.shape[0] // total
    held = partial.reshape((2,) * len(left) + (rows,) + partial.shape[1:])
    for bit in order:
        place = left.index(bit)
        mine = (me >> bit) & 1
        keep = lax.dynamic_index_in_dim(held, mine, place, keepdims=False)
        give = lax.dynamic_index_in_dim(held, 1 - mine, place, keepdims=False).astype(jnp.bfloat16)
        got = lax.ppermute(give, AXES, partner_pairs(total, bit))
        held = (keep.astype(jnp.float32) + got.astype(jnp.float32)).astype(jnp.bfloat16)
        left.remove(bit)
    return held


def gather_rows(shard, total, order):
    me = lax.axis_index(AXES)
    have = []
    held = shard
    for bit in reversed(order):
        mine = (me >> bit) & 1
        got = lax.ppermute(held, AXES, partner_pairs(total, bit))
        low = jnp.where(mine == 0, held, got)
        high = jnp.where(mine == 0, got, held)
        have = sorted(have + [bit], reverse=True)
        held = jnp.stack([low, high], axis=have.index(bit))
    return held.reshape((total * shard.shape[0],) + shard.shape[1:])


def columns_of(vectors):
    block = jnp.stack(vectors, axis=1)
    return jnp.pad(block, ((0, 0), (0, 128 - len(vectors))))


def shards(
    visible,
    keep_index,
    visible_count,
    enc_gain1,
    enc_shift1,
    enc_qkv,
    enc_out,
    enc_gain2,
    enc_shift2,
    enc_up,
    enc_down,
    proj,
    mask_token,
    dec_gain1,
    dec_shift1,
    dec_qkv,
    dec_out,
    dec_gain2,
    dec_shift2,
    dec_up,
    dec_down,
    cotangent,
):
    total = lax.axis_size(AXES)
    order = bit_order(split_bits(total))
    order_two = swap_order(order)
    enc_wide = enc_out.shape[1]
    dec_wide = dec_out.shape[1]
    pack_one = jnp.concatenate(
        [enc_qkv, enc_out, proj, columns_of([enc_gain1, enc_shift1, enc_gain2, enc_shift2])], axis=1
    )
    pack_one = gather_rows(pack_one, total, order)
    whole_up = gather_rows(enc_up, total, order_two)
    whole_down = gather_rows(enc_down, total, order)
    enc_vecs = pack_one[:, 4 * enc_wide + dec_wide : 4 * enc_wide + dec_wide + 4].T
    enc_weights = (
        enc_vecs[0],
        enc_vecs[1],
        pack_one[:, : 3 * enc_wide],
        pack_one[:, 3 * enc_wide : 4 * enc_wide],
        enc_vecs[2],
        enc_vecs[3],
        whole_up,
        whole_down,
    )
    pack_two = jnp.concatenate(
        [
            dec_qkv,
            dec_out,
            columns_of([dec_gain1, dec_shift1, dec_gain2, dec_shift2, mask_token]),
        ],
        axis=1,
    )
    pack_two = gather_rows(pack_two, total, order_two)
    dec_whole_up = gather_rows(dec_up, total, order)
    dec_whole_down = gather_rows(dec_down, total, order_two)
    dec_vecs = pack_two[:, 4 * dec_wide : 4 * dec_wide + 5].T
    weight_proj = pack_one[:, 4 * enc_wide : 4 * enc_wide + dec_wide]
    token_vec = dec_vecs[4].astype(jnp.float32)
    dec_weights = (
        dec_vecs[0],
        dec_vecs[1],
        pack_two[:, : 3 * dec_wide],
        pack_two[:, 3 * dec_wide : 4 * dec_wide],
        dec_vecs[2],
        dec_vecs[3],
        dec_whole_up,
        dec_whole_down,
    )
    clip_count, slot_total, enc_width = visible.shape
    dec_width = weight_proj.shape[1]
    half_clips = clip_count // 2
    band_height = FREQ // 2
    slot_ids = jnp.arange(slot_total)
    valid_rows = slot_ids[None, :] < visible_count[:, None]
    enc_allowed = valid_rows[:, None, None, :]
    encoded, enc_stored = block_forward(
        visible.astype(jnp.float32), enc_weights, HEADS_ENC, enc_allowed
    )
    enc_inputs = encoded.reshape(-1, enc_width).astype(jnp.bfloat16)
    sent_rows = (
        forward_dot(enc_inputs, weight_proj)
        .astype(jnp.bfloat16)
        .reshape(clip_count, slot_total, dec_width)
    )
    rolled_time = (keep_index // FREQ + TIME - SHIFT) % TIME
    rolled_freq = (keep_index % FREQ + FREQ - SHIFT) % FREQ
    target_band = rolled_freq // band_height
    slot_index = rolled_time * band_height + rolled_freq % band_height
    band_ids = jnp.arange(2)
    chosen = valid_rows[:, None, :] & (target_band[:, None, :] == band_ids[None, :, None])
    chosen = chosen.reshape(2, half_clips, 2, slot_total).transpose(0, 2, 1, 3)
    outgoing = jnp.where(
        chosen[..., None],
        sent_rows.reshape(2, 1, half_clips, slot_total, dec_width),
        jnp.zeros((), jnp.bfloat16),
    )
    outgoing = outgoing.reshape(4, half_clips, slot_total, dec_width)
    slot_out = jnp.where(chosen, slot_index.reshape(2, 1, half_clips, slot_total), -1).astype(
        jnp.bfloat16
    )
    slot_out = slot_out.reshape(4, half_clips, slot_total)
    arrived, arrived_slot = (
        lax.all_to_all(outgoing, "band", split_axis=0, concat_axis=0, tiled=True),
        lax.all_to_all(slot_out, "band", split_axis=0, concat_axis=0, tiled=True),
    )
    half_total = 4 * half_clips
    arrived_rows = arrived.reshape(half_total, slot_total, dec_width)
    arrived_index = arrived_slot.reshape(half_total, slot_total).astype(jnp.int32)
    cell_count = TIME * band_height
    places = jnp.arange(cell_count)
    onehot = (arrived_index[:, :, None] == places[None, None, :]).astype(jnp.bfloat16)
    grid_rows = jnp.einsum("mic,mid->mcd", onehot, arrived_rows, preferred_element_type=jnp.float32)
    seen_mask = jnp.sum(onehot.astype(jnp.float32), axis=1)[:, :, None]
    band_pick = lax.axis_index("band") % 2
    cell_time = places // band_height
    cell_freq = band_pick * band_height + places % band_height
    patch_number = (cell_time + SHIFT) % TIME * FREQ + (cell_freq + SHIFT) % FREQ
    filled = seen_mask * grid_rows + (1.0 - seen_mask) * token_vec + position_table(patch_number)
    labels = (cell_time >= TIME - SHIFT).astype(jnp.int32) * 2 + (cell_freq >= FREQ - SHIFT).astype(
        jnp.int32
    )
    labels = labels.reshape(-1, WINDOW * WINDOW)
    allowed_one = labels[:, :, None] == labels[:, None, :]
    dec_allowed = jnp.tile(allowed_one, (half_total, 1, 1))[:, None]
    decoded, dec_stored = block_forward(
        filled.reshape(-1, WINDOW * WINDOW, dec_width), dec_weights, HEADS_DEC, dec_allowed
    )
    decoded_out = decoded.reshape(cotangent.shape).astype(jnp.bfloat16)
    grad_filled, dec_grads = block_backward(
        cotangent.astype(jnp.float32).reshape(-1, WINDOW * WINDOW, dec_width),
        dec_stored,
        dec_weights,
        HEADS_DEC,
        dec_allowed,
    )
    grad_filled = grad_filled.reshape(half_total, cell_count, dec_width)
    grad_token = jnp.sum((1.0 - seen_mask) * grad_filled, axis=(0, 1))
    safe_index = jnp.maximum(arrived_index, 0)
    picked = jax.vmap(lambda grid_one, index_one: grid_one[index_one])(grad_filled, safe_index)
    returning = jnp.where((arrived_index >= 0)[:, :, None], picked, 0.0).astype(jnp.bfloat16)
    returning = returning.reshape(4, half_clips, slot_total, dec_width)
    coming = lax.all_to_all(returning, "band", split_axis=0, concat_axis=0, tiled=True)
    grad_sent = jnp.sum(
        coming.astype(jnp.float32).reshape(2, 2, half_clips, slot_total, dec_width), axis=1
    )
    grad_sent = grad_sent.astype(jnp.bfloat16).reshape(-1, dec_width)
    grad_proj = weight_dot(enc_inputs, grad_sent)
    grad_encoded = backward_dot(grad_sent, weight_proj)
    dec_small = columns_of([dec_grads[0], dec_grads[1], dec_grads[4], dec_grads[5], grad_token])
    dec_pack = jnp.concatenate([dec_grads[2], dec_grads[3], dec_small], axis=1)
    dec_pack = scatter_sum(dec_pack, total, order_two)
    dec_up_sum = scatter_sum(dec_grads[6], total, order)
    dec_down_sum = scatter_sum(dec_grads[7], total, order_two)
    dec_pack = gather_rows(dec_pack, total, order_two).astype(jnp.float32)
    dec_up_sum = gather_rows(dec_up_sum, total, order).astype(jnp.float32)
    dec_down_sum = gather_rows(dec_down_sum, total, order_two).astype(jnp.float32)
    dec_vec_sums = dec_pack[:, 4 * dec_wide : 4 * dec_wide + 5].T
    grad_visible, enc_grads = block_backward(
        grad_encoded.reshape(clip_count, slot_total, enc_width),
        enc_stored,
        enc_weights,
        HEADS_ENC,
        enc_allowed,
    )
    enc_up_sum = scatter_sum(enc_grads[6], total, order_two)
    enc_down_sum = scatter_sum(enc_grads[7], total, order)
    enc_small = columns_of([enc_grads[0], enc_grads[1], enc_grads[4], enc_grads[5]])
    enc_pack = jnp.concatenate([enc_grads[2], enc_grads[3], grad_proj, enc_small], axis=1)
    enc_pack = scatter_sum(enc_pack, total, order)
    enc_up_sum = gather_rows(enc_up_sum, total, order_two).astype(jnp.float32)
    enc_down_sum = gather_rows(enc_down_sum, total, order).astype(jnp.float32)
    enc_pack = gather_rows(enc_pack, total, order).astype(jnp.float32)
    enc_vec_sums = enc_pack[:, 4 * enc_wide + dec_wide : 4 * enc_wide + dec_wide + 4].T
    return (
        decoded_out,
        grad_visible.astype(jnp.bfloat16),
        enc_vec_sums[0],
        enc_vec_sums[1],
        enc_pack[:, : 3 * enc_wide],
        enc_pack[:, 3 * enc_wide : 4 * enc_wide],
        enc_vec_sums[2],
        enc_vec_sums[3],
        enc_up_sum,
        enc_down_sum,
        enc_pack[:, 4 * enc_wide : 4 * enc_wide + dec_wide],
        dec_vec_sums[4],
        dec_vec_sums[0],
        dec_vec_sums[1],
        dec_pack[:, : 3 * dec_wide],
        dec_pack[:, 3 * dec_wide : 4 * dec_wide],
        dec_vec_sums[2],
        dec_vec_sums[3],
        dec_up_sum,
        dec_down_sum,
    )


def solution(mesh):
    return jax.shard_map(
        shards,
        mesh=mesh,
        in_specs=(
            P(("clip", "band"), None, None),
            P(("clip", "band"), None),
            P(("clip", "band")),
            P(("clip", "band")),
            P(("clip", "band")),
            P(("clip", "band"), None),
            P(("clip", "band"), None),
            P(("clip", "band")),
            P(("clip", "band")),
            P(("clip", "band"), None),
            P(("clip", "band"), None),
            P(("clip", "band"), None),
            P(("clip", "band")),
            P(("clip", "band")),
            P(("clip", "band")),
            P(("clip", "band"), None),
            P(("clip", "band"), None),
            P(("clip", "band")),
            P(("clip", "band")),
            P(("clip", "band"), None),
            P(("clip", "band"), None),
            P(("clip", "band"), None, None, None, None),
        ),
        out_specs=(
            P(("clip", "band"), None, None, None, None),
            P(("clip", "band"), None, None),
            P(),
            P(),
            P(),
            P(),
            P(),
            P(),
            P(),
            P(),
            P(),
            P(),
            P(),
            P(),
            P(),
            P(),
            P(),
            P(),
            P(),
            P(),
        ),
        check_vma=False,
    )
```

```python
import math

import jax
import jax.numpy as jnp
from jax import lax
from jax.experimental import pallas as pl
from jax.experimental.pallas import tpu as pltpu
from jax.sharding import PartitionSpec as P

HEADS_ENC = 12
D_DEC = 512
HEADS_DEC = 16
TIME = 64
FREQ = 8
WINDOW = 4
SHIFT = 2
norm_eps = 1e-06
neg_fill = -1e30
F32 = jnp.float32
BF16 = jnp.bfloat16
LANES = 128


def mm(a, b):
    return lax.dot_general(a, b, (((1,), (0,)), ((), ())), preferred_element_type=F32)


def mm_t(a, b):
    return lax.dot_general(a, b, (((1,), (1,)), ((), ())), preferred_element_type=F32)


def bmm(a, b):
    return lax.dot_general(a, b, (((2,), (1,)), ((0,), (0,))), preferred_element_type=F32)


def bmm_t(a, b):
    return lax.dot_general(a, b, (((2,), (2,)), ((0,), (0,))), preferred_element_type=F32)


def bmm_l(a, b):
    return lax.dot_general(a, b, (((1,), (1,)), ((0,), (0,))), preferred_element_type=F32)


def normalise(x):
    centre = jnp.mean(x, axis=-1, keepdims=True)
    centred = x - centre
    rstd = lax.rsqrt(jnp.mean(centred * centred, axis=-1, keepdims=True) + norm_eps)
    return centred * rstd, rstd


def norm_back(da, xhat, rstd, gain):
    dag = da * gain
    return rstd * (
        dag
        - jnp.mean(dag, axis=-1, keepdims=True)
        - xhat * jnp.mean(dag * xhat, axis=-1, keepdims=True)
    )


def gelu_parts(u):
    size = jnp.abs(u) * 0.7071067811865476
    bell = jnp.exp(-0.5 * u * u)
    t = 1.0 / (1.0 + 0.3275911 * size)
    poly = 0.530702715
    poly = poly * t - 0.726576013
    poly = poly * t + 0.710706871
    poly = poly * t - 0.142248368
    poly = poly * t + 0.127414796
    tail = poly * t * bell
    cdf = jnp.where(u >= 0, 1.0 - tail, tail)
    return cdf, u * bell * 0.3989422804014327


def segment_sum(x, ones):
    high = x.astype(BF16)
    low = (x - high.astype(F32)).astype(BF16)
    return mm(high, ones) + mm(low, ones)


def window_max(s):
    ahead = s
    behind = s
    for step in (1, 2, 4, 8):
        ahead = jnp.maximum(ahead, pltpu.roll(ahead, step, 1))
        behind = jnp.maximum(behind, pltpu.roll(behind, LANES - step, 1))
    return jnp.maximum(ahead, behind)


def decoder_kernel(
    rows_ref, idx_ref, cot_ref, pos_ref, mask_ref, vec_ref, wqkv_ref, wo_ref, wu_ref, wd_ref,
    out_ref, ret_ref, gqkv_ref, go_ref, gu_ref, gd_ref, gvec_ref,
    acc_qkv, acc_o, acc_u, acc_d, x_s, qkv_s, p_s, o_s, a2_s, a2t_s, dzt_s, da_s, y_s, dqkv_s,
):
    step = pl.program_id(0)
    last = pl.num_programs(0) - 1
    halves, cells, width = cot_ref.shape
    m_rows = halves * cells
    slots = rows_ref.shape[1]
    head_dim = width // HEADS_DEC
    heads_in = LANES // head_dim
    groups = width // LANES
    block = LANES // heads_in
    blocks = m_rows // block
    scale = head_dim ** (-0.5)
    ff = wu_ref.shape[1]
    chunk = 512

    @pl.when(step == 0)
    def _():
        acc_qkv[...] = jnp.zeros_like(acc_qkv)
        acc_o[...] = jnp.zeros_like(acc_o)
        acc_u[...] = jnp.zeros_like(acc_u)
        acc_d[...] = jnp.zeros_like(acc_d)
        gvec_ref[...] = jnp.zeros_like(gvec_ref)

    gain1, shift1 = vec_ref[0:1, :], vec_ref[1:2, :]
    gain2, shift2 = vec_ref[2:3, :], vec_ref[3:4, :]
    token = vec_ref[4:5, :]

    def place_of(h):
        cell = lax.broadcasted_iota(jnp.int32, (cells, slots), 0)
        return cell == idx_ref[h]

    unseen = []
    for h in range(halves):
        place = place_of(h)
        unseen_h = 1.0 - jnp.sum(place.astype(F32), axis=1, keepdims=True)
        unseen.append(unseen_h)
        x_s[h * cells : (h + 1) * cells, :] = (
            mm(place.astype(BF16), rows_ref[h]) + unseen_h * token + pos_ref[...]
        )
    xhat1, rstd1 = normalise(x_s[...])
    a1 = (xhat1 * gain1 + shift1).astype(BF16)
    qkv_s[...] = mm(a1, wqkv_ref[...]).astype(BF16)

    lane = lax.broadcasted_iota(jnp.int32, (1, LANES), 1)
    head_masks = [(lane // head_dim == h) for h in range(heads_in)]
    ones = (
        lax.broadcasted_iota(jnp.int32, (LANES, LANES), 0) // block
        == lax.broadcasted_iota(jnp.int32, (LANES, LANES), 1) // block
    ).astype(BF16)

    def spread(t):
        parts = [t * hm.astype(BF16)[None] for hm in head_masks]
        return jnp.concatenate(parts, axis=1)

    def fold(t):
        out = t[:, 0:block, :]
        for h in range(1, heads_in):
            out = jnp.where(head_masks[h][None], t[:, h * block : (h + 1) * block, :], out)
        return out

    def part(ref, base, g):
        return ref[:, base + g * LANES : base + (g + 1) * LANES].reshape(blocks, block, LANES)

    allowed = jnp.concatenate([mask_ref[...]] * halves, axis=0) > 0.5
    for g in range(groups):
        q3 = part(qkv_s, 0, g)
        k3 = spread(part(qkv_s, width, g))
        v3 = spread(part(qkv_s, 2 * width, g))
        s = bmm_t(q3, k3).reshape(m_rows, LANES) * scale
        s = jnp.where(allowed, s, neg_fill)
        e = jnp.where(allowed, jnp.exp(s - window_max(s)), 0.0)
        p = e / segment_sum(e, ones)
        p_s[:, g * LANES : (g + 1) * LANES] = p
        o = bmm(p.astype(BF16).reshape(blocks, block, LANES), v3)
        o_s[:, g * LANES : (g + 1) * LANES] = o.reshape(m_rows, LANES).astype(BF16)

    x2 = x_s[...] + mm(o_s[...], wo_ref[...])
    xhat2, rstd2 = normalise(x2)
    a2 = (xhat2 * gain2 + shift2).astype(BF16)
    a2_s[...] = a2
    a2t_s[...] = a2.T
    dz = cot_ref[...].reshape(m_rows, width)
    dzt_s[...] = dz.T
    y_s[...] = x2
    da_s[...] = jnp.zeros_like(da_s)

    def ff_body(c, carry):
        at = pl.ds(pl.multiple_of(c * chunk, chunk), chunk)
        wu = wu_ref[:, at]
        wd = wd_ref[at, :]
        dzc = cot_ref[...].reshape(m_rows, width)
        u = mm(a2_s[...], wu)
        dh = mm_t(dzc, wd)
        cdf, bump = gelu_parts(u)
        h = (u * cdf).astype(BF16)
        du = ((cdf + bump) * dh).astype(BF16)
        y_s[...] += mm(h, wd)
        acc_d[:, at] += mm(dzt_s[...], h)
        acc_u[:, at] += mm(a2t_s[...], du)
        da_s[...] += mm_t(du, wu)
        return carry

    lax.fori_loop(0, ff // chunk, ff_body, 0)

    out_ref[...] = y_s[...].reshape(halves, cells, width).astype(BF16)
    da2 = da_s[...]
    gvec_ref[2:3, :] += jnp.sum(da2 * xhat2, axis=0, keepdims=True)
    gvec_ref[3:4, :] += jnp.sum(da2, axis=0, keepdims=True)
    dx2 = cot_ref[...].reshape(m_rows, width).astype(F32) + norm_back(da2, xhat2, rstd2, gain2)
    dy2 = dx2.astype(BF16)
    acc_o[...] += mm(o_s[...].T, dy2)
    do = mm_t(dy2, wo_ref[...]).astype(BF16)

    for g in range(groups):
        cols = slice(g * LANES, (g + 1) * LANES)
        q3 = part(qkv_s, 0, g)
        k3 = spread(part(qkv_s, width, g))
        v3 = spread(part(qkv_s, 2 * width, g))
        do3 = do[:, cols].reshape(blocks, block, LANES)
        p = p_s[:, cols]
        dp = bmm_t(do3, v3).reshape(m_rows, LANES)
        draw = (p * (dp - segment_sum(p * dp, ones)) * scale).astype(BF16)
        draw3 = draw.reshape(blocks, block, LANES)
        dq = bmm(draw3, k3).reshape(m_rows, LANES)
        dk = fold(bmm_l(draw3, q3)).reshape(m_rows, LANES)
        dv = fold(bmm_l(p.astype(BF16).reshape(blocks, block, LANES), do3)).reshape(m_rows, LANES)
        dqkv_s[:, g * LANES : (g + 1) * LANES] = dq.astype(BF16)
        dqkv_s[:, width + g * LANES : width + (g + 1) * LANES] = dk.astype(BF16)
        dqkv_s[:, 2 * width + g * LANES : 2 * width + (g + 1) * LANES] = dv.astype(BF16)

    xhat1, rstd1 = normalise(x_s[...])
    a1 = (xhat1 * gain1 + shift1).astype(BF16)
    dqkv = dqkv_s[...]
    acc_qkv[...] += mm(a1.T, dqkv)
    da1 = mm_t(dqkv, wqkv_ref[...])
    gvec_ref[0:1, :] += jnp.sum(da1 * xhat1, axis=0, keepdims=True)
    gvec_ref[1:2, :] += jnp.sum(da1, axis=0, keepdims=True)
    dx = dx2 + norm_back(da1, xhat1, rstd1, gain1)
    for h in range(halves):
        dx_h = dx[h * cells : (h + 1) * cells, :]
        gvec_ref[4:5, :] += jnp.sum(unseen[h] * dx_h, axis=0, keepdims=True)
        place = place_of(h).astype(F32).T.astype(BF16)
        ret_ref[h] = mm(place, dx_h.astype(BF16)).astype(BF16)

    @pl.when(step == last)
    def _():
        gqkv_ref[...] = acc_qkv[...].astype(BF16)
        go_ref[...] = acc_o[...].astype(BF16)
        gu_ref[...] = acc_u[...].astype(BF16)
        for c in range(ff // chunk):
            gd_ref[c * chunk : (c + 1) * chunk, :] = acc_d[:, c * chunk : (c + 1) * chunk].T.astype(BF16)


def decoder_block(rows, idx, cot, pos, mask, vecs, wqkv, wo, wu, wd):
    n_half, slots, width = rows.shape
    cells = cot.shape[1]
    ff = wu.shape[1]
    halves = 2
    m_rows = halves * cells
    whole = lambda *shape: pl.BlockSpec(shape, lambda i: (0,) * len(shape), pipeline_mode=pl.Buffered(1))
    vm = pltpu.VMEM
    return pl.pallas_call(
        decoder_kernel,
        grid=(n_half // halves,),
        in_specs=[
            pl.BlockSpec((halves, slots, width), lambda i: (i, 0, 0)),
            pl.BlockSpec((halves, 1, slots), lambda i: (i, 0, 0)),
            pl.BlockSpec((halves, cells, width), lambda i: (i, 0, 0)),
            whole(cells, width),
            whole(cells, LANES),
            whole(8, width),
            whole(width, 3 * width),
            whole(width, width),
            whole(width, ff),
            whole(ff, width),
        ],
        out_specs=[
            pl.BlockSpec((halves, cells, width), lambda i: (i, 0, 0)),
            pl.BlockSpec((halves, slots, width), lambda i: (i, 0, 0)),
            whole(width, 3 * width),
            whole(width, width),
            whole(width, ff),
            whole(ff, width),
            whole(8, width),
        ],
        out_shape=[
            jax.ShapeDtypeStruct((n_half, cells, width), BF16),
            jax.ShapeDtypeStruct((n_half, slots, width), BF16),
            jax.ShapeDtypeStruct((width, 3 * width), BF16),
            jax.ShapeDtypeStruct((width, width), BF16),
            jax.ShapeDtypeStruct((width, ff), BF16),
            jax.ShapeDtypeStruct((ff, width), BF16),
            jax.ShapeDtypeStruct((8, width), F32),
        ],
        scratch_shapes=[
            vm((width, 3 * width), F32),
            vm((width, width), F32),
            vm((width, ff), F32),
            vm((width, ff), F32),
            vm((m_rows, width), F32),
            vm((m_rows, 3 * width), BF16),
            vm((m_rows, width), F32),
            vm((m_rows, width), BF16),
            vm((m_rows, width), BF16),
            vm((width, m_rows), BF16),
            vm((width, m_rows), BF16),
            vm((m_rows, width), F32),
            vm((m_rows, width), F32),
            vm((m_rows, 3 * width), BF16),
        ],
        compiler_params=pltpu.CompilerParams(
            dimension_semantics=("arbitrary",), vmem_limit_bytes=58 * 1024 * 1024
        ),
        name="decoder_block",
    )(rows, idx.reshape(n_half, 1, slots), cot, pos, mask, vecs, wqkv, wo, wu, wd)


def enc_spread(t, head_masks):
    return jnp.concatenate([t * hm.astype(BF16)[None] for hm in head_masks], axis=1)


def enc_heads(width):
    head_dim = width // HEADS_ENC
    lane = lax.broadcasted_iota(jnp.int32, (1, LANES), 1)
    return head_dim, [(lane // head_dim == h) for h in range(LANES // head_dim)]


def enc_attend_kernel(x_ref, mask_ref, vec_ref, wqkv_ref, wo_ref, qkv_ref, p_ref, o_ref, x2_ref):
    clips, slots, width = x_ref.shape
    m_rows = clips * slots
    head_dim, head_masks = enc_heads(width)
    scale = head_dim ** (-0.5)
    x = x_ref[...].reshape(m_rows, width).astype(F32)
    xhat, rstd = normalise(x)
    a1 = (xhat * vec_ref[0:1, :] + vec_ref[1:2, :]).astype(BF16)
    qkv_ref[...] = mm(a1, wqkv_ref[...]).astype(BF16)
    allowed = mask_ref[...] > 0.5
    for g in range(width // LANES):
        cols = lambda part: slice(part * width + g * LANES, part * width + (g + 1) * LANES)
        q3 = qkv_ref[:, cols(0)].reshape(clips, slots, LANES)
        k3 = enc_spread(qkv_ref[:, cols(1)].reshape(clips, slots, LANES), head_masks)
        v3 = enc_spread(qkv_ref[:, cols(2)].reshape(clips, slots, LANES), head_masks)
        s = bmm_t(q3, k3) * scale
        for h in range(len(head_masks)):
            sh = jnp.where(allowed, s[:, :, h * slots : (h + 1) * slots], neg_fill)
            e = jnp.exp(sh - jnp.max(sh, axis=-1, keepdims=True))
            e = e / jnp.sum(e, axis=-1, keepdims=True)
            at = (g * len(head_masks) + h) * slots
            p_ref[:, at : at + slots] = e.reshape(m_rows, slots).astype(BF16)
        span = len(head_masks) * slots
        p3 = p_ref[:, g * span : (g + 1) * span].reshape(clips, slots, span)
        o_ref[:, cols(0)] = bmm(p3, v3).reshape(m_rows, LANES).astype(BF16)
    x2_ref[...] = x_ref[...].reshape(m_rows, width).astype(F32) + mm(o_ref[...], wo_ref[...])


def enc_feed_kernel(
    x2_ref, vec_ref, wu_ref, wd_ref, proj_ref, sent_ref, enc_ref, h_ref, gp_ref, a2_s, y_s
):
    ff = wu_ref.shape[1]
    chunk = 512
    xhat, rstd = normalise(x2_ref[...])
    a2_s[...] = (xhat * vec_ref[2:3, :] + vec_ref[3:4, :]).astype(BF16)
    y_s[...] = x2_ref[...]

    def body(c, carry):
        at = pl.ds(pl.multiple_of(c * chunk, chunk), chunk)
        u = mm(a2_s[...], wu_ref[:, at])
        cdf, bump = gelu_parts(u)
        h = (u * cdf).astype(BF16)
        h_ref[:, at] = h
        gp_ref[:, at] = (cdf + bump).astype(BF16)
        y_s[...] += mm(h, wd_ref[at, :])
        return carry

    lax.fori_loop(0, ff // chunk, body, 0)
    encoded = y_s[...].astype(BF16)
    enc_ref[...] = encoded
    sent_ref[...] = mm(encoded, proj_ref[...]).astype(BF16)


def enc_feed_back_kernel(
    dsent_ref, enc_ref, proj_ref, h_ref, gp_ref, x2_ref, vec_ref, wu_ref, wd_ref,
    gproj_ref, gu_ref, gd_ref, dx2_ref, gvec_ref,
    a2t_s, dz_s, dzt_s, da_s,
):
    ff = wu_ref.shape[1]
    chunk = 512
    gain2 = vec_ref[2:3, :]
    dsent = dsent_ref[...]
    gproj_ref[...] = mm(enc_ref[...].T, dsent).astype(BF16)
    dy = mm_t(dsent, proj_ref[...])
    dx2_ref[...] = dy
    dz = dy.astype(BF16)
    dz_s[...] = dz
    dzt_s[...] = dz.T
    xhat, rstd = normalise(x2_ref[...])
    a2t_s[...] = (xhat * gain2 + vec_ref[3:4, :]).astype(BF16).T
    da_s[...] = jnp.zeros_like(da_s)

    def body(c, carry):
        at = pl.ds(pl.multiple_of(c * chunk, chunk), chunk)
        dh = mm_t(dz_s[...], wd_ref[at, :])
        du = (gp_ref[:, at].astype(F32) * dh).astype(BF16)
        gd_ref[at, :] = mm(dzt_s[...], h_ref[:, at]).T.astype(BF16)
        gu_ref[:, at] = mm(a2t_s[...], du).astype(BF16)
        da_s[...] += mm_t(du, wu_ref[:, at])
        return carry

    lax.fori_loop(0, ff // chunk, body, 0)
    da = da_s[...]
    xhat, rstd = normalise(x2_ref[...])
    gvec_ref[...] = jnp.zeros_like(gvec_ref)
    gvec_ref[2:3, :] = jnp.sum(da * xhat, axis=0, keepdims=True)
    gvec_ref[3:4, :] = jnp.sum(da, axis=0, keepdims=True)
    dx2_ref[...] += norm_back(da, xhat, rstd, gain2)


def enc_attend_back_kernel(
    dx2_ref, o_ref, qkv_ref, p_ref, x_ref, vec_ref, wqkv_ref, wo_ref,
    gqkv_ref, go_ref, dvis_ref, gvec_ref,
    do_s, dqkv_s,
):
    clips, slots, width = x_ref.shape
    m_rows = clips * slots
    head_dim, head_masks = enc_heads(width)
    count = len(head_masks)
    scale = head_dim ** (-0.5)
    gain1, shift1 = vec_ref[0:1, :], vec_ref[1:2, :]
    dy2 = dx2_ref[...].astype(BF16)
    go_ref[...] = mm(o_ref[...].T, dy2).astype(BF16)
    do_s[...] = mm_t(dy2, wo_ref[...]).astype(BF16)

    def fold(t):
        out = t[:, 0:slots, :]
        for h in range(1, count):
            out = jnp.where(head_masks[h][None], t[:, h * slots : (h + 1) * slots, :], out)
        return out.reshape(m_rows, LANES).astype(BF16)

    for g in range(width // LANES):
        cols = lambda part: slice(part * width + g * LANES, part * width + (g + 1) * LANES)
        q3 = qkv_ref[:, cols(0)].reshape(clips, slots, LANES)
        k3 = enc_spread(qkv_ref[:, cols(1)].reshape(clips, slots, LANES), head_masks)
        v3 = enc_spread(qkv_ref[:, cols(2)].reshape(clips, slots, LANES), head_masks)
        do3 = do_s[:, cols(0)].reshape(clips, slots, LANES)
        span = count * slots
        p3 = p_ref[:, g * span : (g + 1) * span].reshape(clips, slots, span)
        dp = bmm_t(do3, v3)
        parts = []
        for h in range(count):
            hs = slice(h * slots, (h + 1) * slots)
            ph = p3[:, :, hs].astype(F32)
            dph = dp[:, :, hs]
            mean = jnp.sum(ph * dph, axis=-1, keepdims=True)
            parts.append((ph * (dph - mean) * scale).astype(BF16))
        draw3 = jnp.concatenate(parts, axis=2)
        dqkv_s[:, cols(0)] = bmm(draw3, k3).reshape(m_rows, LANES).astype(BF16)
        dqkv_s[:, cols(1)] = fold(bmm_l(draw3, q3))
        dqkv_s[:, cols(2)] = fold(bmm_l(p3, do3))

    x = x_ref[...].reshape(m_rows, width).astype(F32)
    xhat, rstd = normalise(x)
    a1t = (xhat * gain1 + shift1).astype(BF16).T
    gqkv_ref[...] = mm(a1t, dqkv_s[...]).astype(BF16)
    da = mm_t(dqkv_s[...], wqkv_ref[...])
    gvec_ref[...] = jnp.zeros_like(gvec_ref)
    gvec_ref[0:1, :] = jnp.sum(da * xhat, axis=0, keepdims=True)
    gvec_ref[1:2, :] = jnp.sum(da, axis=0, keepdims=True)
    dx = dx2_ref[...] + norm_back(da, xhat, rstd, gain1)
    dvis_ref[...] = dx.reshape(clips, slots, width).astype(BF16)


def whole_call(kernel, outs, scratch, name, *args):
    return pl.pallas_call(
        kernel,
        out_shape=[jax.ShapeDtypeStruct(s, d) for s, d in outs],
        scratch_shapes=[pltpu.VMEM(s, d) for s, d in scratch],
        compiler_params=pltpu.CompilerParams(vmem_limit_bytes=58 * 1024 * 1024),
        name=name,
    )(*args)


def enc_attend(x, mask, vecs, wqkv, wo):
    clips, slots, width = x.shape
    m = clips * slots
    outs = [((m, 3 * width), BF16), ((m, HEADS_ENC * slots), BF16), ((m, width), BF16), ((m, width), F32)]
    return whole_call(enc_attend_kernel, outs, [], "enc_attend", x, mask, vecs, wqkv, wo)


def enc_feed(x2, vecs, wu, wd, proj):
    m, width = x2.shape
    ff = wu.shape[1]
    outs = [((m, proj.shape[1]), BF16), ((m, width), BF16), ((m, ff), BF16), ((m, ff), BF16)]
    scratch = [((m, width), BF16), ((m, width), F32)]
    return whole_call(enc_feed_kernel, outs, scratch, "enc_feed", x2, vecs, wu, wd, proj)


def enc_feed_back(dsent, enc, proj, h, gp, x2, vecs, wu, wd):
    m, width = x2.shape
    ff = wu.shape[1]
    outs = [(proj.shape, BF16), (wu.shape, BF16), (wd.shape, BF16), ((m, width), F32), ((8, width), F32)]
    scratch = [((width, m), BF16), ((m, width), BF16), ((width, m), BF16), ((m, width), F32)]
    return whole_call(
        enc_feed_back_kernel, outs, scratch, "enc_feed_back", dsent, enc, proj, h, gp, x2, vecs, wu, wd
    )


def enc_attend_back(dx2, o, qkv, p, x, vecs, wqkv, wo):
    m, width = dx2.shape
    outs = [(wqkv.shape, BF16), (wo.shape, BF16), (x.shape, BF16), ((8, width), F32)]
    scratch = [((m, width), BF16), ((m, 3 * width), BF16)]
    return whole_call(
        enc_attend_back_kernel, outs, scratch, "enc_attend_back", dx2, o, qkv, p, x, vecs, wqkv, wo
    )


AXES = ("clip", "band")


def split_bits(parts):
    return parts.bit_length() - 1


def bit_order(count):
    first = [b for b in (0, 2, 1) if b < count]
    rest = [b for b in range(count - 1, -1, -1) if b not in first]
    return first + rest


def swap_order(order):
    if len(order) < 3:
        return order
    return [order[0], order[2], order[1]] + order[3:]


def partner_pairs(total, bit):
    return [(i, i ^ (1 << bit)) for i in range(total)]


def scatter_sum(partial, total, order):
    me = lax.axis_index(AXES)
    left = list(range(split_bits(total) - 1, -1, -1))
    rows = partial.shape[0] // total
    held = partial.reshape((2,) * len(left) + (rows,) + partial.shape[1:])
    for bit in order:
        place = left.index(bit)
        mine = (me >> bit) & 1
        keep = lax.dynamic_index_in_dim(held, mine, place, keepdims=False)
        give = lax.dynamic_index_in_dim(held, 1 - mine, place, keepdims=False)
        got = lax.ppermute(give, AXES, partner_pairs(total, bit))
        held = (keep.astype(F32) + got.astype(F32)).astype(BF16)
        left.remove(bit)
    return held


def gather_rows(shard, total, order):
    me = lax.axis_index(AXES)
    have = []
    held = shard
    for bit in reversed(order):
        mine = (me >> bit) & 1
        got = lax.ppermute(held, AXES, partner_pairs(total, bit))
        low = jnp.where(mine == 0, held, got)
        high = jnp.where(mine == 0, got, held)
        have = sorted(have + [bit], reverse=True)
        held = jnp.stack([low, high], axis=have.index(bit))
    return held.reshape((total * shard.shape[0],) + shard.shape[1:])


def columns_of(vectors):
    block = jnp.stack(vectors, axis=1)
    return jnp.pad(block, ((0, 0), (0, LANES - len(vectors)))).astype(BF16)


def rows_of(block, count):
    vectors = block[:, :count].T.astype(F32)
    return jnp.pad(vectors, ((0, 8 - count), (0, 0)))


def position_table(places):
    half_width = D_DEC // 2
    omega_vec = jnp.exp(
        jnp.arange(half_width, dtype=F32) * (-math.log(10000.0) / half_width)
    )
    angles = places.astype(F32)[..., None] * omega_vec
    return jnp.concatenate([jnp.sin(angles), jnp.cos(angles)], axis=-1)


def shards(
    visible,
    keep_index,
    visible_count,
    enc_gain1,
    enc_shift1,
    enc_qkv,
    enc_out,
    enc_gain2,
    enc_shift2,
    enc_up,
    enc_down,
    proj,
    mask_token,
    dec_gain1,
    dec_shift1,
    dec_qkv,
    dec_out,
    dec_gain2,
    dec_shift2,
    dec_up,
    dec_down,
    cotangent,
):
    total = lax.axis_size(AXES)
    order = bit_order(split_bits(total))
    order_two = swap_order(order)
    enc_wide = enc_out.shape[1]
    dec_wide = dec_out.shape[1]
    pack_one = jnp.concatenate(
        [enc_qkv, enc_out, proj, columns_of([enc_gain1, enc_shift1, enc_gain2, enc_shift2])], axis=1
    )
    pack_one = gather_rows(pack_one, total, order)
    whole_up = gather_rows(enc_up, total, order_two)
    whole_down = gather_rows(enc_down, total, order)
    enc_vecs = rows_of(pack_one[:, 4 * enc_wide + dec_wide :], 4)
    whole_qkv = pack_one[:, : 3 * enc_wide]
    whole_out = pack_one[:, 3 * enc_wide : 4 * enc_wide]
    whole_proj = pack_one[:, 4 * enc_wide : 4 * enc_wide + dec_wide]
    pack_two = jnp.concatenate(
        [
            dec_qkv,
            dec_out,
            columns_of([dec_gain1, dec_shift1, dec_gain2, dec_shift2, mask_token]),
        ],
        axis=1,
    )
    pack_two = gather_rows(pack_two, total, order_two)
    dec_whole_up = gather_rows(dec_up, total, order)
    dec_whole_down = gather_rows(dec_down, total, order_two)
    dec_vecs = rows_of(pack_two[:, 4 * dec_wide :], 5)

    clip_count, slot_total, _ = visible.shape
    half_clips = clip_count // 2
    band_height = FREQ // 2
    slot_ids = jnp.arange(slot_total)
    valid_rows = slot_ids[None, :] < visible_count[:, None]
    valid_mask = valid_rows.astype(F32)[:, None, :]
    qkv, probs, mixed, middle = enc_attend(visible, valid_mask, enc_vecs, whole_qkv, whole_out)
    sent_rows, encoded, hidden, slope = enc_feed(middle, enc_vecs, whole_up, whole_down, whole_proj)
    sent_rows = sent_rows.reshape(clip_count, slot_total, dec_wide)

    rolled_time = (keep_index // FREQ + TIME - SHIFT) % TIME
    rolled_freq = (keep_index % FREQ + FREQ - SHIFT) % FREQ
    target_band = rolled_freq // band_height
    slot_index = rolled_time * band_height + rolled_freq % band_height
    band_ids = jnp.arange(2)
    chosen = valid_rows[:, None, :] & (target_band[:, None, :] == band_ids[None, :, None])
    chosen = chosen.reshape(2, half_clips, 2, slot_total).transpose(0, 2, 1, 3)
    outgoing = jnp.where(
        chosen[..., None],
        sent_rows.reshape(2, 1, half_clips, slot_total, dec_wide),
        jnp.zeros((), BF16),
    )
    outgoing = outgoing.reshape(4, half_clips, slot_total, dec_wide)
    slot_out = jnp.where(chosen, slot_index.reshape(2, 1, half_clips, slot_total), -1).astype(BF16)
    slot_out = slot_out.reshape(4, half_clips, slot_total)
    arrived = lax.all_to_all(outgoing, "band", split_axis=0, concat_axis=0, tiled=True)
    arrived_slot = lax.all_to_all(slot_out, "band", split_axis=0, concat_axis=0, tiled=True)
    half_total = 4 * half_clips
    arrived_rows = arrived.reshape(half_total, slot_total, dec_wide)
    arrived_index = arrived_slot.reshape(half_total, slot_total).astype(jnp.int32)

    cell_count = TIME * band_height
    places = jnp.arange(cell_count)
    band_pick = lax.axis_index("band") % 2
    cell_freq = band_pick * band_height + places % band_height
    patch_number = (places // band_height + SHIFT) % TIME * FREQ + (cell_freq + SHIFT) % FREQ
    span = LANES * D_DEC // (HEADS_DEC * LANES)
    query = places[:, None]
    key = query // span * span + jnp.arange(LANES)[None, :] % span

    def label(cell):
        late = cell // band_height >= TIME - SHIFT
        high = band_pick * band_height + cell % band_height >= FREQ - SHIFT
        return late.astype(jnp.int32) * 2 + high.astype(jnp.int32)

    cells_in = WINDOW * WINDOW
    allowed = (query // cells_in == key // cells_in) & (label(query) == label(key))
    decoded, returning, g_dqkv, g_dout, g_dup, g_ddown, g_dvec = decoder_block(
        arrived_rows,
        arrived_index,
        cotangent.reshape(half_total, cell_count, dec_wide),
        position_table(patch_number),
        allowed.astype(F32),
        dec_vecs,
        pack_two[:, : 3 * dec_wide],
        pack_two[:, 3 * dec_wide : 4 * dec_wide],
        dec_whole_up,
        dec_whole_down,
    )
    decoded_out = decoded.reshape(cotangent.shape)

    returning = returning.reshape(4, half_clips, slot_total, dec_wide)
    coming = lax.all_to_all(returning, "band", split_axis=0, concat_axis=0, tiled=True)
    grad_sent = jnp.sum(coming.astype(F32).reshape(2, 2, half_clips, slot_total, dec_wide), axis=1)
    grad_sent = grad_sent.astype(BF16).reshape(-1, dec_wide)

    dec_pack = jnp.concatenate([g_dqkv, g_dout, columns_of([g_dvec[i] for i in range(5)])], axis=1)
    dec_pack = scatter_sum(dec_pack, total, order_two)
    dec_up_sum = scatter_sum(g_dup, total, order)
    dec_down_sum = scatter_sum(g_ddown, total, order_two)
    dec_pack = gather_rows(dec_pack, total, order_two).astype(F32)
    dec_up_sum = gather_rows(dec_up_sum, total, order).astype(F32)
    dec_down_sum = gather_rows(dec_down_sum, total, order_two).astype(F32)
    dec_vec_sums = rows_of(dec_pack[:, 4 * dec_wide :], 5)

    g_proj, g_eup, g_edown, grad_middle, g_evec2 = enc_feed_back(
        grad_sent, encoded, whole_proj, hidden, slope, middle, enc_vecs, whole_up, whole_down
    )
    enc_up_sum = scatter_sum(g_eup, total, order_two)
    enc_down_sum = scatter_sum(g_edown, total, order)
    g_eqkv, g_eout, grad_visible, g_evec1 = enc_attend_back(
        grad_middle, mixed, qkv, probs, visible, enc_vecs, whole_qkv, whole_out
    )
    g_evec = g_evec1 + g_evec2
    enc_pack = jnp.concatenate(
        [g_eqkv, g_eout, g_proj, columns_of([g_evec[i] for i in range(4)])], axis=1
    )
    enc_pack = scatter_sum(enc_pack, total, order)
    enc_up_sum = gather_rows(enc_up_sum, total, order_two).astype(F32)
    enc_down_sum = gather_rows(enc_down_sum, total, order).astype(F32)
    enc_pack = gather_rows(enc_pack, total, order).astype(F32)
    enc_vec_sums = rows_of(enc_pack[:, 4 * enc_wide + dec_wide :], 4)
    return (
        decoded_out,
        grad_visible,
        enc_vec_sums[0],
        enc_vec_sums[1],
        enc_pack[:, : 3 * enc_wide],
        enc_pack[:, 3 * enc_wide : 4 * enc_wide],
        enc_vec_sums[2],
        enc_vec_sums[3],
        enc_up_sum,
        enc_down_sum,
        enc_pack[:, 4 * enc_wide : 4 * enc_wide + dec_wide],
        dec_vec_sums[4],
        dec_vec_sums[0],
        dec_vec_sums[1],
        dec_pack[:, : 3 * dec_wide],
        dec_pack[:, 3 * dec_wide : 4 * dec_wide],
        dec_vec_sums[2],
        dec_vec_sums[3],
        dec_up_sum,
        dec_down_sum,
    )


def solution(mesh):
    return jax.shard_map(
        shards,
        mesh=mesh,
        in_specs=(
            P(("clip", "band"), None, None),
            P(("clip", "band"), None),
            P(("clip", "band")),
            P(("clip", "band")),
            P(("clip", "band")),
            P(("clip", "band"), None),
            P(("clip", "band"), None),
            P(("clip", "band")),
            P(("clip", "band")),
            P(("clip", "band"), None),
            P(("clip", "band"), None),
            P(("clip", "band"), None),
            P(("clip", "band")),
            P(("clip", "band")),
            P(("clip", "band")),
            P(("clip", "band"), None),
            P(("clip", "band"), None),
            P(("clip", "band")),
            P(("clip", "band")),
            P(("clip", "band"), None),
            P(("clip", "band"), None),
            P(("clip", "band"), None, None, None, None),
        ),
        out_specs=(
            P(("clip", "band"), None, None, None, None),
            P(("clip", "band"), None, None),
            P(),
            P(),
            P(),
            P(),
            P(),
            P(),
            P(),
            P(),
            P(),
            P(),
            P(),
            P(),
            P(),
            P(),
            P(),
            P(),
            P(),
            P(),
        ),
        check_vma=False,
    )
```

```python
import functools
import math

import jax
import jax.numpy as jnp
from jax import lax
from jax.experimental import pallas as pl
from jax.experimental.pallas import tpu as pltpu
from jax.sharding import PartitionSpec as P

HEADS_ENC = 12
D_DEC = 512
HEADS_DEC = 16
TIME = 64
FREQ = 8
WINDOW = 4
SHIFT = 2
norm_eps = 1e-06
neg_fill = -1e30
F32 = jnp.float32
BF16 = jnp.bfloat16
LANES = 128
VMEM_BYTES = 58 * 1024 * 1024


def mm(a, b):
    return lax.dot_general(a, b, (((1,), (0,)), ((), ())), preferred_element_type=F32)


def mm_t(a, b):
    return lax.dot_general(a, b, (((1,), (1,)), ((), ())), preferred_element_type=F32)


def bmm(a, b):
    return lax.dot_general(a, b, (((2,), (1,)), ((0,), (0,))), preferred_element_type=F32)


def bmm_t(a, b):
    return lax.dot_general(a, b, (((2,), (2,)), ((0,), (0,))), preferred_element_type=F32)


def bmm_l(a, b):
    return lax.dot_general(a, b, (((1,), (1,)), ((0,), (0,))), preferred_element_type=F32)


def normalise(x):
    centre = jnp.mean(x, axis=-1, keepdims=True)
    centred = x - centre
    rstd = lax.rsqrt(jnp.mean(centred * centred, axis=-1, keepdims=True) + norm_eps)
    return centred * rstd, rstd


def norm_back(da, xhat, rstd, gain):
    dag = da * gain
    return rstd * (
        dag
        - jnp.mean(dag, axis=-1, keepdims=True)
        - xhat * jnp.mean(dag * xhat, axis=-1, keepdims=True)
    )


def gelu_parts(u):
    size = jnp.abs(u) * 0.7071067811865476
    bell = jnp.exp(-0.5 * u * u)
    t = 1.0 / (1.0 + 0.3275911 * size)
    poly = 0.530702715
    poly = poly * t - 0.726576013
    poly = poly * t + 0.710706871
    poly = poly * t - 0.142248368
    poly = poly * t + 0.127414796
    tail = poly * t * bell
    cdf = jnp.where(u >= 0, 1.0 - tail, tail)
    return cdf, u * bell * 0.3989422804014327


def vectors_of(small_ref):
    return small_ref[...].astype(F32).T[0:8, :]


def columns_of_vectors(vectors):
    count, width = vectors.shape
    block = jnp.concatenate([vectors, jnp.zeros((LANES - count, width), F32)], axis=0)
    return block.T.astype(BF16)


def segment_sum(x, ones):
    high = x.astype(BF16)
    low = (x - high.astype(F32)).astype(BF16)
    return mm(high, ones) + mm(low, ones)


def window_max(s):
    ahead = s
    behind = s
    for step in (1, 2, 4, 8):
        ahead = jnp.maximum(ahead, pltpu.roll(ahead, step, 1))
        behind = jnp.maximum(behind, pltpu.roll(behind, LANES - step, 1))
    return jnp.maximum(ahead, behind)


def decoder_kernel(
    rows_ref, idx_ref, cot_ref, pos_ref, mask_ref, small_ref, wqkv_ref, wo_ref, wu_ref, wd_ref,
    out_ref, ret_ref, grad_ref,
    acc_qkv, acc_o, acc_u, acc_d, gvec_ref, vec_ref,
    x_s, qkv_s, p_s, o_s, a2_s, a2t_s, dzt_s, da_s, y_s, dqkv_s,
):
    step = pl.program_id(0)
    last = pl.num_programs(0) - 1
    halves, cells, width = cot_ref.shape
    m_rows = halves * cells
    slots = rows_ref.shape[1]
    head_dim = width // HEADS_DEC
    heads_in = LANES // head_dim
    groups = width // LANES
    block = LANES // heads_in
    blocks = m_rows // block
    scale = head_dim ** (-0.5)
    ff = wu_ref.shape[1]
    chunk = 512

    @pl.when(step == 0)
    def _():
        acc_qkv[...] = jnp.zeros_like(acc_qkv)
        acc_o[...] = jnp.zeros_like(acc_o)
        acc_u[...] = jnp.zeros_like(acc_u)
        acc_d[...] = jnp.zeros_like(acc_d)
        gvec_ref[...] = jnp.zeros_like(gvec_ref)
        vec_ref[...] = vectors_of(small_ref)

    gain1, shift1 = vec_ref[0:1, :], vec_ref[1:2, :]
    gain2, shift2 = vec_ref[2:3, :], vec_ref[3:4, :]
    token = vec_ref[4:5, :]

    def place_of(h):
        cell = lax.broadcasted_iota(jnp.int32, (cells, slots), 0)
        return cell == idx_ref[h]

    unseen = []
    for h in range(halves):
        place = place_of(h)
        unseen_h = 1.0 - jnp.sum(place.astype(F32), axis=1, keepdims=True)
        unseen.append(unseen_h)
        x_s[h * cells : (h + 1) * cells, :] = (
            mm(place.astype(BF16), rows_ref[h]) + unseen_h * token + pos_ref[...]
        )
    xhat1, rstd1 = normalise(x_s[...])
    a1 = (xhat1 * gain1 + shift1).astype(BF16)
    qkv_s[...] = mm(a1, wqkv_ref[...]).astype(BF16)

    lane = lax.broadcasted_iota(jnp.int32, (1, LANES), 1)
    head_masks = [(lane // head_dim == h) for h in range(heads_in)]
    ones = (
        lax.broadcasted_iota(jnp.int32, (LANES, LANES), 0) // block
        == lax.broadcasted_iota(jnp.int32, (LANES, LANES), 1) // block
    ).astype(BF16)

    def spread(t):
        parts = [t * hm.astype(BF16)[None] for hm in head_masks]
        return jnp.concatenate(parts, axis=1)

    def fold(t):
        out = t[:, 0:block, :]
        for h in range(1, heads_in):
            out = jnp.where(head_masks[h][None], t[:, h * block : (h + 1) * block, :], out)
        return out

    def part(ref, base, g):
        return ref[:, base + g * LANES : base + (g + 1) * LANES].reshape(blocks, block, LANES)

    allowed = jnp.concatenate([mask_ref[...]] * halves, axis=0) > 0.5
    for g in range(groups):
        q3 = part(qkv_s, 0, g)
        k3 = spread(part(qkv_s, width, g))
        v3 = spread(part(qkv_s, 2 * width, g))
        s = bmm_t(q3, k3).reshape(m_rows, LANES) * scale
        s = jnp.where(allowed, s, neg_fill)
        e = jnp.where(allowed, jnp.exp(s - window_max(s)), 0.0)
        p = e / segment_sum(e, ones)
        p_s[:, g * LANES : (g + 1) * LANES] = p
        o = bmm(p.astype(BF16).reshape(blocks, block, LANES), v3)
        o_s[:, g * LANES : (g + 1) * LANES] = o.reshape(m_rows, LANES).astype(BF16)

    x2 = x_s[...] + mm(o_s[...], wo_ref[...])
    xhat2, rstd2 = normalise(x2)
    a2 = (xhat2 * gain2 + shift2).astype(BF16)
    a2_s[...] = a2
    a2t_s[...] = a2.T
    dz = cot_ref[...].reshape(m_rows, width)
    dzt_s[...] = dz.T
    y_s[...] = x2
    da_s[...] = jnp.zeros_like(da_s)

    def ff_body(c, carry):
        at = pl.ds(pl.multiple_of(c * chunk, chunk), chunk)
        wu = wu_ref[:, at]
        wd = wd_ref[at, :]
        dzc = cot_ref[...].reshape(m_rows, width)
        u = mm(a2_s[...], wu)
        dh = mm_t(dzc, wd)
        cdf, bump = gelu_parts(u)
        h = (u * cdf).astype(BF16)
        du = ((cdf + bump) * dh).astype(BF16)
        y_s[...] += mm(h, wd)
        acc_d[:, at] += mm(dzt_s[...], h)
        acc_u[:, at] += mm(a2t_s[...], du)
        da_s[...] += mm_t(du, wu)
        return carry

    lax.fori_loop(0, ff // chunk, ff_body, 0)

    out_ref[...] = y_s[...].reshape(halves, cells, width).astype(BF16)
    da2 = da_s[...]
    gvec_ref[2:3, :] += jnp.sum(da2 * xhat2, axis=0, keepdims=True)
    gvec_ref[3:4, :] += jnp.sum(da2, axis=0, keepdims=True)
    dx2 = cot_ref[...].reshape(m_rows, width).astype(F32) + norm_back(da2, xhat2, rstd2, gain2)
    dy2 = dx2.astype(BF16)
    acc_o[...] += mm(o_s[...].T, dy2)
    do = mm_t(dy2, wo_ref[...]).astype(BF16)

    for g in range(groups):
        cols = slice(g * LANES, (g + 1) * LANES)
        q3 = part(qkv_s, 0, g)
        k3 = spread(part(qkv_s, width, g))
        v3 = spread(part(qkv_s, 2 * width, g))
        do3 = do[:, cols].reshape(blocks, block, LANES)
        p = p_s[:, cols]
        dp = bmm_t(do3, v3).reshape(m_rows, LANES)
        draw = (p * (dp - segment_sum(p * dp, ones)) * scale).astype(BF16)
        draw3 = draw.reshape(blocks, block, LANES)
        dq = bmm(draw3, k3).reshape(m_rows, LANES)
        dk = fold(bmm_l(draw3, q3)).reshape(m_rows, LANES)
        dv = fold(bmm_l(p.astype(BF16).reshape(blocks, block, LANES), do3)).reshape(m_rows, LANES)
        dqkv_s[:, g * LANES : (g + 1) * LANES] = dq.astype(BF16)
        dqkv_s[:, width + g * LANES : width + (g + 1) * LANES] = dk.astype(BF16)
        dqkv_s[:, 2 * width + g * LANES : 2 * width + (g + 1) * LANES] = dv.astype(BF16)

    xhat1, rstd1 = normalise(x_s[...])
    a1 = (xhat1 * gain1 + shift1).astype(BF16)
    dqkv = dqkv_s[...]
    acc_qkv[...] += mm(a1.T, dqkv)
    da1 = mm_t(dqkv, wqkv_ref[...])
    gvec_ref[0:1, :] += jnp.sum(da1 * xhat1, axis=0, keepdims=True)
    gvec_ref[1:2, :] += jnp.sum(da1, axis=0, keepdims=True)
    dx = dx2 + norm_back(da1, xhat1, rstd1, gain1)
    for h in range(halves):
        dx_h = dx[h * cells : (h + 1) * cells, :]
        gvec_ref[4:5, :] += jnp.sum(unseen[h] * dx_h, axis=0, keepdims=True)
        place = place_of(h).astype(F32).T.astype(BF16)
        ret_ref[h] = mm(place, dx_h.astype(BF16)).astype(BF16)

    @pl.when(step == last)
    def _():
        grad_ref[:, : 3 * width] = acc_qkv[...].astype(BF16)
        grad_ref[:, 3 * width : 4 * width] = acc_o[...].astype(BF16)
        grad_ref[:, 4 * width : 4 * width + ff] = acc_u[...].astype(BF16)
        grad_ref[:, 4 * width + ff : 4 * width + 2 * ff] = acc_d[...].astype(BF16)
        grad_ref[:, 4 * width + 2 * ff :] = columns_of_vectors(gvec_ref[...])


def decoder_block(rows, idx, cot, pos, mask, pack, wd):
    n_half, slots, width = rows.shape
    cells = cot.shape[1]
    ff = wd.shape[0]
    halves = 2
    m_rows = halves * cells
    vm = pltpu.VMEM
    flops = 6 * n_half * cells * (4 * width + 2 * ff) * width * 2

    def whole(*shape, at=0):
        index = (0,) * (len(shape) - 1) + (at,)
        return pl.BlockSpec(shape, lambda i: index, pipeline_mode=pl.Buffered(1))

    return pl.pallas_call(
        decoder_kernel,
        grid=(n_half // halves,),
        in_specs=[
            pl.BlockSpec((halves, slots, width), lambda i: (i, 0, 0)),
            pl.BlockSpec((halves, 1, slots), lambda i: (i, 0, 0)),
            pl.BlockSpec((halves, cells, width), lambda i: (i, 0, 0)),
            whole(cells, width),
            whole(cells, LANES),
            whole(width, LANES, at=(4 * width + 2 * ff) // LANES),
            whole(width, 3 * width),
            whole(width, width, at=3),
            whole(width, ff, at=1),
            whole(ff, width),
        ],
        out_specs=[
            pl.BlockSpec((halves, cells, width), lambda i: (i, 0, 0)),
            pl.BlockSpec((halves, slots, width), lambda i: (i, 0, 0)),
            whole(width, 4 * width + 2 * ff + LANES),
        ],
        out_shape=[
            jax.ShapeDtypeStruct((n_half, cells, width), BF16),
            jax.ShapeDtypeStruct((n_half, slots, width), BF16),
            jax.ShapeDtypeStruct((width, 4 * width + 2 * ff + LANES), BF16),
        ],
        scratch_shapes=[
            vm((width, 3 * width), F32),
            vm((width, width), F32),
            vm((width, ff), F32),
            vm((width, ff), F32),
            vm((8, width), F32),
            vm((8, width), F32),
            vm((m_rows, width), F32),
            vm((m_rows, 3 * width), BF16),
            vm((m_rows, width), F32),
            vm((m_rows, width), BF16),
            vm((m_rows, width), BF16),
            vm((width, m_rows), BF16),
            vm((width, m_rows), BF16),
            vm((m_rows, width), F32),
            vm((m_rows, width), F32),
            vm((m_rows, 3 * width), BF16),
        ],
        compiler_params=pltpu.CompilerParams(
            dimension_semantics=("arbitrary",), vmem_limit_bytes=VMEM_BYTES
        ),
        cost_estimate=pl.CostEstimate(flops=flops, bytes_accessed=40 << 20, transcendentals=0),
        name="decoder_block",
    )(rows, idx.reshape(n_half, 1, slots), cot, pos, mask, pack, pack, pack, pack, wd)


def enc_spread(t, head_masks):
    return jnp.concatenate([t * hm.astype(BF16)[None] for hm in head_masks], axis=1)


def enc_heads(width):
    head_dim = width // HEADS_ENC
    lane = lax.broadcasted_iota(jnp.int32, (1, LANES), 1)
    return head_dim, [(lane // head_dim == h) for h in range(LANES // head_dim)]


def enc_attend_kernel(
    x_ref, mask_ref, small_ref, wqkv_ref, wo_ref, qkv_ref, p_ref, o_ref, x2_ref, vec_ref
):
    vec_ref[...] = vectors_of(small_ref)
    clips, slots, width = x_ref.shape
    m_rows = clips * slots
    head_dim, head_masks = enc_heads(width)
    scale = head_dim ** (-0.5)
    x = x_ref[...].reshape(m_rows, width).astype(F32)
    xhat, rstd = normalise(x)
    a1 = (xhat * vec_ref[0:1, :] + vec_ref[1:2, :]).astype(BF16)
    qkv_ref[...] = mm(a1, wqkv_ref[...]).astype(BF16)
    allowed = mask_ref[...] > 0.5
    for g in range(width // LANES):
        cols = lambda part: slice(part * width + g * LANES, part * width + (g + 1) * LANES)
        q3 = qkv_ref[:, cols(0)].reshape(clips, slots, LANES)
        k3 = enc_spread(qkv_ref[:, cols(1)].reshape(clips, slots, LANES), head_masks)
        v3 = enc_spread(qkv_ref[:, cols(2)].reshape(clips, slots, LANES), head_masks)
        s = bmm_t(q3, k3) * scale
        for h in range(len(head_masks)):
            sh = jnp.where(allowed, s[:, :, h * slots : (h + 1) * slots], neg_fill)
            e = jnp.exp(sh - jnp.max(sh, axis=-1, keepdims=True))
            e = e / jnp.sum(e, axis=-1, keepdims=True)
            at = (g * len(head_masks) + h) * slots
            p_ref[:, at : at + slots] = e.reshape(m_rows, slots).astype(BF16)
        span = len(head_masks) * slots
        p3 = p_ref[:, g * span : (g + 1) * span].reshape(clips, slots, span)
        o_ref[:, cols(0)] = bmm(p3, v3).reshape(m_rows, LANES).astype(BF16)
    x2_ref[...] = x_ref[...].reshape(m_rows, width).astype(F32) + mm(o_ref[...], wo_ref[...])


def enc_feed_kernel(
    x2_ref, vec_ref, wu_ref, wd_ref, proj_ref, sent_ref, enc_ref, h_ref, gp_ref, a2_s, y_s
):
    ff = wu_ref.shape[1]
    chunk = 512
    xhat, rstd = normalise(x2_ref[...])
    a2_s[...] = (xhat * vec_ref[2:3, :] + vec_ref[3:4, :]).astype(BF16)
    y_s[...] = x2_ref[...]

    def body(c, carry):
        at = pl.ds(pl.multiple_of(c * chunk, chunk), chunk)
        u = mm(a2_s[...], wu_ref[:, at])
        cdf, bump = gelu_parts(u)
        h = (u * cdf).astype(BF16)
        h_ref[:, at] = h
        gp_ref[:, at] = (cdf + bump).astype(BF16)
        y_s[...] += mm(h, wd_ref[at, :])
        return carry

    lax.fori_loop(0, ff // chunk, body, 0)
    encoded = y_s[...].astype(BF16)
    enc_ref[...] = encoded
    sent_ref[...] = mm(encoded, proj_ref[...]).astype(BF16)


def enc_feed_back_kernel(
    dsent_ref, enc_ref, proj_ref, h_ref, gp_ref, x2_ref, vec_ref, wu_ref, wd_ref,
    gproj_ref, grad_ref, dx2_ref, gvec_ref,
    a2t_s, dz_s, dzt_s, da_s,
):
    ff = wu_ref.shape[1]
    chunk = 512
    gain2 = vec_ref[2:3, :]
    dsent = dsent_ref[...]
    gproj_ref[...] = mm(enc_ref[...].T, dsent).astype(BF16)
    dy = mm_t(dsent, proj_ref[...])
    dx2_ref[...] = dy
    dz = dy.astype(BF16)
    dz_s[...] = dz
    dzt_s[...] = dz.T
    xhat, rstd = normalise(x2_ref[...])
    a2t_s[...] = (xhat * gain2 + vec_ref[3:4, :]).astype(BF16).T
    da_s[...] = jnp.zeros_like(da_s)

    def body(c, carry):
        at = pl.ds(pl.multiple_of(c * chunk, chunk), chunk)
        dh = mm_t(dz_s[...], wd_ref[at, :])
        du = (gp_ref[:, at].astype(F32) * dh).astype(BF16)
        below = pl.ds(pl.multiple_of(ff + c * chunk, chunk), chunk)
        grad_ref[:, at] = mm(a2t_s[...], du).astype(BF16)
        grad_ref[:, below] = mm(dzt_s[...], h_ref[:, at]).astype(BF16)
        da_s[...] += mm_t(du, wu_ref[:, at])
        return carry

    lax.fori_loop(0, ff // chunk, body, 0)
    da = da_s[...]
    xhat, rstd = normalise(x2_ref[...])
    gvec_ref[...] = jnp.zeros_like(gvec_ref)
    gvec_ref[2:3, :] = jnp.sum(da * xhat, axis=0, keepdims=True)
    gvec_ref[3:4, :] = jnp.sum(da, axis=0, keepdims=True)
    dx2_ref[...] += norm_back(da, xhat, rstd, gain2)


def enc_attend_back_kernel(
    dx2_ref, o_ref, qkv_ref, p_ref, x_ref, vec_ref, wqkv_ref, wo_ref, gproj_ref, gvec2_ref,
    grad_ref, dvis_ref,
    gvec_ref, do_s, dqkv_s,
):
    clips, slots, width = x_ref.shape
    m_rows = clips * slots
    head_dim, head_masks = enc_heads(width)
    count = len(head_masks)
    scale = head_dim ** (-0.5)
    gain1, shift1 = vec_ref[0:1, :], vec_ref[1:2, :]
    dy2 = dx2_ref[...].astype(BF16)
    grad_ref[:, 3 * width : 4 * width] = mm(o_ref[...].T, dy2).astype(BF16)
    do_s[...] = mm_t(dy2, wo_ref[...]).astype(BF16)

    def fold(t):
        out = t[:, 0:slots, :]
        for h in range(1, count):
            out = jnp.where(head_masks[h][None], t[:, h * slots : (h + 1) * slots, :], out)
        return out.reshape(m_rows, LANES).astype(BF16)

    for g in range(width // LANES):
        cols = lambda part: slice(part * width + g * LANES, part * width + (g + 1) * LANES)
        q3 = qkv_ref[:, cols(0)].reshape(clips, slots, LANES)
        k3 = enc_spread(qkv_ref[:, cols(1)].reshape(clips, slots, LANES), head_masks)
        v3 = enc_spread(qkv_ref[:, cols(2)].reshape(clips, slots, LANES), head_masks)
        do3 = do_s[:, cols(0)].reshape(clips, slots, LANES)
        span = count * slots
        p3 = p_ref[:, g * span : (g + 1) * span].reshape(clips, slots, span)
        dp = bmm_t(do3, v3)
        parts = []
        for h in range(count):
            hs = slice(h * slots, (h + 1) * slots)
            ph = p3[:, :, hs].astype(F32)
            dph = dp[:, :, hs]
            mean = jnp.sum(ph * dph, axis=-1, keepdims=True)
            parts.append((ph * (dph - mean) * scale).astype(BF16))
        draw3 = jnp.concatenate(parts, axis=2)
        dqkv_s[:, cols(0)] = bmm(draw3, k3).reshape(m_rows, LANES).astype(BF16)
        dqkv_s[:, cols(1)] = fold(bmm_l(draw3, q3))
        dqkv_s[:, cols(2)] = fold(bmm_l(p3, do3))

    x = x_ref[...].reshape(m_rows, width).astype(F32)
    xhat, rstd = normalise(x)
    a1t = (xhat * gain1 + shift1).astype(BF16).T
    grad_ref[:, : 3 * width] = mm(a1t, dqkv_s[...]).astype(BF16)
    da = mm_t(dqkv_s[...], wqkv_ref[...])
    gvec_ref[...] = gvec2_ref[...]
    gvec_ref[0:1, :] = jnp.sum(da * xhat, axis=0, keepdims=True)
    gvec_ref[1:2, :] = jnp.sum(da, axis=0, keepdims=True)
    dx = dx2_ref[...] + norm_back(da, xhat, rstd, gain1)
    dvis_ref[...] = dx.reshape(clips, slots, width).astype(BF16)
    grad_ref[:, 4 * width : -LANES] = gproj_ref[...]
    grad_ref[:, -LANES:] = columns_of_vectors(gvec_ref[...])


def whole_call(kernel, args, outs, scratch, name, flops):
    arrays, specs = [], []
    for arg in args:
        array, shape, at = arg if isinstance(arg, tuple) else (arg, arg.shape, 0)
        index = (0,) * (len(shape) - 1) + (at,)
        arrays.append(array)
        specs.append(pl.BlockSpec(shape, lambda i, index=index: index, pipeline_mode=pl.Buffered(1)))
    zero = lambda shape: pl.BlockSpec(shape, lambda i: (0,) * len(shape), pipeline_mode=pl.Buffered(1))
    return pl.pallas_call(
        kernel,
        grid=(1,),
        in_specs=specs,
        out_specs=[zero(s) for s, _ in outs],
        out_shape=[jax.ShapeDtypeStruct(s, d) for s, d in outs],
        scratch_shapes=[pltpu.VMEM(s, d) for s, d in scratch],
        compiler_params=pltpu.CompilerParams(vmem_limit_bytes=VMEM_BYTES),
        cost_estimate=pl.CostEstimate(flops=flops, bytes_accessed=16 << 20, transcendentals=0),
        name=name,
    )(*arrays)


def enc_blocks(pack, width, ff, sent):
    return (
        (pack, (width, 3 * width), 0),
        (pack, (width, width), 3),
        (pack, (width, ff), 4 * width // ff),
        (pack, (width, sent), (4 * width + ff) // sent),
        (pack, (width, LANES), (4 * width + ff + sent) // LANES),
    )


def enc_attend(x, mask, blocks):
    clips, slots, width = x.shape
    m = clips * slots
    outs = [
        ((m, 3 * width), BF16),
        ((m, HEADS_ENC * slots), BF16),
        ((m, width), BF16),
        ((m, width), F32),
        ((8, width), F32),
    ]
    qkv, out, _, _, small = blocks
    return whole_call(enc_attend_kernel, (x, mask, small, qkv, out), outs, [], "enc_attend", 10**10)


def enc_feed(x2, vecs, blocks, wd):
    m, width = x2.shape
    ff = wd.shape[0]
    _, _, up, proj, _ = blocks
    outs = [((m, proj[1][1]), BF16), ((m, width), BF16), ((m, ff), BF16), ((m, ff), BF16)]
    scratch = [((m, width), BF16), ((m, width), F32)]
    return whole_call(enc_feed_kernel, (x2, vecs, up, wd, proj), outs, scratch, "enc_feed", 18 * 10**9)


def enc_feed_back(dsent, enc, h, gp, x2, vecs, blocks, wd):
    m, width = x2.shape
    ff = wd.shape[0]
    _, _, up, proj, _ = blocks
    outs = [(proj[1], BF16), ((width, 2 * ff), BF16), ((m, width), F32), ((8, width), F32)]
    scratch = [((width, m), BF16), ((m, width), BF16), ((width, m), BF16), ((m, width), F32)]
    args = (dsent, enc, proj, h, gp, x2, vecs, up, wd)
    return whole_call(enc_feed_back_kernel, args, outs, scratch, "enc_feed_back", 24 * 10**9)


def enc_attend_back(dx2, o, qkv, p, x, vecs, blocks, gproj, gvec):
    m, width = dx2.shape
    w_qkv, w_out, _, _, _ = blocks
    outs = [((width, 4 * width + gproj.shape[1] + LANES), BF16), (x.shape, BF16)]
    scratch = [((8, width), F32), ((m, width), BF16), ((m, 3 * width), BF16)]
    args = (dx2, o, qkv, p, x, vecs, w_qkv, w_out, gproj, gvec)
    return whole_call(enc_attend_back_kernel, args, outs, scratch, "enc_attend_back", 14 * 10**9)


def unpack_kernel(spans, tall, sum_ref, *out_refs):
    for (start, size), ref in zip(spans, out_refs[:-2]):
        ref[...] = sum_ref[:, start : start + size].astype(F32)
    start, size = tall
    chunk = 512
    for c in range(size // chunk):
        part = sum_ref[:, start + c * chunk : start + (c + 1) * chunk].astype(F32)
        out_refs[-2][c * chunk : (c + 1) * chunk, :] = part.T
    out_refs[-1][...] = sum_ref[:, start + size :].astype(F32).T[0:8, :]


def unpack_sums(packed, spans, tall):
    rows, wide = packed.shape
    step = LANES
    size = tall[1]
    side = lambda n: pl.BlockSpec((step, n), lambda i: (i, 0))
    down = lambda n: pl.BlockSpec((n, step), lambda i: (0, i))
    return pl.pallas_call(
        functools.partial(unpack_kernel, spans, tall),
        grid=(rows // step,),
        in_specs=[side(wide)],
        out_specs=[side(n) for _, n in spans] + [down(size), down(8)],
        out_shape=[jax.ShapeDtypeStruct((rows, n), F32) for _, n in spans]
        + [jax.ShapeDtypeStruct((size, rows), F32), jax.ShapeDtypeStruct((8, rows), F32)],
        compiler_params=pltpu.CompilerParams(vmem_limit_bytes=VMEM_BYTES),
        cost_estimate=pl.CostEstimate(flops=0, bytes_accessed=6 * rows * wide, transcendentals=0),
        name="unpack_sums",
    )(packed)


AXES = ("clip", "band")


def partner_pairs(total, mask):
    return [(i, i ^ mask) for i in range(total)]


def add_low(*parts):
    return sum(part.astype(F32) for part in parts).astype(BF16)


class RunningSum:
    def __init__(self, partial, total, cut):
        bits = total.bit_length() - 1
        rows = partial.shape[0] // total
        self.total = total
        self.held = [partial.reshape((2,) * bits + (rows, partial.shape[1]))]
        self.left = [list(range(bits - 1, -1, -1))]
        self.cut = cut
        self.plan = [[[0]], [[2], [1]], [[1], [2]]]
        rest = list(range(3, bits))
        while rest:
            self.plan.append([rest[:2]])
            rest = rest[2:]

    def offers(self):
        me = lax.axis_index(AXES)
        groups = self.plan[0]
        if len(groups) > len(self.held):
            (held,), (left,) = self.held, self.left
            self.held = [held[..., : self.cut], held[..., self.cut :]]
            self.left = [list(left), list(left)]
        if len(groups) < len(self.held):
            self.held = [jnp.concatenate(self.held, axis=-1)]
            self.left = self.left[:1]
        self.keep, gives, self.masks = [], [], []
        for held, left, group in zip(self.held, self.left, groups):
            low, ways = group[0], 1 << len(group)
            place = left.index(group[-1])
            mine = (me >> low) & (ways - 1)
            shape = held.shape
            held = held.reshape(shape[:place] + (ways,) + shape[place + len(group) :])
            self.keep.append(lax.dynamic_index_in_dim(held, mine, place, keepdims=False))
            for k in range(1, ways):
                gives.append(lax.dynamic_index_in_dim(held, mine ^ k, place, keepdims=False))
                self.masks.append(k << low)
            for bit in group:
                left.remove(bit)
        return gives

    def deliver(self, gives):
        got = [
            lax.ppermute(give, AXES, partner_pairs(self.total, mask))
            for give, mask in zip(gives, self.masks)
        ]
        each = len(got) // len(self.keep)
        self.held = [
            add_low(keep, *got[i * each : (i + 1) * each]) for i, keep in enumerate(self.keep)
        ]
        self.plan = self.plan[1:]

    def step(self):
        self.deliver(self.offers())

    def finish(self):
        while self.plan:
            self.step()
        return jnp.concatenate(self.held, axis=-1)


def together(*groups):
    return lax.optimization_barrier(groups)


def gather_rows(shard):
    return lax.all_gather(shard, AXES, axis=0, tiled=True)


def columns_of(vectors):
    block = jnp.stack(vectors, axis=1)
    return jnp.pad(block, ((0, 0), (0, LANES - len(vectors))))


def blocks_beside(tall, rows):
    return [tall[i : i + rows] for i in range(0, tall.shape[0], rows)]


def blocks_below(beside, total, width):
    rows = beside.shape[0] // total
    count = beside.shape[1] // width
    parts = [beside[:, i * width : (i + 1) * width].reshape(total, rows, width) for i in range(count)]
    return jnp.concatenate(parts, axis=1).reshape(-1, width)


def swap_band(array, bit):
    return lax.ppermute(array, "band", [(i, i ^ bit) for i in range(4)])


def owners_to_bands(array):
    band = lax.axis_index("band")
    half, side = band // 2, band % 2
    own = lax.dynamic_index_in_dim(array, half, 0, keepdims=False)
    got = swap_band(lax.dynamic_index_in_dim(array, 1 - half, 0, keepdims=False), 2)
    pair = jnp.stack([jnp.where(half == 0, own, got), jnp.where(half == 0, got, own)])
    other = swap_band(pair, 1)
    return jnp.stack([jnp.where(side == 0, pair, other), jnp.where(side == 0, other, pair)], axis=1)


def bands_to_owners(array):
    band = lax.axis_index("band")
    half, side = band // 2, band % 2
    own = lax.dynamic_index_in_dim(array, side, 1, keepdims=False)
    got = swap_band(lax.dynamic_index_in_dim(array, 1 - side, 1, keepdims=False), 1)
    pair = own + got
    own = lax.dynamic_index_in_dim(pair, half, 0, keepdims=False)
    got = swap_band(lax.dynamic_index_in_dim(pair, 1 - half, 0, keepdims=False), 2)
    return jnp.stack([jnp.where(half == 0, own, got), jnp.where(half == 0, got, own)])


def position_table(places):
    half_width = D_DEC // 2
    omega_vec = jnp.exp(
        jnp.arange(half_width, dtype=F32) * (-math.log(10000.0) / half_width)
    )
    angles = places.astype(F32)[..., None] * omega_vec
    return jnp.concatenate([jnp.sin(angles), jnp.cos(angles)], axis=-1)


def shards(
    visible,
    keep_index,
    visible_count,
    enc_gain1,
    enc_shift1,
    enc_qkv,
    enc_out,
    enc_gain2,
    enc_shift2,
    enc_up,
    enc_down,
    proj,
    mask_token,
    dec_gain1,
    dec_shift1,
    dec_qkv,
    dec_out,
    dec_gain2,
    dec_shift2,
    dec_up,
    dec_down,
    cotangent,
):
    total = lax.axis_size(AXES)
    enc_wide, dec_wide = enc_out.shape[1], dec_out.shape[1]
    enc_ff, dec_ff = enc_up.shape[1], dec_up.shape[1]
    enc_small = columns_of([enc_gain1, enc_shift1, enc_gain2, enc_shift2])
    enc_pack = jnp.concatenate(
        [enc_qkv, enc_out, enc_up, proj, enc_small] + blocks_beside(enc_down, enc_out.shape[0]), axis=1
    )
    enc_pack = gather_rows(enc_pack)
    enc_end = 4 * enc_wide + enc_ff + dec_wide + LANES
    whole_down = blocks_below(enc_pack[:, enc_end:], total, enc_wide)
    dec_small = columns_of([dec_gain1, dec_shift1, dec_gain2, dec_shift2, mask_token])
    dec_pack = jnp.concatenate(
        [dec_qkv, dec_out, dec_up] + blocks_beside(dec_down, dec_out.shape[0]) + [dec_small], axis=1
    )
    dec_pack = gather_rows(dec_pack)
    dec_end = 4 * dec_wide + dec_ff
    dec_whole_down = blocks_below(dec_pack[:, dec_end : dec_end + dec_ff], total, dec_wide)

    clip_count, slot_total, _ = visible.shape
    half_clips = clip_count // 2
    band_height = FREQ // 2
    slot_ids = jnp.arange(slot_total)
    valid_rows = slot_ids[None, :] < visible_count[:, None]
    valid_mask = valid_rows.astype(F32)[:, None, :]
    cell_number = jnp.where(valid_rows, keep_index, -1).reshape(2, half_clips, slot_total)
    cell_number = owners_to_bands(cell_number).reshape(-1, slot_total)
    band_pick = lax.axis_index("band") % 2
    rolled_time = (cell_number // FREQ + TIME - SHIFT) % TIME
    rolled_freq = (cell_number % FREQ + FREQ - SHIFT) % FREQ
    here = (cell_number >= 0) & (rolled_freq // band_height == band_pick)
    arrived_index = jnp.where(here, rolled_time * band_height + rolled_freq % band_height, -1)

    blocks = enc_blocks(enc_pack, enc_wide, enc_ff, dec_wide)
    qkv, probs, mixed, middle, vecs = enc_attend(visible, valid_mask, blocks)
    sent_rows, encoded, hidden, slope = enc_feed(middle, vecs, blocks, whole_down)
    arrived_rows = owners_to_bands(sent_rows.reshape(2, half_clips, slot_total, dec_wide))
    half_total = 4 * half_clips

    cell_count = TIME * band_height
    places = jnp.arange(cell_count)
    cell_freq = band_pick * band_height + places % band_height
    patch_number = (places // band_height + SHIFT) % TIME * FREQ + (cell_freq + SHIFT) % FREQ
    span = D_DEC // HEADS_DEC
    query = places[:, None]
    key = query // span * span + jnp.arange(LANES)[None, :] % span

    def label(cell):
        late = cell // band_height >= TIME - SHIFT
        high = band_pick * band_height + cell % band_height >= FREQ - SHIFT
        return late.astype(jnp.int32) * 2 + high.astype(jnp.int32)

    cells_in = WINDOW * WINDOW
    allowed = (query // cells_in == key // cells_in) & (label(query) == label(key))
    decoded, returning, dec_grad = decoder_block(
        arrived_rows.reshape(half_total, slot_total, dec_wide),
        arrived_index,
        cotangent.reshape(half_total, cell_count, dec_wide),
        position_table(patch_number),
        allowed.astype(F32),
        dec_pack,
        dec_whole_down,
    )
    decoded_out = decoded.reshape(cotangent.shape)

    middle_cut = lambda grad: grad.shape[1] // 256 * 128
    dec_run = RunningSum(dec_grad, total, middle_cut(dec_grad))
    dec_run.step()
    grad_sent = bands_to_owners(returning.reshape(2, 2, half_clips, slot_total, dec_wide))
    grad_sent = grad_sent.reshape(-1, dec_wide)
    grad_sent, gives = together(grad_sent, dec_run.offers())
    dec_run.deliver(gives)
    g_proj, grad_feed, grad_middle, g_vec = enc_feed_back(
        grad_sent, encoded, hidden, slope, middle, vecs, blocks, whole_down
    )
    grad_feed, grad_middle, gives = together(grad_feed, grad_middle, dec_run.offers())
    dec_run.deliver(gives)
    feed_run = RunningSum(grad_feed, total, enc_ff)
    feed_run.step()
    grad_attend, grad_visible = enc_attend_back(
        grad_middle, mixed, qkv, probs, visible, vecs, blocks, g_proj, g_vec
    )
    grad_attend, gives, feed_gives = together(grad_attend, dec_run.offers(), feed_run.offers())
    dec_run.deliver(gives)
    feed_run.deliver(feed_gives)
    attend_run = RunningSum(grad_attend, total, middle_cut(grad_attend))
    attend_run.step()
    dec_shard = dec_run.finish()
    dec_shard, feed_gives, gives = together(dec_shard, feed_run.offers(), attend_run.offers())
    dec_sum = gather_rows(dec_shard)
    feed_run.deliver(feed_gives)
    feed_gives, gives = together(feed_run.offers(), gives)
    feed_run.deliver(feed_gives)
    attend_run.deliver(gives)
    attend_run.step()
    feed_sum = feed_run.finish()
    attend_sum = attend_run.finish()
    small_at = attend_sum.shape[1] - LANES
    enc_shard = jnp.concatenate(
        [attend_sum[:, :small_at], feed_sum, attend_sum[:, small_at:]], axis=1
    )
    enc_sum = gather_rows(enc_shard)

    spans = [(0, 3 * dec_wide), (3 * dec_wide, dec_wide), (4 * dec_wide, dec_ff)]
    d_qkv, d_out, d_up, d_down, dec_vecs = unpack_sums(dec_sum, spans, (dec_end, dec_ff))
    start = 4 * enc_wide + dec_wide
    spans = [(0, 3 * enc_wide), (3 * enc_wide, enc_wide), (4 * enc_wide, dec_wide), (start, enc_ff)]
    e_qkv, e_out, e_proj, e_up, e_down, enc_vecs = unpack_sums(enc_sum, spans, (start + enc_ff, enc_ff))
    return (
        decoded_out,
        grad_visible,
        enc_vecs[0],
        enc_vecs[1],
        e_qkv,
        e_out,
        enc_vecs[2],
        enc_vecs[3],
        e_up,
        e_down,
        e_proj,
        dec_vecs[4],
        dec_vecs[0],
        dec_vecs[1],
        d_qkv,
        d_out,
        dec_vecs[2],
        dec_vecs[3],
        d_up,
        d_down,
    )


def solution(mesh):
    return jax.shard_map(
        shards,
        mesh=mesh,
        in_specs=(
            P(("clip", "band"), None, None),
            P(("clip", "band"), None),
            P(("clip", "band")),
            P(("clip", "band")),
            P(("clip", "band")),
            P(("clip", "band"), None),
            P(("clip", "band"), None),
            P(("clip", "band")),
            P(("clip", "band")),
            P(("clip", "band"), None),
            P(("clip", "band"), None),
            P(("clip", "band"), None),
            P(("clip", "band")),
            P(("clip", "band")),
            P(("clip", "band")),
            P(("clip", "band"), None),
            P(("clip", "band"), None),
            P(("clip", "band")),
            P(("clip", "band")),
            P(("clip", "band"), None),
            P(("clip", "band"), None),
            P(("clip", "band"), None, None, None, None),
        ),
        out_specs=(
            P(("clip", "band"), None, None, None, None),
            P(("clip", "band"), None, None),
            P(),
            P(),
            P(),
            P(),
            P(),
            P(),
            P(),
            P(),
            P(),
            P(),
            P(),
            P(),
            P(),
            P(),
            P(),
            P(),
            P(),
            P(),
        ),
        check_vma=False,
    )
```

```python
import functools
import math

import jax
import jax.numpy as jnp
from jax import lax
from jax.experimental import pallas as pl
from jax.experimental.pallas import tpu as pltpu
from jax.sharding import PartitionSpec as P

HEADS_ENC = 12
D_DEC = 512
HEADS_DEC = 16
TIME = 64
FREQ = 8
WINDOW = 4
SHIFT = 2
norm_eps = 1e-06
neg_fill = -1e30
F32 = jnp.float32
BF16 = jnp.bfloat16
LANES = 128
VMEM_BYTES = 58 * 1024 * 1024


def mm(a, b):
    return lax.dot_general(a, b, (((1,), (0,)), ((), ())), preferred_element_type=F32)


def mm_t(a, b):
    return lax.dot_general(a, b, (((1,), (1,)), ((), ())), preferred_element_type=F32)


def bmm(a, b):
    return lax.dot_general(a, b, (((2,), (1,)), ((0,), (0,))), preferred_element_type=F32)


def bmm_t(a, b):
    return lax.dot_general(a, b, (((2,), (2,)), ((0,), (0,))), preferred_element_type=F32)


def bmm_l(a, b):
    return lax.dot_general(a, b, (((1,), (1,)), ((0,), (0,))), preferred_element_type=F32)


def normalise(x):
    centre = jnp.mean(x, axis=-1, keepdims=True)
    centred = x - centre
    rstd = lax.rsqrt(jnp.mean(centred * centred, axis=-1, keepdims=True) + norm_eps)
    return centred * rstd, rstd


def norm_back(da, xhat, rstd, gain):
    dag = da * gain
    return rstd * (
        dag
        - jnp.mean(dag, axis=-1, keepdims=True)
        - xhat * jnp.mean(dag * xhat, axis=-1, keepdims=True)
    )


def gelu_parts(u):
    size = jnp.abs(u) * 0.7071067811865476
    bell = jnp.exp(-0.5 * u * u)
    t = 1.0 / (1.0 + 0.3275911 * size)
    poly = 0.530702715
    poly = poly * t - 0.726576013
    poly = poly * t + 0.710706871
    poly = poly * t - 0.142248368
    poly = poly * t + 0.127414796
    tail = poly * t * bell
    cdf = jnp.where(u >= 0, 1.0 - tail, tail)
    return cdf, u * bell * 0.3989422804014327


def vectors_of(small_ref):
    return small_ref[...].astype(F32).T[0:8, :]


def columns_of_vectors(vectors):
    count, width = vectors.shape
    block = jnp.concatenate([vectors, jnp.zeros((LANES - count, width), F32)], axis=0)
    return block.T.astype(BF16)


def by_core(core_ref, fill, keep_ref, give_ref):
    @pl.when(core_ref[0] == 0)
    def _():
        fill(keep_ref, give_ref)

    @pl.when(core_ref[0] != 0)
    def _():
        fill(give_ref, keep_ref)


def segment_sum(x, ones):
    high = x.astype(BF16)
    low = (x - high.astype(F32)).astype(BF16)
    return mm(high, ones) + mm(low, ones)


def window_max(s):
    ahead = s
    behind = s
    for step in (1, 2, 4, 8):
        ahead = jnp.maximum(ahead, pltpu.roll(ahead, step, 1))
        behind = jnp.maximum(behind, pltpu.roll(behind, LANES - step, 1))
    return jnp.maximum(ahead, behind)


def decoder_kernel(
    core_ref, rows_ref, idx_ref, cot_ref, pos_ref, mask_ref, small_ref, wqkv_ref, wo_ref, wu_ref, wd_ref,
    out_ref, ret_ref, keep_ref, give_ref,
    acc_qkv, acc_o, acc_u, acc_d, gvec_ref, vec_ref,
    x_s, qkv_s, p_s, o_s, a2_s, a2t_s, dzt_s, da_s, y_s, dqkv_s,
):
    step = pl.program_id(0)
    last = pl.num_programs(0) - 1
    halves, cells, width = cot_ref.shape
    m_rows = halves * cells
    slots = rows_ref.shape[1]
    head_dim = width // HEADS_DEC
    heads_in = LANES // head_dim
    groups = width // LANES
    block = LANES // heads_in
    blocks = m_rows // block
    scale = head_dim ** (-0.5)
    ff = wu_ref.shape[1]
    chunk = 512

    @pl.when(step == 0)
    def _():
        acc_qkv[...] = jnp.zeros_like(acc_qkv)
        acc_o[...] = jnp.zeros_like(acc_o)
        acc_u[...] = jnp.zeros_like(acc_u)
        acc_d[...] = jnp.zeros_like(acc_d)
        gvec_ref[...] = jnp.zeros_like(gvec_ref)
        vec_ref[...] = vectors_of(small_ref)

    gain1, shift1 = vec_ref[0:1, :], vec_ref[1:2, :]
    gain2, shift2 = vec_ref[2:3, :], vec_ref[3:4, :]
    token = vec_ref[4:5, :]

    def place_of(h):
        cell = lax.broadcasted_iota(jnp.int32, (cells, slots), 0)
        return cell == idx_ref[h]

    unseen = []
    for h in range(halves):
        place = place_of(h)
        unseen_h = 1.0 - jnp.sum(place.astype(F32), axis=1, keepdims=True)
        unseen.append(unseen_h)
        x_s[h * cells : (h + 1) * cells, :] = (
            mm(place.astype(BF16), rows_ref[h]) + unseen_h * token + pos_ref[...]
        )
    xhat1, rstd1 = normalise(x_s[...])
    a1 = (xhat1 * gain1 + shift1).astype(BF16)
    qkv_s[...] = mm(a1, wqkv_ref[...]).astype(BF16)

    lane = lax.broadcasted_iota(jnp.int32, (1, LANES), 1)
    head_masks = [(lane // head_dim == h) for h in range(heads_in)]
    ones = (
        lax.broadcasted_iota(jnp.int32, (LANES, LANES), 0) // block
        == lax.broadcasted_iota(jnp.int32, (LANES, LANES), 1) // block
    ).astype(BF16)

    def spread(t):
        parts = [t * hm.astype(BF16)[None] for hm in head_masks]
        return jnp.concatenate(parts, axis=1)

    def fold(t):
        out = t[:, 0:block, :]
        for h in range(1, heads_in):
            out = jnp.where(head_masks[h][None], t[:, h * block : (h + 1) * block, :], out)
        return out

    def part(ref, base, g):
        return ref[:, base + g * LANES : base + (g + 1) * LANES].reshape(blocks, block, LANES)

    allowed = jnp.concatenate([mask_ref[...]] * halves, axis=0) > 0.5
    for g in range(groups):
        q3 = part(qkv_s, 0, g)
        k3 = spread(part(qkv_s, width, g))
        v3 = spread(part(qkv_s, 2 * width, g))
        s = bmm_t(q3, k3).reshape(m_rows, LANES) * scale
        s = jnp.where(allowed, s, neg_fill)
        e = jnp.where(allowed, jnp.exp(s - window_max(s)), 0.0)
        p = e / segment_sum(e, ones)
        p_s[:, g * LANES : (g + 1) * LANES] = p
        o = bmm(p.astype(BF16).reshape(blocks, block, LANES), v3)
        o_s[:, g * LANES : (g + 1) * LANES] = o.reshape(m_rows, LANES).astype(BF16)

    x2 = x_s[...] + mm(o_s[...], wo_ref[...])
    xhat2, rstd2 = normalise(x2)
    a2 = (xhat2 * gain2 + shift2).astype(BF16)
    a2_s[...] = a2
    a2t_s[...] = a2.T
    dz = cot_ref[...].reshape(m_rows, width)
    dzt_s[...] = dz.T
    y_s[...] = x2
    da_s[...] = jnp.zeros_like(da_s)

    def ff_body(c, carry):
        at = pl.ds(pl.multiple_of(c * chunk, chunk), chunk)
        wu = wu_ref[:, at]
        wd = wd_ref[at, :]
        dzc = cot_ref[...].reshape(m_rows, width)
        u = mm(a2_s[...], wu)
        dh = mm_t(dzc, wd)
        cdf, bump = gelu_parts(u)
        h = (u * cdf).astype(BF16)
        du = ((cdf + bump) * dh).astype(BF16)
        y_s[...] += mm(h, wd)
        acc_d[:, at] += mm(dzt_s[...], h)
        acc_u[:, at] += mm(a2t_s[...], du)
        da_s[...] += mm_t(du, wu)
        return carry

    lax.fori_loop(0, ff // chunk, ff_body, 0)

    out_ref[...] = y_s[...].reshape(halves, cells, width).astype(BF16)
    da2 = da_s[...]
    gvec_ref[2:3, :] += jnp.sum(da2 * xhat2, axis=0, keepdims=True)
    gvec_ref[3:4, :] += jnp.sum(da2, axis=0, keepdims=True)
    dx2 = cot_ref[...].reshape(m_rows, width).astype(F32) + norm_back(da2, xhat2, rstd2, gain2)
    dy2 = dx2.astype(BF16)
    acc_o[...] += mm(o_s[...].T, dy2)
    do = mm_t(dy2, wo_ref[...]).astype(BF16)

    for g in range(groups):
        cols = slice(g * LANES, (g + 1) * LANES)
        q3 = part(qkv_s, 0, g)
        k3 = spread(part(qkv_s, width, g))
        v3 = spread(part(qkv_s, 2 * width, g))
        do3 = do[:, cols].reshape(blocks, block, LANES)
        p = p_s[:, cols]
        dp = bmm_t(do3, v3).reshape(m_rows, LANES)
        draw = (p * (dp - segment_sum(p * dp, ones)) * scale).astype(BF16)
        draw3 = draw.reshape(blocks, block, LANES)
        dq = bmm(draw3, k3).reshape(m_rows, LANES)
        dk = fold(bmm_l(draw3, q3)).reshape(m_rows, LANES)
        dv = fold(bmm_l(p.astype(BF16).reshape(blocks, block, LANES), do3)).reshape(m_rows, LANES)
        dqkv_s[:, g * LANES : (g + 1) * LANES] = dq.astype(BF16)
        dqkv_s[:, width + g * LANES : width + (g + 1) * LANES] = dk.astype(BF16)
        dqkv_s[:, 2 * width + g * LANES : 2 * width + (g + 1) * LANES] = dv.astype(BF16)

    xhat1, rstd1 = normalise(x_s[...])
    a1 = (xhat1 * gain1 + shift1).astype(BF16)
    dqkv = dqkv_s[...]
    acc_qkv[...] += mm(a1.T, dqkv)
    da1 = mm_t(dqkv, wqkv_ref[...])
    gvec_ref[0:1, :] += jnp.sum(da1 * xhat1, axis=0, keepdims=True)
    gvec_ref[1:2, :] += jnp.sum(da1, axis=0, keepdims=True)
    dx = dx2 + norm_back(da1, xhat1, rstd1, gain1)
    for h in range(halves):
        dx_h = dx[h * cells : (h + 1) * cells, :]
        gvec_ref[4:5, :] += jnp.sum(unseen[h] * dx_h, axis=0, keepdims=True)
        place = place_of(h).astype(F32).T.astype(BF16)
        ret_ref[h] = mm(place, dx_h.astype(BF16)).astype(BF16)

    @pl.when(step == last)
    def _():
        half = ff // 2

        def fill(first, second):
            first[:, : 3 * width] = acc_qkv[...].astype(BF16)
            first[:, 3 * width : 4 * width] = acc_o[...].astype(BF16)
            first[:, 4 * width : 4 * width + half] = acc_u[:, :half].astype(BF16)
            first[:, 4 * width + half :] = columns_of_vectors(gvec_ref[...])
            second[:, :half] = acc_u[:, half:].astype(BF16)
            second[:, half : half + ff] = acc_d[...].astype(BF16)
            second[:, half + ff :] = jnp.zeros((width, second.shape[1] - half - ff), BF16)

        by_core(core_ref, fill, keep_ref, give_ref)


def decoder_block(core, rows, idx, cot, pos, mask, pack_one, pack_two, wd):
    n_half, slots, width = rows.shape
    cells = cot.shape[1]
    ff = wd.shape[0]
    halves = 2
    m_rows = halves * cells
    half_wide = 4 * width + ff // 2 + LANES
    vm = pltpu.VMEM
    flops = 6 * n_half * cells * (4 * width + 2 * ff) * width * 2

    def whole(*shape, at=0):
        index = (0,) * (len(shape) - 1) + (at,)
        return pl.BlockSpec(shape, lambda i: index, pipeline_mode=pl.Buffered(1))

    return pl.pallas_call(
        decoder_kernel,
        grid=(n_half // halves,),
        in_specs=[
            pl.BlockSpec(memory_space=pltpu.SMEM),
            pl.BlockSpec((halves, slots, width), lambda i: (i, 0, 0)),
            pl.BlockSpec((halves, 1, slots), lambda i: (i, 0, 0)),
            pl.BlockSpec((halves, cells, width), lambda i: (i, 0, 0)),
            whole(cells, width),
            whole(cells, LANES),
            whole(width, LANES, at=(4 * width + ff // 2) // LANES),
            whole(width, 3 * width),
            whole(width, width, at=3),
            whole(width, ff),
            whole(ff, width),
        ],
        out_specs=[
            pl.BlockSpec((halves, cells, width), lambda i: (i, 0, 0)),
            pl.BlockSpec((halves, slots, width), lambda i: (i, 0, 0)),
            whole(width, half_wide),
            whole(width, half_wide),
        ],
        out_shape=[
            jax.ShapeDtypeStruct((n_half, cells, width), BF16),
            jax.ShapeDtypeStruct((n_half, slots, width), BF16),
            jax.ShapeDtypeStruct((width, half_wide), BF16),
            jax.ShapeDtypeStruct((width, half_wide), BF16),
        ],
        scratch_shapes=[
            vm((width, 3 * width), F32),
            vm((width, width), F32),
            vm((width, ff), F32),
            vm((width, ff), F32),
            vm((8, width), F32),
            vm((8, width), F32),
            vm((m_rows, width), F32),
            vm((m_rows, 3 * width), BF16),
            vm((m_rows, width), F32),
            vm((m_rows, width), BF16),
            vm((m_rows, width), BF16),
            vm((width, m_rows), BF16),
            vm((width, m_rows), BF16),
            vm((m_rows, width), F32),
            vm((m_rows, width), F32),
            vm((m_rows, 3 * width), BF16),
        ],
        compiler_params=pltpu.CompilerParams(
            dimension_semantics=("arbitrary",), vmem_limit_bytes=VMEM_BYTES
        ),
        cost_estimate=pl.CostEstimate(flops=flops, bytes_accessed=40 << 20, transcendentals=0),
        name="decoder_block",
    )(
        core, rows, idx.reshape(n_half, 1, slots), cot, pos, mask,
        pack_one, pack_one, pack_one, pack_two, wd,
    )


def enc_spread(t, head_masks):
    return jnp.concatenate([t * hm.astype(BF16)[None] for hm in head_masks], axis=1)


def enc_heads(width):
    head_dim = width // HEADS_ENC
    lane = lax.broadcasted_iota(jnp.int32, (1, LANES), 1)
    return head_dim, [(lane // head_dim == h) for h in range(LANES // head_dim)]


def enc_attend_kernel(
    x_ref, mask_ref, small_ref, wqkv_ref, wo_ref, qkv_ref, p_ref, o_ref, x2_ref, vec_ref
):
    vec_ref[...] = vectors_of(small_ref)
    clips, slots, width = x_ref.shape
    m_rows = clips * slots
    head_dim, head_masks = enc_heads(width)
    scale = head_dim ** (-0.5)
    x = x_ref[...].reshape(m_rows, width).astype(F32)
    xhat, rstd = normalise(x)
    a1 = (xhat * vec_ref[0:1, :] + vec_ref[1:2, :]).astype(BF16)
    qkv_ref[...] = mm(a1, wqkv_ref[...]).astype(BF16)
    allowed = mask_ref[...] > 0.5
    for g in range(width // LANES):
        cols = lambda part: slice(part * width + g * LANES, part * width + (g + 1) * LANES)
        q3 = qkv_ref[:, cols(0)].reshape(clips, slots, LANES)
        k3 = enc_spread(qkv_ref[:, cols(1)].reshape(clips, slots, LANES), head_masks)
        v3 = enc_spread(qkv_ref[:, cols(2)].reshape(clips, slots, LANES), head_masks)
        s = bmm_t(q3, k3) * scale
        for h in range(len(head_masks)):
            sh = jnp.where(allowed, s[:, :, h * slots : (h + 1) * slots], neg_fill)
            e = jnp.exp(sh - jnp.max(sh, axis=-1, keepdims=True))
            e = e / jnp.sum(e, axis=-1, keepdims=True)
            at = (g * len(head_masks) + h) * slots
            p_ref[:, at : at + slots] = e.reshape(m_rows, slots).astype(BF16)
        span = len(head_masks) * slots
        p3 = p_ref[:, g * span : (g + 1) * span].reshape(clips, slots, span)
        o_ref[:, cols(0)] = bmm(p3, v3).reshape(m_rows, LANES).astype(BF16)
    x2_ref[...] = x_ref[...].reshape(m_rows, width).astype(F32) + mm(o_ref[...], wo_ref[...])


def enc_feed_kernel(
    x2_ref, vec_ref, wu_ref, wd_ref, proj_ref, sent_ref, enc_ref, h_ref, gp_ref, a2_s, y_s
):
    ff = wu_ref.shape[1]
    chunk = 512
    xhat, rstd = normalise(x2_ref[...])
    a2_s[...] = (xhat * vec_ref[2:3, :] + vec_ref[3:4, :]).astype(BF16)
    y_s[...] = x2_ref[...]

    def body(c, carry):
        at = pl.ds(pl.multiple_of(c * chunk, chunk), chunk)
        u = mm(a2_s[...], wu_ref[:, at])
        cdf, bump = gelu_parts(u)
        h = (u * cdf).astype(BF16)
        h_ref[:, at] = h
        gp_ref[:, at] = (cdf + bump).astype(BF16)
        y_s[...] += mm(h, wd_ref[at, :])
        return carry

    lax.fori_loop(0, ff // chunk, body, 0)
    encoded = y_s[...].astype(BF16)
    enc_ref[...] = encoded
    sent_ref[...] = mm(encoded, proj_ref[...]).astype(BF16)


def enc_feed_back_kernel(
    core_ref, dsent_ref, enc_ref, proj_ref, h_ref, gp_ref, x2_ref, vec_ref, wu_ref, wd_ref,
    gproj_ref, keep_ref, give_ref, dx2_ref, gvec_ref,
    a2t_s, dz_s, dzt_s, da_s,
):
    ff = wu_ref.shape[1]
    chunk = 512
    gain2 = vec_ref[2:3, :]
    dsent = dsent_ref[...]
    gproj_ref[...] = mm(enc_ref[...].T, dsent).astype(BF16)
    dy = mm_t(dsent, proj_ref[...])
    dx2_ref[...] = dy
    dz = dy.astype(BF16)
    dz_s[...] = dz
    dzt_s[...] = dz.T
    xhat, rstd = normalise(x2_ref[...])
    a2t_s[...] = (xhat * gain2 + vec_ref[3:4, :]).astype(BF16).T
    da_s[...] = jnp.zeros_like(da_s)

    def body(c, carry):
        at = pl.ds(pl.multiple_of(c * chunk, chunk), chunk)
        dh = mm_t(dz_s[...], wd_ref[at, :])
        du = (gp_ref[:, at].astype(F32) * dh).astype(BF16)
        up_grad = mm(a2t_s[...], du).astype(BF16)
        down_grad = mm(dzt_s[...], h_ref[:, at]).astype(BF16)
        first = core_ref[0] == 0
        keep_ref[:, at] = jnp.where(first, up_grad, down_grad)
        give_ref[:, at] = jnp.where(first, down_grad, up_grad)
        da_s[...] += mm_t(du, wu_ref[:, at])
        return carry

    lax.fori_loop(0, ff // chunk, body, 0)
    da = da_s[...]
    xhat, rstd = normalise(x2_ref[...])
    gvec_ref[...] = jnp.zeros_like(gvec_ref)
    gvec_ref[2:3, :] = jnp.sum(da * xhat, axis=0, keepdims=True)
    gvec_ref[3:4, :] = jnp.sum(da, axis=0, keepdims=True)
    dx2_ref[...] += norm_back(da, xhat, rstd, gain2)


def enc_attend_back_kernel(
    core_ref, dx2_ref, o_ref, qkv_ref, p_ref, x_ref, vec_ref, wqkv_ref, wo_ref, gproj_ref, gvec2_ref,
    keep_ref, give_ref, dvis_ref,
    gvec_ref, do_s, dqkv_s, gqkv_s, go_s,
):
    clips, slots, width = x_ref.shape
    m_rows = clips * slots
    head_dim, head_masks = enc_heads(width)
    count = len(head_masks)
    scale = head_dim ** (-0.5)
    gain1, shift1 = vec_ref[0:1, :], vec_ref[1:2, :]
    dy2 = dx2_ref[...].astype(BF16)
    go_s[...] = mm(o_ref[...].T, dy2).astype(BF16)
    do_s[...] = mm_t(dy2, wo_ref[...]).astype(BF16)

    def fold(t):
        out = t[:, 0:slots, :]
        for h in range(1, count):
            out = jnp.where(head_masks[h][None], t[:, h * slots : (h + 1) * slots, :], out)
        return out.reshape(m_rows, LANES).astype(BF16)

    for g in range(width // LANES):
        cols = lambda part: slice(part * width + g * LANES, part * width + (g + 1) * LANES)
        q3 = qkv_ref[:, cols(0)].reshape(clips, slots, LANES)
        k3 = enc_spread(qkv_ref[:, cols(1)].reshape(clips, slots, LANES), head_masks)
        v3 = enc_spread(qkv_ref[:, cols(2)].reshape(clips, slots, LANES), head_masks)
        do3 = do_s[:, cols(0)].reshape(clips, slots, LANES)
        span = count * slots
        p3 = p_ref[:, g * span : (g + 1) * span].reshape(clips, slots, span)
        dp = bmm_t(do3, v3)
        parts = []
        for h in range(count):
            hs = slice(h * slots, (h + 1) * slots)
            ph = p3[:, :, hs].astype(F32)
            dph = dp[:, :, hs]
            mean = jnp.sum(ph * dph, axis=-1, keepdims=True)
            parts.append((ph * (dph - mean) * scale).astype(BF16))
        draw3 = jnp.concatenate(parts, axis=2)
        dqkv_s[:, cols(0)] = bmm(draw3, k3).reshape(m_rows, LANES).astype(BF16)
        dqkv_s[:, cols(1)] = fold(bmm_l(draw3, q3))
        dqkv_s[:, cols(2)] = fold(bmm_l(p3, do3))

    x = x_ref[...].reshape(m_rows, width).astype(F32)
    xhat, rstd = normalise(x)
    a1t = (xhat * gain1 + shift1).astype(BF16).T
    gqkv_s[...] = mm(a1t, dqkv_s[...]).astype(BF16)
    da = mm_t(dqkv_s[...], wqkv_ref[...])
    gvec_ref[...] = gvec2_ref[...]
    gvec_ref[0:1, :] = jnp.sum(da * xhat, axis=0, keepdims=True)
    gvec_ref[1:2, :] = jnp.sum(da, axis=0, keepdims=True)
    dx = dx2_ref[...] + norm_back(da, xhat, rstd, gain1)
    dvis_ref[...] = dx.reshape(clips, slots, width).astype(BF16)
    half = keep_ref.shape[1]
    tail = 3 * width - half
    sent = gproj_ref.shape[1]

    def fill(first, second):
        first[...] = gqkv_s[:, :half]
        second[:, :tail] = gqkv_s[:, half:]
        second[:, tail : tail + width] = go_s[...]
        second[:, tail + width : tail + width + sent] = gproj_ref[...]
        end = tail + width + sent
        second[:, end : end + LANES] = columns_of_vectors(gvec_ref[...])
        second[:, end + LANES :] = jnp.zeros((width, half - end - LANES), BF16)

    by_core(core_ref, fill, keep_ref, give_ref)


def whole_call(kernel, args, outs, scratch, name, flops):
    arrays, specs = [], []
    for arg in args:
        array, shape, at = arg if isinstance(arg, tuple) else (arg, arg.shape, 0)
        if len(shape) == 1:
            arrays.append(array)
            specs.append(pl.BlockSpec(memory_space=pltpu.SMEM))
            continue
        index = (0,) * (len(shape) - 1) + (at,)
        arrays.append(array)
        specs.append(pl.BlockSpec(shape, lambda i, index=index: index, pipeline_mode=pl.Buffered(1)))
    zero = lambda shape: pl.BlockSpec(shape, lambda i: (0,) * len(shape), pipeline_mode=pl.Buffered(1))
    return pl.pallas_call(
        kernel,
        grid=(1,),
        in_specs=specs,
        out_specs=[zero(s) for s, _ in outs],
        out_shape=[jax.ShapeDtypeStruct(s, d) for s, d in outs],
        scratch_shapes=[pltpu.VMEM(s, d) for s, d in scratch],
        compiler_params=pltpu.CompilerParams(vmem_limit_bytes=VMEM_BYTES),
        cost_estimate=pl.CostEstimate(flops=flops, bytes_accessed=16 << 20, transcendentals=0),
        name=name,
    )(*arrays)


def enc_blocks(pack, width, ff, sent):
    return (
        (pack, (width, 3 * width), 0),
        (pack, (width, width), 3),
        (pack, (width, ff), 4 * width // ff),
        (pack, (width, sent), (4 * width + ff) // sent),
        (pack, (width, LANES), (4 * width + ff + sent) // LANES),
    )


def enc_attend(x, mask, blocks):
    clips, slots, width = x.shape
    m = clips * slots
    outs = [
        ((m, 3 * width), BF16),
        ((m, HEADS_ENC * slots), BF16),
        ((m, width), BF16),
        ((m, width), F32),
        ((8, width), F32),
    ]
    qkv, out, _, _, small = blocks
    return whole_call(enc_attend_kernel, (x, mask, small, qkv, out), outs, [], "enc_attend", 10**10)


def enc_feed(x2, vecs, blocks, wd):
    m, width = x2.shape
    ff = wd.shape[0]
    _, _, up, proj, _ = blocks
    outs = [((m, proj[1][1]), BF16), ((m, width), BF16), ((m, ff), BF16), ((m, ff), BF16)]
    scratch = [((m, width), BF16), ((m, width), F32)]
    return whole_call(enc_feed_kernel, (x2, vecs, up, wd, proj), outs, scratch, "enc_feed", 18 * 10**9)


def enc_feed_back(core, dsent, enc, h, gp, x2, vecs, blocks, wd):
    m, width = x2.shape
    ff = wd.shape[0]
    _, _, up, proj, _ = blocks
    half = (width, ff)
    outs = [(proj[1], BF16), (half, BF16), (half, BF16), ((m, width), F32), ((8, width), F32)]
    scratch = [((width, m), BF16), ((m, width), BF16), ((width, m), BF16), ((m, width), F32)]
    args = (core, dsent, enc, proj, h, gp, x2, vecs, up, wd)
    return whole_call(enc_feed_back_kernel, args, outs, scratch, "enc_feed_back", 24 * 10**9)


def attend_half(width, sent):
    blocks = (4 * width + sent + LANES) // LANES
    return (blocks + 1) // 2 * LANES


def enc_attend_back(core, dx2, o, qkv, p, x, vecs, blocks, gproj, gvec):
    m, width = dx2.shape
    w_qkv, w_out, _, _, _ = blocks
    half = (width, attend_half(width, gproj.shape[1]))
    outs = [(half, BF16), (half, BF16), (x.shape, BF16)]
    scratch = [
        ((8, width), F32),
        ((m, width), BF16),
        ((m, 3 * width), BF16),
        ((width, 3 * width), BF16),
        ((width, width), BF16),
    ]
    args = (core, dx2, o, qkv, p, x, vecs, w_qkv, w_out, gproj, gvec)
    return whole_call(enc_attend_back_kernel, args, outs, scratch, "enc_attend_back", 14 * 10**9)


def unpack_kernel(pieces, tall, small, packed_ref, *out_refs):
    chips, _, rows, _ = packed_ref.shape

    def read(part, start, size):
        return packed_ref[:, part, :, start : start + size].reshape(chips * rows, size).astype(F32)

    for out, to, part, start, size in pieces:
        out_refs[out][:, to : to + size] = read(part, start, size)
    part, start, size = tall
    chunk = 512
    for c in range(size // chunk):
        out_refs[-2][c * chunk : (c + 1) * chunk, :] = read(part, start + c * chunk, chunk).T
    out_refs[-1][...] = read(*small, LANES).T[0:8, :]


def unpack_sums(packed, widths, pieces, tall, small):
    chips, _, rows, wide = packed.shape
    height = chips * rows
    if rows % 16:
        packed = packed.transpose(1, 0, 2, 3).reshape(2, 16, height // 16, wide).transpose(1, 0, 2, 3)
        chips, _, rows, wide = packed.shape
    group = LANES // math.gcd(rows, LANES)
    step = group * rows
    size = tall[2]
    side = lambda n: pl.BlockSpec((step, n), lambda i: (i, 0))
    down = lambda n: pl.BlockSpec((n, step), lambda i: (0, i))
    return pl.pallas_call(
        functools.partial(unpack_kernel, pieces, tall, small),
        grid=(chips // group,),
        in_specs=[pl.BlockSpec((group, 2, rows, wide), lambda i: (i, 0, 0, 0))],
        out_specs=[side(n) for n in widths] + [down(size), down(8)],
        out_shape=[jax.ShapeDtypeStruct((height, n), F32) for n in widths]
        + [jax.ShapeDtypeStruct((size, height), F32), jax.ShapeDtypeStruct((8, height), F32)],
        compiler_params=pltpu.CompilerParams(vmem_limit_bytes=VMEM_BYTES),
        cost_estimate=pl.CostEstimate(flops=0, bytes_accessed=6 * height * wide, transcendentals=0),
        name="unpack_sums",
    )(packed)


AXES = ("clip", "band")


def partner_pairs(total, mask):
    return [(i, i ^ mask) for i in range(total)]


def add_low(*parts):
    return sum(part.astype(F32) for part in parts).astype(BF16)


class RunningSum:
    def __init__(self, keep, give, total):
        bits = total.bit_length() - 1
        self.total = total
        self.cut = keep.shape[1] // 256 * 128
        got = lax.ppermute(give, AXES, partner_pairs(total, 1))
        rows = keep.shape[0] // (total // 2)
        self.held = [add_low(keep, got).reshape((2,) * (bits - 1) + (rows, keep.shape[1]))]
        self.left = [list(range(bits - 1, 0, -1))]
        self.plan = [[[2], [1]], [[1], [2]]]
        rest = list(range(3, bits))
        while rest:
            self.plan.append([rest[:2]])
            rest = rest[2:]

    def offers(self):
        me = lax.axis_index(AXES)
        groups = self.plan[0]
        if len(groups) > len(self.held):
            (held,), (left,) = self.held, self.left
            self.held = [held[..., : self.cut], held[..., self.cut :]]
            self.left = [list(left), list(left)]
        if len(groups) < len(self.held):
            self.held = [jnp.concatenate(self.held, axis=-1)]
            self.left = self.left[:1]
        self.keep, gives, self.masks = [], [], []
        for held, left, group in zip(self.held, self.left, groups):
            low, ways = group[0], 1 << len(group)
            place = left.index(group[-1])
            mine = (me >> low) & (ways - 1)
            shape = held.shape
            held = held.reshape(shape[:place] + (ways,) + shape[place + len(group) :])
            self.keep.append(lax.dynamic_index_in_dim(held, mine, place, keepdims=False))
            for k in range(1, ways):
                gives.append(lax.dynamic_index_in_dim(held, mine ^ k, place, keepdims=False))
                self.masks.append(k << low)
            for bit in group:
                left.remove(bit)
        return gives

    def deliver(self, gives):
        got = [
            lax.ppermute(give, AXES, partner_pairs(self.total, mask))
            for give, mask in zip(gives, self.masks)
        ]
        each = len(got) // len(self.keep)
        self.held = [
            add_low(keep, *got[i * each : (i + 1) * each]) for i, keep in enumerate(self.keep)
        ]
        self.plan = self.plan[1:]

    def finish(self):
        while self.plan:
            self.deliver(self.offers())
        return jnp.concatenate(self.held, axis=-1)


class RunningGather:
    def __init__(self, shard, total, cut, axis):
        bits = total.bit_length() - 1
        self.total, self.cut, self.axis = total, cut, axis
        self.shape = shard.shape
        rest, self.plan = list(range(3, bits)), []
        while rest:
            self.plan.append([rest[:2]])
            rest = rest[2:]
        self.plan += [[[1], [2]], [[2], [1]], [[0], [0]]]
        self.held, self.have = [shard], [[]]

    def offers(self):
        groups = self.plan[0]
        if len(groups) > len(self.held):
            held, at = self.held[0], self.held[0].ndim - 2 + self.axis
            first = lax.slice_in_dim(held, 0, self.cut, axis=at)
            self.held = [first, lax.slice_in_dim(held, self.cut, held.shape[at], axis=at)]
            self.have = [list(self.have[0]), list(self.have[0])]
        gives, self.masks = [], []
        for held, group in zip(self.held, groups):
            for k in range(1, 1 << len(group)):
                gives.append(held)
                self.masks.append(k << group[0])
        return gives

    def deliver(self, gives):
        me = lax.axis_index(AXES)
        got = [
            lax.ppermute(give, AXES, partner_pairs(self.total, mask))
            for give, mask in zip(gives, self.masks)
        ]
        each = len(got) // len(self.held)
        for i, group in enumerate(self.plan[0]):
            parts = [self.held[i]] + got[i * each : (i + 1) * each]
            for b, bit in enumerate(group):
                flip = ((me >> bit) & 1) == 1
                parts = [jnp.where(flip, parts[k ^ (1 << b)], part) for k, part in enumerate(parts)]
            self.have[i] = sorted(self.have[i] + group, reverse=True)
            at = self.have[i].index(group[-1])
            held = jnp.stack(parts, axis=at)
            self.held[i] = held.reshape(held.shape[:at] + (2,) * len(group) + held.shape[at + 1 :])
        self.plan = self.plan[1:]

    def result(self):
        return [held.reshape((self.total,) + held.shape[-2:]) for held in self.held]


def together(*groups):
    return lax.optimization_barrier(groups)


def gather_rows(shard):
    return lax.all_gather(shard, AXES, axis=0, tiled=True)


def columns_of(vectors):
    block = jnp.stack(vectors, axis=1)
    return jnp.pad(block, ((0, 0), (0, LANES - len(vectors))))


def blocks_beside(tall, rows):
    return [tall[i : i + rows] for i in range(0, tall.shape[0], rows)]


def blocks_below(beside, total, width):
    rows = beside.shape[0] // total
    count = beside.shape[1] // width
    parts = [beside[:, i * width : (i + 1) * width].reshape(total, rows, width) for i in range(count)]
    return jnp.concatenate(parts, axis=1)


def swap_band(array, bit):
    return lax.ppermute(array, "band", [(i, i ^ bit) for i in range(4)])


def owners_to_bands(array):
    band = lax.axis_index("band")
    half, side = band // 2, band % 2
    own = lax.dynamic_index_in_dim(array, half, 0, keepdims=False)
    got = swap_band(lax.dynamic_index_in_dim(array, 1 - half, 0, keepdims=False), 2)
    pair = jnp.stack([jnp.where(half == 0, own, got), jnp.where(half == 0, got, own)])
    other = swap_band(pair, 1)
    return jnp.stack([jnp.where(side == 0, pair, other), jnp.where(side == 0, other, pair)], axis=1)


def bands_to_owners(array):
    band = lax.axis_index("band")
    half, side = band // 2, band % 2
    own = lax.dynamic_index_in_dim(array, side, 1, keepdims=False)
    got = swap_band(lax.dynamic_index_in_dim(array, 1 - side, 1, keepdims=False), 1)
    pair = own + got
    own = lax.dynamic_index_in_dim(pair, half, 0, keepdims=False)
    got = swap_band(lax.dynamic_index_in_dim(pair, 1 - half, 0, keepdims=False), 2)
    return jnp.stack([jnp.where(half == 0, own, got), jnp.where(half == 0, got, own)])


def position_table(places):
    half_width = D_DEC // 2
    omega_vec = jnp.exp(
        jnp.arange(half_width, dtype=F32) * (-math.log(10000.0) / half_width)
    )
    angles = places.astype(F32)[..., None] * omega_vec
    return jnp.concatenate([jnp.sin(angles), jnp.cos(angles)], axis=-1)


def shards(
    visible,
    keep_index,
    visible_count,
    enc_gain1,
    enc_shift1,
    enc_qkv,
    enc_out,
    enc_gain2,
    enc_shift2,
    enc_up,
    enc_down,
    proj,
    mask_token,
    dec_gain1,
    dec_shift1,
    dec_qkv,
    dec_out,
    dec_gain2,
    dec_shift2,
    dec_up,
    dec_down,
    cotangent,
):
    total = lax.axis_size(AXES)
    enc_wide, dec_wide = enc_out.shape[1], dec_out.shape[1]
    enc_ff, dec_ff = enc_up.shape[1], dec_up.shape[1]
    core = (lax.axis_index(AXES) % 2).reshape(1)
    enc_small = columns_of([enc_gain1, enc_shift1, enc_gain2, enc_shift2])
    enc_pack = gather_rows(jnp.concatenate([enc_qkv, enc_out, enc_up, proj, enc_small], axis=1))
    dec_small = columns_of([dec_gain1, dec_shift1, dec_gain2, dec_shift2, mask_token])
    dec_tall = blocks_beside(dec_down, dec_out.shape[0])
    near, far = dec_tall[: len(dec_tall) // 2], dec_tall[len(dec_tall) // 2 :]
    dec_first = jnp.concatenate([dec_qkv, dec_out] + near + [dec_small], axis=1)
    dec_pack = jnp.concatenate([dec_first, dec_up] + far, axis=1)
    down_run = RunningGather(enc_down, total, enc_down.shape[0] // 2, 0)
    dec_run = RunningGather(dec_pack, total, dec_first.shape[1], 1)
    while len(down_run.plan) > 3:
        down_run.deliver(down_run.offers())
    gives, dec_gives = together(down_run.offers(), dec_run.offers())
    down_run.deliver(gives)
    dec_run.deliver(dec_gives)
    while len(dec_run.plan) > 3:
        dec_run.deliver(dec_run.offers())
    down_run.deliver(down_run.offers())
    gives, dec_gives = together(down_run.offers(), dec_run.offers())
    down_run.deliver(gives)
    dec_run.deliver(dec_gives)
    whole_down = jnp.concatenate(down_run.result(), axis=1).reshape(-1, enc_wide)
    enc_pack, whole_down, gives = together(enc_pack, whole_down, dec_run.offers())
    dec_run.deliver(gives)

    clip_count, slot_total, _ = visible.shape
    half_clips = clip_count // 2
    band_height = FREQ // 2
    slot_ids = jnp.arange(slot_total)
    valid_rows = slot_ids[None, :] < visible_count[:, None]
    valid_mask = valid_rows.astype(F32)[:, None, :]
    cell_number = jnp.where(valid_rows, keep_index, -1).reshape(2, half_clips, slot_total)
    cell_number = owners_to_bands(cell_number).reshape(-1, slot_total)
    band_pick = lax.axis_index("band") % 2
    rolled_time = (cell_number // FREQ + TIME - SHIFT) % TIME
    rolled_freq = (cell_number % FREQ + FREQ - SHIFT) % FREQ
    here = (cell_number >= 0) & (rolled_freq // band_height == band_pick)
    arrived_index = jnp.where(here, rolled_time * band_height + rolled_freq % band_height, -1)

    blocks = enc_blocks(enc_pack, enc_wide, enc_ff, dec_wide)
    qkv, probs, mixed, middle, vecs = enc_attend(visible, valid_mask, blocks)
    sent_rows, encoded, hidden, slope = enc_feed(middle, vecs, blocks, whole_down)
    sent_rows, gives = together(sent_rows, dec_run.offers())
    dec_run.deliver(gives)
    pack_one, pack_two = [part.reshape(-1, part.shape[2]) for part in dec_run.result()]
    tall_one = blocks_below(pack_one[:, 4 * dec_wide : 4 * dec_wide + dec_ff // 2], total, dec_wide)
    tall_two = blocks_below(pack_two[:, dec_ff:], total, dec_wide)
    dec_whole_down = jnp.concatenate([tall_one, tall_two], axis=1).reshape(-1, dec_wide)
    arrived_rows = owners_to_bands(sent_rows.reshape(2, half_clips, slot_total, dec_wide))
    half_total = 4 * half_clips

    cell_count = TIME * band_height
    places = jnp.arange(cell_count)
    cell_freq = band_pick * band_height + places % band_height
    patch_number = (places // band_height + SHIFT) % TIME * FREQ + (cell_freq + SHIFT) % FREQ
    span = D_DEC // HEADS_DEC
    query = places[:, None]
    key = query // span * span + jnp.arange(LANES)[None, :] % span

    def label(cell):
        late = cell // band_height >= TIME - SHIFT
        high = band_pick * band_height + cell % band_height >= FREQ - SHIFT
        return late.astype(jnp.int32) * 2 + high.astype(jnp.int32)

    cells_in = WINDOW * WINDOW
    allowed = (query // cells_in == key // cells_in) & (label(query) == label(key))
    decoded, returning, keep, give = decoder_block(
        core,
        arrived_rows.reshape(half_total, slot_total, dec_wide),
        arrived_index,
        cotangent.reshape(half_total, cell_count, dec_wide),
        position_table(patch_number),
        allowed.astype(F32),
        pack_one,
        pack_two,
        dec_whole_down,
    )
    decoded_out = decoded.reshape(cotangent.shape)

    dec_run = RunningSum(keep, give, total)
    grad_sent = bands_to_owners(returning.reshape(2, 2, half_clips, slot_total, dec_wide))
    grad_sent = grad_sent.reshape(-1, dec_wide)
    grad_sent, gives = together(grad_sent, dec_run.offers())
    dec_run.deliver(gives)
    g_proj, keep, give, grad_middle, g_vec = enc_feed_back(
        core, grad_sent, encoded, hidden, slope, middle, vecs, blocks, whole_down
    )
    keep, give, grad_middle, gives = together(keep, give, grad_middle, dec_run.offers())
    dec_run.deliver(gives)
    feed_run = RunningSum(keep, give, total)
    keep, give, grad_visible = enc_attend_back(
        core, grad_middle, mixed, qkv, probs, visible, vecs, blocks, g_proj, g_vec
    )
    keep, give, gives, feed_gives = together(keep, give, dec_run.offers(), feed_run.offers())
    dec_run.deliver(gives)
    feed_run.deliver(feed_gives)
    attend_run = RunningSum(keep, give, total)
    dec_shard = dec_run.finish()
    dec_shard, feed_gives, gives = together(dec_shard, feed_run.offers(), attend_run.offers())
    dec_sum = gather_rows(dec_shard)
    feed_run.deliver(feed_gives)
    feed_gives, gives = together(feed_run.offers(), gives)
    feed_run.deliver(feed_gives)
    attend_run.deliver(gives)
    attend_run.deliver(attend_run.offers())
    feed_sum = feed_run.finish()
    attend_sum = attend_run.finish()
    enc_sum = gather_rows(jnp.concatenate([attend_sum, feed_sum], axis=1))

    by_chip = lambda packed, shard: packed.reshape(total // 2, 2, shard.shape[0], packed.shape[1])
    half = dec_ff // 2
    d_qkv, d_out, d_up, d_down, dec_vecs = unpack_sums(
        by_chip(dec_sum, dec_shard),
        (3 * dec_wide, dec_wide, dec_ff),
        (
            (0, 0, 0, 0, 3 * dec_wide),
            (1, 0, 0, 3 * dec_wide, dec_wide),
            (2, 0, 0, 4 * dec_wide, half),
            (2, half, 1, 0, half),
        ),
        (1, half, dec_ff),
        (0, 4 * dec_wide + half),
    )
    half = attend_sum.shape[1]
    tail = 3 * enc_wide - half
    e_qkv, e_out, e_proj, e_up, e_down, enc_vecs = unpack_sums(
        by_chip(enc_sum, attend_sum),
        (3 * enc_wide, enc_wide, dec_wide, enc_ff),
        (
            (0, 0, 0, 0, half),
            (0, half, 1, 0, tail),
            (1, 0, 1, tail, enc_wide),
            (2, 0, 1, tail + enc_wide, dec_wide),
            (3, 0, 0, half, enc_ff),
        ),
        (1, half, enc_ff),
        (1, tail + enc_wide + dec_wide),
    )
    return (
        decoded_out,
        grad_visible,
        enc_vecs[0],
        enc_vecs[1],
        e_qkv,
        e_out,
        enc_vecs[2],
        enc_vecs[3],
        e_up,
        e_down,
        e_proj,
        dec_vecs[4],
        dec_vecs[0],
        dec_vecs[1],
        d_qkv,
        d_out,
        dec_vecs[2],
        dec_vecs[3],
        d_up,
        d_down,
    )


def solution(mesh):
    return jax.shard_map(
        shards,
        mesh=mesh,
        in_specs=(
            P(("clip", "band"), None, None),
            P(("clip", "band"), None),
            P(("clip", "band")),
            P(("clip", "band")),
            P(("clip", "band")),
            P(("clip", "band"), None),
            P(("clip", "band"), None),
            P(("clip", "band")),
            P(("clip", "band")),
            P(("clip", "band"), None),
            P(("clip", "band"), None),
            P(("clip", "band"), None),
            P(("clip", "band")),
            P(("clip", "band")),
            P(("clip", "band")),
            P(("clip", "band"), None),
            P(("clip", "band"), None),
            P(("clip", "band")),
            P(("clip", "band")),
            P(("clip", "band"), None),
            P(("clip", "band"), None),
            P(("clip", "band"), None, None, None, None),
        ),
        out_specs=(
            P(("clip", "band"), None, None, None, None),
            P(("clip", "band"), None, None),
            P(),
            P(),
            P(),
            P(),
            P(),
            P(),
            P(),
            P(),
            P(),
            P(),
            P(),
            P(),
            P(),
            P(),
            P(),
            P(),
            P(),
            P(),
        ),
        check_vma=False,
    )
```

```python
import functools
import math

import jax
import jax.numpy as jnp
from jax import lax
from jax.experimental import pallas as pl
from jax.experimental.pallas import tpu as pltpu
from jax.sharding import PartitionSpec as P

HEADS_ENC = 12
D_DEC = 512
HEADS_DEC = 16
TIME = 64
FREQ = 8
WINDOW = 4
SHIFT = 2
norm_eps = 1e-06
neg_fill = -1e30
F32 = jnp.float32
BF16 = jnp.bfloat16
LANES = 128
VMEM_BYTES = 58 * 1024 * 1024


def mm(a, b):
    return lax.dot_general(a, b, (((1,), (0,)), ((), ())), preferred_element_type=F32)


def mm_t(a, b):
    return lax.dot_general(a, b, (((1,), (1,)), ((), ())), preferred_element_type=F32)


def bmm(a, b):
    return lax.dot_general(a, b, (((2,), (1,)), ((0,), (0,))), preferred_element_type=F32)


def bmm_t(a, b):
    return lax.dot_general(a, b, (((2,), (2,)), ((0,), (0,))), preferred_element_type=F32)


def bmm_l(a, b):
    return lax.dot_general(a, b, (((1,), (1,)), ((0,), (0,))), preferred_element_type=F32)


def normalise(x):
    centre = jnp.mean(x, axis=-1, keepdims=True)
    centred = x - centre
    rstd = lax.rsqrt(jnp.mean(centred * centred, axis=-1, keepdims=True) + norm_eps)
    return centred * rstd, rstd


def norm_back(da, xhat, rstd, gain):
    dag = da * gain
    return rstd * (
        dag
        - jnp.mean(dag, axis=-1, keepdims=True)
        - xhat * jnp.mean(dag * xhat, axis=-1, keepdims=True)
    )


def gelu_parts(u):
    size = jnp.abs(u) * 0.7071067811865476
    bell = jnp.exp(-0.5 * u * u)
    t = 1.0 / (1.0 + 0.3275911 * size)
    poly = 0.530702715
    poly = poly * t - 0.726576013
    poly = poly * t + 0.710706871
    poly = poly * t - 0.142248368
    poly = poly * t + 0.127414796
    tail = poly * t * bell
    cdf = jnp.where(u >= 0, 1.0 - tail, tail)
    return cdf, u * bell * 0.3989422804014327


def vectors_of(small_ref):
    return small_ref[...].astype(F32).T[0:8, :]


def columns_of_vectors(vectors):
    count, width = vectors.shape
    block = jnp.concatenate([vectors, jnp.zeros((LANES - count, width), F32)], axis=0)
    return block.T.astype(BF16)


def by_core(core_ref, fill, keep_ref, give_ref):
    @pl.when(core_ref[0] == 0)
    def _():
        fill(keep_ref, give_ref)

    @pl.when(core_ref[0] != 0)
    def _():
        fill(give_ref, keep_ref)


def segment_sum(x, ones):
    return mm(x.astype(BF16), ones)


def window_max(s):
    ahead = s
    behind = s
    for step in (1, 2, 4, 8):
        ahead = jnp.maximum(ahead, pltpu.roll(ahead, step, 1))
        behind = jnp.maximum(behind, pltpu.roll(behind, LANES - step, 1))
    return jnp.maximum(ahead, behind)


def decoder_kernel(
    core_ref, rows_ref, idx_ref, cot_ref, pos_ref, mask_ref, small_ref, wqkv_ref, wo_ref, wu_ref, wd_ref,
    out_ref, ret_ref, keep_ref, give_ref,
    acc_qkv, acc_o, acc_u, acc_d, gvec_ref, vec_ref,
    x_s, qkv_s, p_s, o_s, a2_s, a2t_s, dzt_s, da_s, y_s, dqkv_s,
):
    step = pl.program_id(0)
    last = pl.num_programs(0) - 1
    halves, cells, width = cot_ref.shape
    m_rows = halves * cells
    slots = rows_ref.shape[1]
    head_dim = width // HEADS_DEC
    heads_in = LANES // head_dim
    groups = width // LANES
    block = LANES // heads_in
    blocks = m_rows // block
    scale = head_dim ** (-0.5)
    ff = wu_ref.shape[1]
    chunk = 512

    @pl.when(step == 0)
    def _():
        acc_qkv[...] = jnp.zeros_like(acc_qkv)
        acc_o[...] = jnp.zeros_like(acc_o)
        acc_u[...] = jnp.zeros_like(acc_u)
        acc_d[...] = jnp.zeros_like(acc_d)
        gvec_ref[...] = jnp.zeros_like(gvec_ref)
        vec_ref[...] = vectors_of(small_ref)

    gain1, shift1 = vec_ref[0:1, :], vec_ref[1:2, :]
    gain2, shift2 = vec_ref[2:3, :], vec_ref[3:4, :]
    token = vec_ref[4:5, :]

    def place_of(h):
        cell = lax.broadcasted_iota(jnp.int32, (cells, slots), 0)
        return cell == idx_ref[h]

    unseen = []
    for h in range(halves):
        place = place_of(h)
        unseen_h = 1.0 - jnp.sum(place.astype(F32), axis=1, keepdims=True)
        unseen.append(unseen_h)
        x_s[h * cells : (h + 1) * cells, :] = (
            mm(place.astype(BF16), rows_ref[h]) + unseen_h * token + pos_ref[...]
        )
    xhat1, rstd1 = normalise(x_s[...])
    a1 = (xhat1 * gain1 + shift1).astype(BF16)
    qkv_s[...] = mm(a1, wqkv_ref[...]).astype(BF16)

    lane = lax.broadcasted_iota(jnp.int32, (1, LANES), 1)
    head_masks = [(lane // head_dim == h) for h in range(heads_in)]
    ones = (
        lax.broadcasted_iota(jnp.int32, (LANES, LANES), 0) // block
        == lax.broadcasted_iota(jnp.int32, (LANES, LANES), 1) // block
    ).astype(BF16)

    def spread(t):
        parts = [t * hm.astype(BF16)[None] for hm in head_masks]
        return jnp.concatenate(parts, axis=1)

    def fold(t):
        out = t[:, 0:block, :]
        for h in range(1, heads_in):
            out = jnp.where(head_masks[h][None], t[:, h * block : (h + 1) * block, :], out)
        return out

    def part(ref, base, g):
        return ref[:, base + g * LANES : base + (g + 1) * LANES].reshape(blocks, block, LANES)

    allowed = jnp.concatenate([mask_ref[...]] * halves, axis=0) > 0.5
    for g in range(groups):
        q3 = part(qkv_s, 0, g)
        k3 = spread(part(qkv_s, width, g))
        v3 = spread(part(qkv_s, 2 * width, g))
        s = bmm_t(q3, k3).reshape(m_rows, LANES) * scale
        s = jnp.where(allowed, s, neg_fill)
        e = jnp.where(allowed, jnp.exp(s - window_max(s)), 0.0)
        p = e / segment_sum(e, ones)
        p_s[:, g * LANES : (g + 1) * LANES] = p
        o = bmm(p.astype(BF16).reshape(blocks, block, LANES), v3)
        o_s[:, g * LANES : (g + 1) * LANES] = o.reshape(m_rows, LANES).astype(BF16)

    x2 = x_s[...] + mm(o_s[...], wo_ref[...])
    xhat2, rstd2 = normalise(x2)
    a2 = (xhat2 * gain2 + shift2).astype(BF16)
    a2_s[...] = a2
    a2t_s[...] = a2.T
    dz = cot_ref[...].reshape(m_rows, width)
    dzt_s[...] = dz.T
    y_s[...] = x2
    da_s[...] = jnp.zeros_like(da_s)

    for c in range(ff // chunk):
        at = slice(c * chunk, (c + 1) * chunk)
        u = mm(a2_s[...], wu_ref[:, at])
        dh = mm_t(cot_ref[...].reshape(m_rows, width), wd_ref[at, :])
        cdf, bump = gelu_parts(u)
        h = (u * cdf).astype(BF16)
        du = ((cdf + bump) * dh).astype(BF16)
        y_s[...] += mm(h, wd_ref[at, :])
        acc_d[:, at] += mm(dzt_s[...], h)
        acc_u[:, at] += mm(a2t_s[...], du)
        da_s[...] += mm_t(du, wu_ref[:, at])

    out_ref[...] = y_s[...].reshape(halves, cells, width).astype(BF16)
    da2 = da_s[...]
    gvec_ref[2:3, :] += jnp.sum(da2 * xhat2, axis=0, keepdims=True)
    gvec_ref[3:4, :] += jnp.sum(da2, axis=0, keepdims=True)
    dx2 = cot_ref[...].reshape(m_rows, width).astype(F32) + norm_back(da2, xhat2, rstd2, gain2)
    dy2 = dx2.astype(BF16)
    acc_o[...] += mm(o_s[...].T, dy2)
    do = mm_t(dy2, wo_ref[...]).astype(BF16)

    for g in range(groups):
        cols = slice(g * LANES, (g + 1) * LANES)
        q3 = part(qkv_s, 0, g)
        k3 = spread(part(qkv_s, width, g))
        v3 = spread(part(qkv_s, 2 * width, g))
        do3 = do[:, cols].reshape(blocks, block, LANES)
        p = p_s[:, cols]
        dp = bmm_t(do3, v3).reshape(m_rows, LANES)
        draw = (p * (dp - segment_sum(p * dp, ones)) * scale).astype(BF16)
        draw3 = draw.reshape(blocks, block, LANES)
        dq = bmm(draw3, k3).reshape(m_rows, LANES)
        dk = fold(bmm_l(draw3, q3)).reshape(m_rows, LANES)
        dv = fold(bmm_l(p.astype(BF16).reshape(blocks, block, LANES), do3)).reshape(m_rows, LANES)
        dqkv_s[:, g * LANES : (g + 1) * LANES] = dq.astype(BF16)
        dqkv_s[:, width + g * LANES : width + (g + 1) * LANES] = dk.astype(BF16)
        dqkv_s[:, 2 * width + g * LANES : 2 * width + (g + 1) * LANES] = dv.astype(BF16)

    xhat1, rstd1 = normalise(x_s[...])
    a1 = (xhat1 * gain1 + shift1).astype(BF16)
    dqkv = dqkv_s[...]
    acc_qkv[...] += mm(a1.T, dqkv)
    da1 = mm_t(dqkv, wqkv_ref[...])
    gvec_ref[0:1, :] += jnp.sum(da1 * xhat1, axis=0, keepdims=True)
    gvec_ref[1:2, :] += jnp.sum(da1, axis=0, keepdims=True)
    dx = dx2 + norm_back(da1, xhat1, rstd1, gain1)
    for h in range(halves):
        dx_h = dx[h * cells : (h + 1) * cells, :]
        gvec_ref[4:5, :] += jnp.sum(unseen[h] * dx_h, axis=0, keepdims=True)
        place = place_of(h).astype(F32).T.astype(BF16)
        ret_ref[h] = mm(place, dx_h.astype(BF16)).astype(BF16)

    @pl.when(step == last)
    def _():
        half = ff // 2

        def fill(first, second):
            first[:, : 3 * width] = acc_qkv[...].astype(BF16)
            first[:, 3 * width : 4 * width] = acc_o[...].astype(BF16)
            first[:, 4 * width : 4 * width + half] = acc_u[:, :half].astype(BF16)
            first[:, 4 * width + half :] = columns_of_vectors(gvec_ref[...])
            second[:, :half] = acc_u[:, half:].astype(BF16)
            second[:, half : half + ff] = acc_d[...].astype(BF16)
            second[:, half + ff :] = jnp.zeros((width, second.shape[1] - half - ff), BF16)

        by_core(core_ref, fill, keep_ref, give_ref)


def decoder_block(core, rows, idx, cot, pos, mask, pack, wd):
    n_half, slots, width = rows.shape
    cells = cot.shape[1]
    ff = wd.shape[0]
    halves = 2
    m_rows = halves * cells
    half_wide = 4 * width + ff // 2 + LANES
    vm = pltpu.VMEM
    flops = 6 * n_half * cells * (4 * width + 2 * ff) * width * 2

    def whole(*shape, at=0):
        index = (0,) * (len(shape) - 1) + (at,)
        return pl.BlockSpec(shape, lambda i: index, pipeline_mode=pl.Buffered(1))

    return pl.pallas_call(
        decoder_kernel,
        grid=(n_half // halves,),
        in_specs=[
            pl.BlockSpec(memory_space=pltpu.SMEM),
            pl.BlockSpec((halves, slots, width), lambda i: (i, 0, 0)),
            pl.BlockSpec((halves, 1, slots), lambda i: (i, 0, 0)),
            pl.BlockSpec((halves, cells, width), lambda i: (i, 0, 0)),
            whole(cells, width),
            whole(cells, LANES),
            whole(width, LANES, at=(4 * width + 2 * ff) // LANES),
            whole(width, 3 * width),
            whole(width, width, at=3),
            whole(width, ff, at=1),
            whole(ff, width),
        ],
        out_specs=[
            pl.BlockSpec((halves, cells, width), lambda i: (i, 0, 0)),
            pl.BlockSpec((halves, slots, width), lambda i: (i, 0, 0)),
            whole(width, half_wide),
            whole(width, half_wide),
        ],
        out_shape=[
            jax.ShapeDtypeStruct((n_half, cells, width), BF16),
            jax.ShapeDtypeStruct((n_half, slots, width), BF16),
            jax.ShapeDtypeStruct((width, half_wide), BF16),
            jax.ShapeDtypeStruct((width, half_wide), BF16),
        ],
        scratch_shapes=[
            vm((width, 3 * width), F32),
            vm((width, width), F32),
            vm((width, ff), F32),
            vm((width, ff), F32),
            vm((8, width), F32),
            vm((8, width), F32),
            vm((m_rows, width), F32),
            vm((m_rows, 3 * width), BF16),
            vm((m_rows, width), F32),
            vm((m_rows, width), BF16),
            vm((m_rows, width), BF16),
            vm((width, m_rows), BF16),
            vm((width, m_rows), BF16),
            vm((m_rows, width), F32),
            vm((m_rows, width), F32),
            vm((m_rows, 3 * width), BF16),
        ],
        compiler_params=pltpu.CompilerParams(
            dimension_semantics=("arbitrary",), vmem_limit_bytes=VMEM_BYTES
        ),
        cost_estimate=pl.CostEstimate(flops=flops, bytes_accessed=40 << 20, transcendentals=0),
        name="decoder_block",
    )(
        core, rows, idx.reshape(n_half, 1, slots), cot, pos, mask,
        pack, pack, pack, pack, wd,
    )


def enc_spread(t, head_masks):
    return jnp.concatenate([t * hm.astype(BF16)[None] for hm in head_masks], axis=1)


def enc_heads(width):
    head_dim = width // HEADS_ENC
    lane = lax.broadcasted_iota(jnp.int32, (1, LANES), 1)
    return head_dim, [(lane // head_dim == h) for h in range(LANES // head_dim)]


def enc_attend_kernel(
    x_ref, mask_ref, small_ref, wqkv_ref, wo_ref, qkv_ref, p_ref, o_ref, x2_ref, vec_ref
):
    vec_ref[...] = vectors_of(small_ref)
    clips, slots, width = x_ref.shape
    m_rows = clips * slots
    head_dim, head_masks = enc_heads(width)
    scale = head_dim ** (-0.5)
    x = x_ref[...].reshape(m_rows, width).astype(F32)
    xhat, rstd = normalise(x)
    a1 = (xhat * vec_ref[0:1, :] + vec_ref[1:2, :]).astype(BF16)
    qkv_ref[...] = mm(a1, wqkv_ref[...]).astype(BF16)
    allowed = mask_ref[...] > 0.5
    for g in range(width // LANES):
        cols = lambda part: slice(part * width + g * LANES, part * width + (g + 1) * LANES)
        q3 = qkv_ref[:, cols(0)].reshape(clips, slots, LANES)
        k3 = enc_spread(qkv_ref[:, cols(1)].reshape(clips, slots, LANES), head_masks)
        v3 = enc_spread(qkv_ref[:, cols(2)].reshape(clips, slots, LANES), head_masks)
        s = bmm_t(q3, k3) * scale
        for h in range(len(head_masks)):
            sh = jnp.where(allowed, s[:, :, h * slots : (h + 1) * slots], neg_fill)
            e = jnp.exp(sh - jnp.max(sh, axis=-1, keepdims=True))
            e = e / jnp.sum(e, axis=-1, keepdims=True)
            at = (g * len(head_masks) + h) * slots
            p_ref[:, at : at + slots] = e.reshape(m_rows, slots).astype(BF16)
        span = len(head_masks) * slots
        p3 = p_ref[:, g * span : (g + 1) * span].reshape(clips, slots, span)
        o_ref[:, cols(0)] = bmm(p3, v3).reshape(m_rows, LANES).astype(BF16)
    x2_ref[...] = x_ref[...].reshape(m_rows, width).astype(F32) + mm(o_ref[...], wo_ref[...])


def enc_feed_kernel(
    x2_ref, vec_ref, wu_ref, wd_ref, proj_ref, sent_ref, enc_ref, h_ref, gp_ref, a2_s, y_s
):
    step = pl.program_id(0)

    @pl.when(step == 0)
    def _():
        xhat, rstd = normalise(x2_ref[...])
        a2_s[...] = (xhat * vec_ref[2:3, :] + vec_ref[3:4, :]).astype(BF16)
        y_s[...] = x2_ref[...]

    u = mm(a2_s[...], wu_ref[...])
    cdf, bump = gelu_parts(u)
    h = (u * cdf).astype(BF16)
    h_ref[...] = h
    gp_ref[...] = (cdf + bump).astype(BF16)
    y_s[...] += mm(h, wd_ref[...])

    @pl.when(step == pl.num_programs(0) - 1)
    def _():
        encoded = y_s[...].astype(BF16)
        enc_ref[...] = encoded
        sent_ref[...] = mm(encoded, proj_ref[...]).astype(BF16)


def enc_feed_back_kernel(
    core_ref, dsent_ref, enc_ref, proj_ref, h_ref, gp_ref, x2_ref, vec_ref, wu_ref, wd_ref,
    gproj_ref, keep_ref, give_ref, dx2_ref, gvec_ref,
    a2t_s, dz_s, dzt_s, da_s,
):
    step = pl.program_id(0)
    gain2 = vec_ref[2:3, :]

    @pl.when(step == 0)
    def _():
        dsent = dsent_ref[...]
        gproj_ref[...] = mm(enc_ref[...].T, dsent).astype(BF16)
        dy = mm_t(dsent, proj_ref[...])
        dx2_ref[...] = dy
        dz = dy.astype(BF16)
        dz_s[...] = dz
        dzt_s[...] = dz.T
        xhat, rstd = normalise(x2_ref[...])
        a2t_s[...] = (xhat * gain2 + vec_ref[3:4, :]).astype(BF16).T
        da_s[...] = jnp.zeros_like(da_s)

    dh = mm_t(dz_s[...], wd_ref[...])
    du = (gp_ref[...].astype(F32) * dh).astype(BF16)
    down_grad = mm(dzt_s[...], h_ref[...]).astype(BF16)
    up_grad = mm(a2t_s[...], du).astype(BF16)
    da_s[...] += mm_t(du, wu_ref[...])
    first = core_ref[0] == 0
    keep_ref[...] = jnp.where(first, up_grad, down_grad)
    give_ref[...] = jnp.where(first, down_grad, up_grad)

    @pl.when(step == pl.num_programs(0) - 1)
    def _():
        da = da_s[...]
        xhat, rstd = normalise(x2_ref[...])
        gvec_ref[...] = jnp.zeros_like(gvec_ref)
        gvec_ref[2:3, :] = jnp.sum(da * xhat, axis=0, keepdims=True)
        gvec_ref[3:4, :] = jnp.sum(da, axis=0, keepdims=True)
        dx2_ref[...] += norm_back(da, xhat, rstd, gain2)


def enc_attend_back_kernel(
    core_ref, dx2_ref, o_ref, qkv_ref, p_ref, x_ref, vec_ref, wqkv_ref, wo_ref, gproj_ref, gvec2_ref,
    keep_ref, give_ref, dvis_ref,
    gvec_ref, do_s, dqkv_s, gqkv_s, go_s,
):
    clips, slots, width = x_ref.shape
    m_rows = clips * slots
    head_dim, head_masks = enc_heads(width)
    count = len(head_masks)
    scale = head_dim ** (-0.5)
    gain1, shift1 = vec_ref[0:1, :], vec_ref[1:2, :]
    dy2 = dx2_ref[...].astype(BF16)
    go_s[...] = mm(o_ref[...].T, dy2).astype(BF16)
    do_s[...] = mm_t(dy2, wo_ref[...]).astype(BF16)

    def fold(t):
        out = t[:, 0:slots, :]
        for h in range(1, count):
            out = jnp.where(head_masks[h][None], t[:, h * slots : (h + 1) * slots, :], out)
        return out.reshape(m_rows, LANES).astype(BF16)

    for g in range(width // LANES):
        cols = lambda part: slice(part * width + g * LANES, part * width + (g + 1) * LANES)
        q3 = qkv_ref[:, cols(0)].reshape(clips, slots, LANES)
        k3 = enc_spread(qkv_ref[:, cols(1)].reshape(clips, slots, LANES), head_masks)
        v3 = enc_spread(qkv_ref[:, cols(2)].reshape(clips, slots, LANES), head_masks)
        do3 = do_s[:, cols(0)].reshape(clips, slots, LANES)
        span = count * slots
        p3 = p_ref[:, g * span : (g + 1) * span].reshape(clips, slots, span)
        dp = bmm_t(do3, v3)
        parts = []
        for h in range(count):
            hs = slice(h * slots, (h + 1) * slots)
            ph = p3[:, :, hs].astype(F32)
            dph = dp[:, :, hs]
            mean = jnp.sum(ph * dph, axis=-1, keepdims=True)
            parts.append((ph * (dph - mean) * scale).astype(BF16))
        draw3 = jnp.concatenate(parts, axis=2)
        dqkv_s[:, cols(0)] = bmm(draw3, k3).reshape(m_rows, LANES).astype(BF16)
        dqkv_s[:, cols(1)] = fold(bmm_l(draw3, q3))
        dqkv_s[:, cols(2)] = fold(bmm_l(p3, do3))

    x = x_ref[...].reshape(m_rows, width).astype(F32)
    xhat, rstd = normalise(x)
    a1t = (xhat * gain1 + shift1).astype(BF16).T
    gqkv_s[...] = mm(a1t, dqkv_s[...]).astype(BF16)
    da = mm_t(dqkv_s[...], wqkv_ref[...])
    gvec_ref[...] = gvec2_ref[...]
    gvec_ref[0:1, :] = jnp.sum(da * xhat, axis=0, keepdims=True)
    gvec_ref[1:2, :] = jnp.sum(da, axis=0, keepdims=True)
    dx = dx2_ref[...] + norm_back(da, xhat, rstd, gain1)
    dvis_ref[...] = dx.reshape(clips, slots, width).astype(BF16)
    half = keep_ref.shape[1]
    tail = 3 * width - half
    sent = gproj_ref.shape[1]

    def fill(first, second):
        first[...] = gqkv_s[:, :half]
        second[:, :tail] = gqkv_s[:, half:]
        second[:, tail : tail + width] = go_s[...]
        second[:, tail + width : tail + width + sent] = gproj_ref[...]
        end = tail + width + sent
        second[:, end : end + LANES] = columns_of_vectors(gvec_ref[...])
        second[:, end + LANES :] = jnp.zeros((width, half - end - LANES), BF16)

    by_core(core_ref, fill, keep_ref, give_ref)


FEED_CHUNK = 512


def whole_call(kernel, args, outs, scratch, name, flops, steps=1):
    arrays, specs = [], []

    def block(shape, at):
        if callable(at):
            return pl.BlockSpec(shape, at)
        index = (0,) * (len(shape) - 1) + (at,)
        return pl.BlockSpec(shape, lambda i: index, pipeline_mode=pl.Buffered(1))

    for arg in args:
        array, shape, at = arg if isinstance(arg, tuple) else (arg, arg.shape, 0)
        arrays.append(array)
        specs.append(pl.BlockSpec(memory_space=pltpu.SMEM) if len(shape) == 1 else block(shape, at))
    out_specs, shapes = [], []
    for out in outs:
        shape, dtype, part, at = out if len(out) == 4 else out + (out[0], 0)
        out_specs.append(block(part, at))
        shapes.append(jax.ShapeDtypeStruct(shape, dtype))
    return pl.pallas_call(
        kernel,
        grid=(steps,),
        in_specs=specs,
        out_specs=out_specs,
        out_shape=shapes,
        scratch_shapes=[pltpu.VMEM(s, d) for s, d in scratch],
        compiler_params=pltpu.CompilerParams(
            dimension_semantics=("arbitrary",), vmem_limit_bytes=VMEM_BYTES
        ),
        cost_estimate=pl.CostEstimate(flops=flops, bytes_accessed=16 << 20, transcendentals=0),
        name=name,
    )(*arrays)


def enc_blocks(pack, width, ff, sent):
    return (
        (pack, (width, 3 * width), 0),
        (pack, (width, width), 3),
        (pack, (width, ff), 4 * width // ff),
        (pack, (width, sent), (4 * width + ff) // sent),
        (pack, (width, LANES), (4 * width + ff + sent) // LANES),
    )


def enc_attend(x, mask, blocks):
    clips, slots, width = x.shape
    m = clips * slots
    outs = [
        ((m, 3 * width), BF16),
        ((m, HEADS_ENC * slots), BF16),
        ((m, width), BF16),
        ((m, width), F32),
        ((8, width), F32),
    ]
    qkv, out, _, _, small = blocks
    return whole_call(enc_attend_kernel, (x, mask, small, qkv, out), outs, [], "enc_attend", 10**10)


def enc_feed(x2, vecs, blocks, wd):
    m, width = x2.shape
    ff, chunk = wd.shape[0], FEED_CHUNK
    _, _, up, proj, _ = blocks
    across, down = lambda i: (0, i), lambda i: (i, 0)
    up = (up[0], (width, chunk), lambda i: (0, 4 * width // chunk + i))
    kept = ((m, ff), BF16, (m, chunk), across)
    outs = [((m, proj[1][1]), BF16), ((m, width), BF16), kept, kept]
    scratch = [((m, width), BF16), ((m, width), F32)]
    args = (x2, vecs, up, (wd, (chunk, width), down), proj)
    return whole_call(enc_feed_kernel, args, outs, scratch, "enc_feed", 14 * 10**9, ff // chunk)


def enc_feed_back(core, dsent, enc, h, gp, x2, vecs, blocks, wd):
    m, width = x2.shape
    ff, chunk = wd.shape[0], FEED_CHUNK
    _, _, up, proj, _ = blocks
    across, down = lambda i: (0, i), lambda i: (i, 0)
    up = (up[0], (width, chunk), lambda i: (0, 4 * width // chunk + i))
    half = ((width, ff), BF16, (width, chunk), across)
    outs = [(proj[1], BF16), half, half, ((m, width), F32), ((8, width), F32)]
    scratch = [((width, m), BF16), ((m, width), BF16), ((width, m), BF16), ((m, width), F32)]
    args = (core, dsent, enc, proj, (h, (m, chunk), across), (gp, (m, chunk), across), x2, vecs, up)
    args += ((wd, (chunk, width), down),)
    return whole_call(
        enc_feed_back_kernel, args, outs, scratch, "enc_feed_back", 18 * 10**9, ff // chunk
    )


def attend_half(width, sent):
    blocks = (4 * width + sent + LANES) // LANES
    return (blocks + 1) // 2 * LANES


def enc_attend_back(core, dx2, o, qkv, p, x, vecs, blocks, gproj, gvec):
    m, width = dx2.shape
    w_qkv, w_out, _, _, _ = blocks
    half = (width, attend_half(width, gproj.shape[1]))
    outs = [(half, BF16), (half, BF16), (x.shape, BF16)]
    scratch = [
        ((8, width), F32),
        ((m, width), BF16),
        ((m, 3 * width), BF16),
        ((width, 3 * width), BF16),
        ((width, width), BF16),
    ]
    args = (core, dx2, o, qkv, p, x, vecs, w_qkv, w_out, gproj, gvec)
    return whole_call(enc_attend_back_kernel, args, outs, scratch, "enc_attend_back", 14 * 10**9)


def unpack_kernel(sections, pieces, talls, smalls, packed_ref, *out_refs):
    chips, _, unit, _ = packed_ref.shape

    def read(place, start, size):
        at, part = place
        first, width, count = sections[at]
        blocks = [
            packed_ref[:, part, :, first + k * width + start : first + k * width + start + size]
            for k in range(count)
        ]
        block = blocks[0] if count == 1 else jnp.concatenate(blocks, axis=1)
        return block.reshape(chips * unit * count, size).astype(F32)

    for out, to, place, start, size in pieces:
        out_refs[out][:, to : to + size] = read(place, start, size)
    chunk = 512
    for out, place, start, size in talls:
        for c in range(size // chunk):
            rows = slice(c * chunk, (c + 1) * chunk)
            out_refs[out][rows, :] = read(place, start + c * chunk, chunk).T
    for out, place, start in smalls:
        out_refs[out][...] = read(place, start, LANES).T[0:8, :]


def even_units(packed, sections):
    parts = []
    for first, width, count in sections:
        chips, two, unit, _ = packed.shape
        part = packed[..., first : first + width * count].reshape(chips, two, unit, count, width)
        part = part.transpose(1, 0, 3, 2, 4).reshape(two, 16, count, chips * unit // 16, width)
        parts.append(part.transpose(1, 0, 3, 2, 4).reshape(16, two, chips * unit // 16, count * width))
    return jnp.concatenate(parts, axis=-1)


def unpack_sums(packed, sections, outs, pieces, talls, smalls):
    if packed.shape[2] % 16:
        packed = even_units(packed, sections)
    chips, _, unit, wide = packed.shape
    group = 8
    specs, shapes = [], []
    for at, width, turned in outs:
        step = group * unit * sections[at][2]
        height = chips * unit * sections[at][2]
        if turned:
            specs.append(pl.BlockSpec((turned, step), lambda i: (0, i)))
            shapes.append(jax.ShapeDtypeStruct((turned, height), F32))
        else:
            specs.append(pl.BlockSpec((step, width), lambda i: (i, 0)))
            shapes.append(jax.ShapeDtypeStruct((height, width), F32))
    return pl.pallas_call(
        functools.partial(unpack_kernel, sections, pieces, talls, smalls),
        grid=(chips // group,),
        in_specs=[pl.BlockSpec((group, 2, unit, wide), lambda i: (i, 0, 0, 0))],
        out_specs=specs,
        out_shape=shapes,
        compiler_params=pltpu.CompilerParams(vmem_limit_bytes=VMEM_BYTES),
        cost_estimate=pl.CostEstimate(
            flops=0, bytes_accessed=12 * chips * unit * wide, transcendentals=0
        ),
        name="unpack_sums",
    )(packed)


AXES = ("clip", "band")


def partner_pairs(total, mask):
    return [(i, i ^ mask) for i in range(total)]


def add_low(*parts):
    return sum(part.astype(F32) for part in parts).astype(BF16)


class RunningSum:
    def __init__(self, keep, give, total):
        bits = total.bit_length() - 1
        self.total = total
        self.cut = keep.shape[1] // 256 * 128
        got = lax.ppermute(give, AXES, partner_pairs(total, 1))
        rows = keep.shape[0] // (total // 2)
        self.held = [add_low(keep, got).reshape((2,) * (bits - 1) + (rows, keep.shape[1]))]
        self.left = [list(range(bits - 1, 0, -1))]
        self.plan = [[[2], [1]], [[1], [2]]]
        rest = list(range(3, bits))
        while rest:
            self.plan.append([rest[:2]])
            rest = rest[2:]

    def offers(self):
        me = lax.axis_index(AXES)
        groups = self.plan[0]
        if len(groups) > len(self.held):
            (held,), (left,) = self.held, self.left
            self.held = [held[..., : self.cut], held[..., self.cut :]]
            self.left = [list(left), list(left)]
        if len(groups) < len(self.held):
            self.held = [jnp.concatenate(self.held, axis=-1)]
            self.left = self.left[:1]
        self.keep, gives, self.masks = [], [], []
        for held, left, group in zip(self.held, self.left, groups):
            low, ways = group[0], 1 << len(group)
            place = left.index(group[-1])
            mine = (me >> low) & (ways - 1)
            shape = held.shape
            held = held.reshape(shape[:place] + (ways,) + shape[place + len(group) :])
            self.keep.append(lax.dynamic_index_in_dim(held, mine, place, keepdims=False))
            for k in range(1, ways):
                gives.append(lax.dynamic_index_in_dim(held, mine ^ k, place, keepdims=False))
                self.masks.append(k << low)
            for bit in group:
                left.remove(bit)
        return gives

    def deliver(self, gives):
        got = [
            lax.ppermute(give, AXES, partner_pairs(self.total, mask))
            for give, mask in zip(gives, self.masks)
        ]
        each = len(got) // len(self.keep)
        self.held = [
            add_low(keep, *got[i * each : (i + 1) * each]) for i, keep in enumerate(self.keep)
        ]
        self.plan = self.plan[1:]

    def finish(self):
        while self.plan:
            self.deliver(self.offers())
        return jnp.concatenate(self.held, axis=-1)


class RunningGather:
    def __init__(self, shard, total):
        bits = total.bit_length() - 1
        self.total = total
        self.cut = (shard.shape[1] + LANES) // 256 * 128
        self.shape = shard.shape
        rest, self.plan = list(range(3, bits)), []
        while rest:
            self.plan.append([rest[:2]])
            rest = rest[2:]
        self.plan += [[[1], [2]], [[2], [1]], [[0]]]
        self.held, self.have = [shard], [[]]

    def offers(self):
        groups = self.plan[0]
        if len(groups) > len(self.held):
            (held,), (have,) = self.held, self.have
            self.held = [held[..., : self.cut], held[..., self.cut :]]
            self.have = [list(have), list(have)]
        if len(groups) < len(self.held):
            self.held = [jnp.concatenate(self.held, axis=-1)]
            self.have = self.have[:1]
        gives, self.masks = [], []
        for held, group in zip(self.held, groups):
            for k in range(1, 1 << len(group)):
                gives.append(held)
                self.masks.append(k << group[0])
        return gives

    def deliver(self, gives):
        me = lax.axis_index(AXES)
        got = [
            lax.ppermute(give, AXES, partner_pairs(self.total, mask))
            for give, mask in zip(gives, self.masks)
        ]
        each = len(got) // len(self.held)
        for i, group in enumerate(self.plan[0]):
            parts = [self.held[i]] + got[i * each : (i + 1) * each]
            for b, bit in enumerate(group):
                flip = ((me >> bit) & 1) == 1
                parts = [jnp.where(flip, parts[k ^ (1 << b)], part) for k, part in enumerate(parts)]
            self.have[i] = sorted(self.have[i] + group, reverse=True)
            at = self.have[i].index(group[-1])
            held = jnp.stack(parts, axis=at)
            self.held[i] = held.reshape(held.shape[:at] + (2,) * len(group) + held.shape[at + 1 :])
        self.plan = self.plan[1:]

    def finish(self):
        while self.plan:
            self.deliver(self.offers())
        return self.held[0].reshape((self.total,) + self.shape)


def together(*groups):
    return lax.optimization_barrier(groups)


def gather_rows(shard):
    return lax.all_gather(shard, AXES, axis=0, tiled=True)


def columns_of(vectors):
    block = jnp.stack(vectors, axis=1)
    return jnp.pad(block, ((0, 0), (0, LANES - len(vectors))))


def blocks_beside(tall, rows):
    return [tall[i : i + rows] for i in range(0, tall.shape[0], rows)]


def blocks_below(beside, total, width):
    rows = beside.shape[0] // total
    count = beside.shape[1] // width
    parts = [beside[:, i * width : (i + 1) * width].reshape(total, rows, width) for i in range(count)]
    return jnp.concatenate(parts, axis=1)


def swap_band(array, bit):
    return lax.ppermute(array, "band", [(i, i ^ bit) for i in range(4)])


def owners_to_bands(array):
    band = lax.axis_index("band")
    half, side = band // 2, band % 2
    own = lax.dynamic_index_in_dim(array, half, 0, keepdims=False)
    got = swap_band(lax.dynamic_index_in_dim(array, 1 - half, 0, keepdims=False), 2)
    pair = jnp.stack([jnp.where(half == 0, own, got), jnp.where(half == 0, got, own)])
    other = swap_band(pair, 1)
    return jnp.stack([jnp.where(side == 0, pair, other), jnp.where(side == 0, other, pair)], axis=1)


def join_bands(array):
    side = lax.axis_index("band") % 2
    own = lax.dynamic_index_in_dim(array, side, 1, keepdims=False)
    return own + swap_band(lax.dynamic_index_in_dim(array, 1 - side, 1, keepdims=False), 1)


def bands_to_owners(pair):
    half = lax.axis_index("band") // 2
    own = lax.dynamic_index_in_dim(pair, half, 0, keepdims=False)
    got = swap_band(lax.dynamic_index_in_dim(pair, 1 - half, 0, keepdims=False), 2)
    return jnp.stack([jnp.where(half == 0, own, got), jnp.where(half == 0, got, own)])


def position_table(places):
    half_width = D_DEC // 2
    omega_vec = jnp.exp(
        jnp.arange(half_width, dtype=F32) * (-math.log(10000.0) / half_width)
    )
    angles = places.astype(F32)[..., None] * omega_vec
    return jnp.concatenate([jnp.sin(angles), jnp.cos(angles)], axis=-1)


def shards(
    visible,
    keep_index,
    visible_count,
    enc_gain1,
    enc_shift1,
    enc_qkv,
    enc_out,
    enc_gain2,
    enc_shift2,
    enc_up,
    enc_down,
    proj,
    mask_token,
    dec_gain1,
    dec_shift1,
    dec_qkv,
    dec_out,
    dec_gain2,
    dec_shift2,
    dec_up,
    dec_down,
    cotangent,
):
    total = lax.axis_size(AXES)
    enc_wide, dec_wide = enc_out.shape[1], dec_out.shape[1]
    enc_ff, dec_ff = enc_up.shape[1], dec_up.shape[1]
    core = (lax.axis_index(AXES) % 2).reshape(1)
    enc_small = columns_of([enc_gain1, enc_shift1, enc_gain2, enc_shift2])
    enc_pack = gather_rows(jnp.concatenate([enc_qkv, enc_out, enc_up, proj, enc_small], axis=1))
    down_run = RunningGather(enc_down, total)
    while len(down_run.plan) > 3:
        down_run.deliver(down_run.offers())

    clip_count, slot_total, _ = visible.shape
    half_clips = clip_count // 2
    band_height = FREQ // 2
    slot_ids = jnp.arange(slot_total)
    valid_rows = slot_ids[None, :] < visible_count[:, None]
    valid_mask = valid_rows.astype(F32)[:, None, :]
    cell_number = jnp.where(valid_rows, keep_index, -1).reshape(2, half_clips, slot_total)
    cell_number = owners_to_bands(cell_number).reshape(-1, slot_total)

    dec_small = columns_of([dec_gain1, dec_shift1, dec_gain2, dec_shift2, mask_token])
    dec_tall = blocks_beside(dec_down, dec_out.shape[0])
    dec_pack = jnp.concatenate([dec_qkv, dec_out, dec_up] + dec_tall + [dec_small], axis=1)
    dec_run = RunningGather(dec_pack, total)
    cell_number, gives, dec_gives = together(cell_number, down_run.offers(), dec_run.offers())
    down_run.deliver(gives)
    dec_run.deliver(dec_gives)
    while len(dec_run.plan) > 3:
        dec_run.deliver(dec_run.offers())
    down_run.deliver(down_run.offers())
    gives, dec_gives = together(down_run.offers(), dec_run.offers())
    down_run.deliver(gives)
    dec_run.deliver(dec_gives)
    whole_down = down_run.finish().reshape(-1, enc_wide)
    enc_pack, whole_down, gives = together(enc_pack, whole_down, dec_run.offers())
    dec_run.deliver(gives)

    band_pick = lax.axis_index("band") % 2
    rolled_time = (cell_number // FREQ + TIME - SHIFT) % TIME
    rolled_freq = (cell_number % FREQ + FREQ - SHIFT) % FREQ
    here = (cell_number >= 0) & (rolled_freq // band_height == band_pick)
    arrived_index = jnp.where(here, rolled_time * band_height + rolled_freq % band_height, -1)

    blocks = enc_blocks(enc_pack, enc_wide, enc_ff, dec_wide)
    qkv, probs, mixed, middle, vecs = enc_attend(visible, valid_mask, blocks)
    sent_rows, encoded, hidden, slope = enc_feed(middle, vecs, blocks, whole_down)
    sent_rows, gives = together(sent_rows, dec_run.offers())
    dec_run.deliver(gives)
    dec_pack = dec_run.finish().reshape(-1, dec_pack.shape[1])
    dec_end = 4 * dec_wide + dec_ff
    dec_whole_down = blocks_below(dec_pack[:, dec_end : dec_end + dec_ff], total, dec_wide)
    dec_whole_down = dec_whole_down.reshape(-1, dec_wide)
    arrived_rows = owners_to_bands(sent_rows.reshape(2, half_clips, slot_total, dec_wide))
    half_total = 4 * half_clips

    cell_count = TIME * band_height
    places = jnp.arange(cell_count)
    cell_freq = band_pick * band_height + places % band_height
    patch_number = (places // band_height + SHIFT) % TIME * FREQ + (cell_freq + SHIFT) % FREQ
    span = D_DEC // HEADS_DEC
    query = places[:, None]
    key = query // span * span + jnp.arange(LANES)[None, :] % span

    def label(cell):
        late = cell // band_height >= TIME - SHIFT
        high = band_pick * band_height + cell % band_height >= FREQ - SHIFT
        return late.astype(jnp.int32) * 2 + high.astype(jnp.int32)

    cells_in = WINDOW * WINDOW
    allowed = (query // cells_in == key // cells_in) & (label(query) == label(key))
    decoded, returning, keep, give = decoder_block(
        core,
        arrived_rows.reshape(half_total, slot_total, dec_wide),
        arrived_index,
        cotangent.reshape(half_total, cell_count, dec_wide),
        position_table(patch_number),
        allowed.astype(F32),
        dec_pack,
        dec_whole_down,
    )
    decoded_out = decoded.reshape(cotangent.shape)

    returning = join_bands(returning.reshape(2, 2, half_clips, slot_total, dec_wide))
    returning, keep, give = together(returning, keep, give)
    dec_run = RunningSum(keep, give, total)
    grad_sent = bands_to_owners(returning).reshape(-1, dec_wide)
    grad_sent, gives = together(grad_sent, dec_run.offers())
    dec_run.deliver(gives)
    g_proj, keep, give, grad_middle, g_vec = enc_feed_back(
        core, grad_sent, encoded, hidden, slope, middle, vecs, blocks, whole_down
    )
    keep, give, grad_middle, gives = together(keep, give, grad_middle, dec_run.offers())
    dec_run.deliver(gives)
    feed_run = RunningSum(keep, give, total)
    keep, give, grad_visible = enc_attend_back(
        core, grad_middle, mixed, qkv, probs, visible, vecs, blocks, g_proj, g_vec
    )
    keep, give, gives, feed_gives = together(keep, give, dec_run.offers(), feed_run.offers())
    dec_run.deliver(gives)
    feed_run.deliver(feed_gives)
    keep, give, dec_shard, feed_gives = together(keep, give, dec_run.finish(), feed_run.offers())
    feed_run.deliver(feed_gives)
    attend_run = RunningSum(keep, give, total)
    feed_gives, gives = together(feed_run.offers(), attend_run.offers())
    feed_run.deliver(feed_gives)
    attend_run.deliver(gives)
    feed_shard = feed_run.finish()
    feed_shard, gives = together(feed_shard, attend_run.offers())
    unit = dec_shard.shape[0] // 2
    dec_units = [dec_shard[k * unit : (k + 1) * unit] for k in range(2)]
    feed_units = [feed_shard[k * unit : (k + 1) * unit] for k in range(3)]
    most_sum = gather_rows(jnp.concatenate(dec_units + feed_units, axis=1))
    attend_run.deliver(gives)
    attend_shard = attend_run.finish()
    attend_sum = RunningGather(attend_shard, total).finish()

    half = attend_shard.shape[1]
    tail = 3 * enc_wide - half
    e_qkv, e_out, e_proj, enc_vecs = unpack_sums(
        attend_sum.reshape((total // 2, 2) + attend_shard.shape),
        ((0, half, 1),),
        ((0, 3 * enc_wide, 0), (0, enc_wide, 0), (0, dec_wide, 0), (0, 0, 8)),
        (
            (0, 0, (0, 0), 0, half),
            (0, half, (0, 1), 0, tail),
            (1, 0, (0, 1), tail, enc_wide),
            (2, 0, (0, 1), tail + enc_wide, dec_wide),
        ),
        (),
        ((3, (0, 1), tail + enc_wide + dec_wide),),
    )
    half = dec_ff // 2
    dec_half = dec_shard.shape[1]
    d_qkv, d_out, d_up, d_down, dec_vecs, e_up, e_down = unpack_sums(
        most_sum.reshape(total // 2, 2, unit, most_sum.shape[1]),
        ((0, dec_half, 2), (2 * dec_half, enc_ff, 3)),
        (
            (0, 3 * dec_wide, 0),
            (0, dec_wide, 0),
            (0, dec_ff, 0),
            (0, 0, dec_ff),
            (0, 0, 8),
            (1, enc_ff, 0),
            (1, 0, enc_ff),
        ),
        (
            (0, 0, (0, 0), 0, 3 * dec_wide),
            (1, 0, (0, 0), 3 * dec_wide, dec_wide),
            (2, 0, (0, 0), 4 * dec_wide, half),
            (2, half, (0, 1), 0, half),
            (5, 0, (1, 0), 0, enc_ff),
        ),
        ((3, (0, 1), half, dec_ff), (6, (1, 1), 0, enc_ff)),
        ((4, (0, 0), 4 * dec_wide + half),),
    )
    return (
        decoded_out,
        grad_visible,
        enc_vecs[0],
        enc_vecs[1],
        e_qkv,
        e_out,
        enc_vecs[2],
        enc_vecs[3],
        e_up,
        e_down,
        e_proj,
        dec_vecs[4],
        dec_vecs[0],
        dec_vecs[1],
        d_qkv,
        d_out,
        dec_vecs[2],
        dec_vecs[3],
        d_up,
        d_down,
    )


def solution(mesh):
    return jax.shard_map(
        shards,
        mesh=mesh,
        in_specs=(
            P(("clip", "band"), None, None),
            P(("clip", "band"), None),
            P(("clip", "band")),
            P(("clip", "band")),
            P(("clip", "band")),
            P(("clip", "band"), None),
            P(("clip", "band"), None),
            P(("clip", "band")),
            P(("clip", "band")),
            P(("clip", "band"), None),
            P(("clip", "band"), None),
            P(("clip", "band"), None),
            P(("clip", "band")),
            P(("clip", "band")),
            P(("clip", "band")),
            P(("clip", "band"), None),
            P(("clip", "band"), None),
            P(("clip", "band")),
            P(("clip", "band")),
            P(("clip", "band"), None),
            P(("clip", "band"), None),
            P(("clip", "band"), None, None, None, None),
        ),
        out_specs=(
            P(("clip", "band"), None, None, None, None),
            P(("clip", "band"), None, None),
            P(),
            P(),
            P(),
            P(),
            P(),
            P(),
            P(),
            P(),
            P(),
            P(),
            P(),
            P(),
            P(),
            P(),
            P(),
            P(),
            P(),
            P(),
        ),
        check_vma=False,
    )
```

```python
import functools
import math

import jax
import jax.numpy as jnp
from jax import lax
from jax.experimental import pallas as pl
from jax.experimental.pallas import tpu as pltpu
from jax.sharding import PartitionSpec as P

HEADS_ENC = 12
D_DEC = 512
HEADS_DEC = 16
TIME = 64
FREQ = 8
WINDOW = 4
SHIFT = 2
norm_eps = 1e-06
neg_fill = -1e30
F32 = jnp.float32
BF16 = jnp.bfloat16
LANES = 128
VMEM_BYTES = 58 * 1024 * 1024


def mm(a, b):
    return lax.dot_general(a, b, (((1,), (0,)), ((), ())), preferred_element_type=F32)


def mm_t(a, b):
    return lax.dot_general(a, b, (((1,), (1,)), ((), ())), preferred_element_type=F32)


def bmm(a, b):
    return lax.dot_general(a, b, (((2,), (1,)), ((0,), (0,))), preferred_element_type=F32)


def bmm_t(a, b):
    return lax.dot_general(a, b, (((2,), (2,)), ((0,), (0,))), preferred_element_type=F32)


def bmm_l(a, b):
    return lax.dot_general(a, b, (((1,), (1,)), ((0,), (0,))), preferred_element_type=F32)


def normalise(x):
    centre = jnp.mean(x, axis=-1, keepdims=True)
    centred = x - centre
    rstd = lax.rsqrt(jnp.mean(centred * centred, axis=-1, keepdims=True) + norm_eps)
    return centred * rstd, rstd


def norm_back(da, xhat, rstd, gain):
    dag = da * gain
    return rstd * (
        dag
        - jnp.mean(dag, axis=-1, keepdims=True)
        - xhat * jnp.mean(dag * xhat, axis=-1, keepdims=True)
    )


def gelu_parts(u):
    size = jnp.abs(u) * 0.7071067811865476
    bell = jnp.exp(-0.5 * u * u)
    t = 1.0 / (1.0 + 0.3275911 * size)
    poly = 0.530702715
    poly = poly * t - 0.726576013
    poly = poly * t + 0.710706871
    poly = poly * t - 0.142248368
    poly = poly * t + 0.127414796
    tail = poly * t * bell
    cdf = jnp.where(u >= 0, 1.0 - tail, tail)
    return cdf, u * bell * 0.3989422804014327


def vectors_of(small_ref):
    return small_ref[...].astype(F32).T[0:8, :]


def columns_of_vectors(vectors):
    count, width = vectors.shape
    block = jnp.concatenate([vectors, jnp.zeros((LANES - count, width), F32)], axis=0)
    return block.T.astype(BF16)


def by_core(core_ref, fill, keep_ref, give_ref):
    @pl.when(core_ref[0] == 0)
    def _():
        fill(keep_ref, give_ref)

    @pl.when(core_ref[0] != 0)
    def _():
        fill(give_ref, keep_ref)


def segment_sum(x, ones):
    return mm(x.astype(BF16), ones)


def window_max(s):
    ahead = s
    behind = s
    for step in (1, 2, 4, 8):
        ahead = jnp.maximum(ahead, pltpu.roll(ahead, step, 1))
        behind = jnp.maximum(behind, pltpu.roll(behind, LANES - step, 1))
    return jnp.maximum(ahead, behind)


def decoder_kernel(
    core_ref, rows_ref, idx_ref, cot_ref, pos_ref, mask_ref, small_ref, wqkv_ref, wo_ref, wu_ref, wd_ref,
    out_ref, ret_ref, keep_ref, give_ref,
    acc_qkv, acc_o, acc_u, acc_d, gvec_ref, vec_ref,
    x_s, qkv_s, p_s, o_s, a2_s, a2t_s, dzt_s, da_s, y_s, dqkv_s,
):
    step = pl.program_id(0)
    last = pl.num_programs(0) - 1
    halves, cells, width = cot_ref.shape
    m_rows = halves * cells
    slots = rows_ref.shape[1]
    head_dim = width // HEADS_DEC
    heads_in = LANES // head_dim
    groups = width // LANES
    block = LANES // heads_in
    blocks = m_rows // block
    scale = head_dim ** (-0.5)
    ff = wu_ref.shape[1]
    chunk = 512

    @pl.when(step == 0)
    def _():
        acc_qkv[...] = jnp.zeros_like(acc_qkv)
        acc_o[...] = jnp.zeros_like(acc_o)
        acc_u[...] = jnp.zeros_like(acc_u)
        acc_d[...] = jnp.zeros_like(acc_d)
        gvec_ref[...] = jnp.zeros_like(gvec_ref)
        vec_ref[...] = vectors_of(small_ref)

    gain1, shift1 = vec_ref[0:1, :], vec_ref[1:2, :]
    gain2, shift2 = vec_ref[2:3, :], vec_ref[3:4, :]
    token = vec_ref[4:5, :]

    def place_of(h):
        cell = lax.broadcasted_iota(jnp.int32, (cells, slots), 0)
        return cell == idx_ref[h]

    unseen = []
    for h in range(halves):
        place = place_of(h)
        unseen_h = 1.0 - jnp.sum(place.astype(F32), axis=1, keepdims=True)
        unseen.append(unseen_h)
        x_s[h * cells : (h + 1) * cells, :] = (
            mm(place.astype(BF16), rows_ref[h]) + unseen_h * token + pos_ref[...]
        )
    xhat1, rstd1 = normalise(x_s[...])
    a1 = (xhat1 * gain1 + shift1).astype(BF16)
    qkv_s[...] = mm(a1, wqkv_ref[...]).astype(BF16)

    lane = lax.broadcasted_iota(jnp.int32, (1, LANES), 1)
    head_masks = [(lane // head_dim == h) for h in range(heads_in)]
    ones = (
        lax.broadcasted_iota(jnp.int32, (LANES, LANES), 0) // block
        == lax.broadcasted_iota(jnp.int32, (LANES, LANES), 1) // block
    ).astype(BF16)

    def spread(t):
        parts = [t * hm.astype(BF16)[None] for hm in head_masks]
        return jnp.concatenate(parts, axis=1)

    def fold(t):
        out = t[:, 0:block, :]
        for h in range(1, heads_in):
            out = jnp.where(head_masks[h][None], t[:, h * block : (h + 1) * block, :], out)
        return out

    def part(ref, base, g):
        return ref[:, base + g * LANES : base + (g + 1) * LANES].reshape(blocks, block, LANES)

    allowed = jnp.concatenate([mask_ref[...]] * halves, axis=0) > 0.5
    for g in range(groups):
        q3 = part(qkv_s, 0, g)
        k3 = spread(part(qkv_s, width, g))
        v3 = spread(part(qkv_s, 2 * width, g))
        s = bmm_t(q3, k3).reshape(m_rows, LANES) * scale
        s = jnp.where(allowed, s, neg_fill)
        e = jnp.where(allowed, jnp.exp(s - window_max(s)), 0.0)
        p = e / segment_sum(e, ones)
        p_s[:, g * LANES : (g + 1) * LANES] = p
        o = bmm(p.astype(BF16).reshape(blocks, block, LANES), v3)
        o_s[:, g * LANES : (g + 1) * LANES] = o.reshape(m_rows, LANES).astype(BF16)

    x2 = x_s[...] + mm(o_s[...], wo_ref[...])
    xhat2, rstd2 = normalise(x2)
    a2 = (xhat2 * gain2 + shift2).astype(BF16)
    a2_s[...] = a2
    a2t_s[...] = a2.T
    dz = cot_ref[...].reshape(m_rows, width)
    dzt_s[...] = dz.T
    y_s[...] = x2
    da_s[...] = jnp.zeros_like(da_s)

    for c in range(ff // chunk):
        at = slice(c * chunk, (c + 1) * chunk)
        u = mm(a2_s[...], wu_ref[:, at])
        dh = mm_t(cot_ref[...].reshape(m_rows, width), wd_ref[at, :])
        cdf, bump = gelu_parts(u)
        h = (u * cdf).astype(BF16)
        du = ((cdf + bump) * dh).astype(BF16)
        y_s[...] += mm(h, wd_ref[at, :])
        acc_d[:, at] += mm(dzt_s[...], h)
        acc_u[:, at] += mm(a2t_s[...], du)
        da_s[...] += mm_t(du, wu_ref[:, at])

    out_ref[...] = y_s[...].reshape(halves, cells, width).astype(BF16)
    da2 = da_s[...]
    gvec_ref[2:3, :] += jnp.sum(da2 * xhat2, axis=0, keepdims=True)
    gvec_ref[3:4, :] += jnp.sum(da2, axis=0, keepdims=True)
    dx2 = cot_ref[...].reshape(m_rows, width).astype(F32) + norm_back(da2, xhat2, rstd2, gain2)
    dy2 = dx2.astype(BF16)
    acc_o[...] += mm(o_s[...].T, dy2)
    do = mm_t(dy2, wo_ref[...]).astype(BF16)

    for g in range(groups):
        cols = slice(g * LANES, (g + 1) * LANES)
        q3 = part(qkv_s, 0, g)
        k3 = spread(part(qkv_s, width, g))
        v3 = spread(part(qkv_s, 2 * width, g))
        do3 = do[:, cols].reshape(blocks, block, LANES)
        p = p_s[:, cols]
        dp = bmm_t(do3, v3).reshape(m_rows, LANES)
        draw = (p * (dp - segment_sum(p * dp, ones)) * scale).astype(BF16)
        draw3 = draw.reshape(blocks, block, LANES)
        dq = bmm(draw3, k3).reshape(m_rows, LANES)
        dk = fold(bmm_l(draw3, q3)).reshape(m_rows, LANES)
        dv = fold(bmm_l(p.astype(BF16).reshape(blocks, block, LANES), do3)).reshape(m_rows, LANES)
        dqkv_s[:, g * LANES : (g + 1) * LANES] = dq.astype(BF16)
        dqkv_s[:, width + g * LANES : width + (g + 1) * LANES] = dk.astype(BF16)
        dqkv_s[:, 2 * width + g * LANES : 2 * width + (g + 1) * LANES] = dv.astype(BF16)

    xhat1, rstd1 = normalise(x_s[...])
    a1 = (xhat1 * gain1 + shift1).astype(BF16)
    dqkv = dqkv_s[...]
    acc_qkv[...] += mm(a1.T, dqkv)
    da1 = mm_t(dqkv, wqkv_ref[...])
    gvec_ref[0:1, :] += jnp.sum(da1 * xhat1, axis=0, keepdims=True)
    gvec_ref[1:2, :] += jnp.sum(da1, axis=0, keepdims=True)
    dx = dx2 + norm_back(da1, xhat1, rstd1, gain1)
    for h in range(halves):
        dx_h = dx[h * cells : (h + 1) * cells, :]
        gvec_ref[4:5, :] += jnp.sum(unseen[h] * dx_h, axis=0, keepdims=True)
        place = place_of(h).astype(F32).T.astype(BF16)
        ret_ref[h] = mm(place, dx_h.astype(BF16)).astype(BF16)

    @pl.when(step == last)
    def _():
        half = ff // 2

        def fill(first, second):
            first[:, : 3 * width] = acc_qkv[...].astype(BF16)
            first[:, 3 * width : 4 * width] = acc_o[...].astype(BF16)
            first[:, 4 * width : 4 * width + half] = acc_u[:, :half].astype(BF16)
            first[:, 4 * width + half :] = columns_of_vectors(gvec_ref[...])
            second[:, :half] = acc_u[:, half:].astype(BF16)
            second[:, half : half + ff] = acc_d[...].astype(BF16)
            second[:, half + ff :] = jnp.zeros((width, second.shape[1] - half - ff), BF16)

        by_core(core_ref, fill, keep_ref, give_ref)


def decoder_block(core, rows, idx, cot, pos, mask, pack, wd):
    n_half, slots, width = rows.shape
    cells = cot.shape[1]
    ff = wd.shape[0]
    halves = 2
    m_rows = halves * cells
    half_wide = 4 * width + ff // 2 + LANES
    vm = pltpu.VMEM
    flops = 6 * n_half * cells * (4 * width + 2 * ff) * width * 2

    def whole(*shape, at=0):
        index = (0,) * (len(shape) - 1) + (at,)
        return pl.BlockSpec(shape, lambda i: index, pipeline_mode=pl.Buffered(1))

    return pl.pallas_call(
        decoder_kernel,
        grid=(n_half // halves,),
        in_specs=[
            pl.BlockSpec(memory_space=pltpu.SMEM),
            pl.BlockSpec((halves, slots, width), lambda i: (i, 0, 0)),
            pl.BlockSpec((halves, 1, slots), lambda i: (i, 0, 0)),
            pl.BlockSpec((halves, cells, width), lambda i: (i, 0, 0)),
            whole(cells, width),
            whole(cells, LANES),
            whole(width, LANES, at=(4 * width + 2 * ff) // LANES),
            whole(width, 3 * width),
            whole(width, width, at=3),
            whole(width, ff, at=1),
            whole(ff, width),
        ],
        out_specs=[
            pl.BlockSpec((halves, cells, width), lambda i: (i, 0, 0)),
            pl.BlockSpec((halves, slots, width), lambda i: (i, 0, 0)),
            whole(width, half_wide),
            whole(width, half_wide),
        ],
        out_shape=[
            jax.ShapeDtypeStruct((n_half, cells, width), BF16),
            jax.ShapeDtypeStruct((n_half, slots, width), BF16),
            jax.ShapeDtypeStruct((width, half_wide), BF16),
            jax.ShapeDtypeStruct((width, half_wide), BF16),
        ],
        scratch_shapes=[
            vm((width, 3 * width), F32),
            vm((width, width), F32),
            vm((width, ff), F32),
            vm((width, ff), F32),
            vm((8, width), F32),
            vm((8, width), F32),
            vm((m_rows, width), F32),
            vm((m_rows, 3 * width), BF16),
            vm((m_rows, width), F32),
            vm((m_rows, width), BF16),
            vm((m_rows, width), BF16),
            vm((width, m_rows), BF16),
            vm((width, m_rows), BF16),
            vm((m_rows, width), F32),
            vm((m_rows, width), F32),
            vm((m_rows, 3 * width), BF16),
        ],
        compiler_params=pltpu.CompilerParams(
            dimension_semantics=("arbitrary",), vmem_limit_bytes=VMEM_BYTES
        ),
        cost_estimate=pl.CostEstimate(flops=flops, bytes_accessed=40 << 20, transcendentals=0),
        name="decoder_block",
    )(
        core, rows, idx.reshape(n_half, 1, slots), cot, pos, mask,
        pack, pack, pack, pack, wd,
    )


def enc_spread(t, head_masks):
    return jnp.concatenate([t * hm.astype(BF16)[None] for hm in head_masks], axis=1)


def enc_heads(width):
    head_dim = width // HEADS_ENC
    lane = lax.broadcasted_iota(jnp.int32, (1, LANES), 1)
    return head_dim, [(lane // head_dim == h) for h in range(LANES // head_dim)]


def enc_attend_kernel(
    x_ref, mask_ref, small_ref, wqkv_ref, wo_ref, qkv_ref, p_ref, o_ref, x2_ref, vec_ref
):
    vec_ref[...] = vectors_of(small_ref)
    clips, slots, width = x_ref.shape
    m_rows = clips * slots
    head_dim, head_masks = enc_heads(width)
    scale = head_dim ** (-0.5)
    x = x_ref[...].reshape(m_rows, width).astype(F32)
    xhat, rstd = normalise(x)
    a1 = (xhat * vec_ref[0:1, :] + vec_ref[1:2, :]).astype(BF16)
    qkv_ref[...] = mm(a1, wqkv_ref[...]).astype(BF16)
    allowed = mask_ref[...] > 0.5
    for g in range(width // LANES):
        cols = lambda part: slice(part * width + g * LANES, part * width + (g + 1) * LANES)
        q3 = qkv_ref[:, cols(0)].reshape(clips, slots, LANES)
        k3 = enc_spread(qkv_ref[:, cols(1)].reshape(clips, slots, LANES), head_masks)
        v3 = enc_spread(qkv_ref[:, cols(2)].reshape(clips, slots, LANES), head_masks)
        s = bmm_t(q3, k3) * scale
        for h in range(len(head_masks)):
            sh = jnp.where(allowed, s[:, :, h * slots : (h + 1) * slots], neg_fill)
            e = jnp.exp(sh - jnp.max(sh, axis=-1, keepdims=True))
            e = e / jnp.sum(e, axis=-1, keepdims=True)
            at = (g * len(head_masks) + h) * slots
            p_ref[:, at : at + slots] = e.reshape(m_rows, slots).astype(BF16)
        span = len(head_masks) * slots
        p3 = p_ref[:, g * span : (g + 1) * span].reshape(clips, slots, span)
        o_ref[:, cols(0)] = bmm(p3, v3).reshape(m_rows, LANES).astype(BF16)
    x2_ref[...] = x_ref[...].reshape(m_rows, width).astype(F32) + mm(o_ref[...], wo_ref[...])


def enc_feed_kernel(
    x2_ref, vec_ref, wu_ref, wd_ref, proj_ref, sent_ref, enc_ref, h_ref, gp_ref, a2_s, y_s
):
    step = pl.program_id(0)

    @pl.when(step == 0)
    def _():
        xhat, rstd = normalise(x2_ref[...])
        a2_s[...] = (xhat * vec_ref[2:3, :] + vec_ref[3:4, :]).astype(BF16)
        y_s[...] = x2_ref[...]

    u = mm(a2_s[...], wu_ref[...])
    cdf, bump = gelu_parts(u)
    h = (u * cdf).astype(BF16)
    h_ref[...] = h
    gp_ref[...] = (cdf + bump).astype(BF16)
    y_s[...] += mm(h, wd_ref[...])

    @pl.when(step == pl.num_programs(0) - 1)
    def _():
        encoded = y_s[...].astype(BF16)
        enc_ref[...] = encoded
        sent_ref[...] = mm(encoded, proj_ref[...]).astype(BF16)


def enc_feed_back_kernel(
    core_ref, dsent_ref, enc_ref, proj_ref, h_ref, gp_ref, x2_ref, vec_ref, wu_ref, wd_ref,
    gproj_ref, keep_ref, give_ref, dx2_ref, gvec_ref,
    a2t_s, dz_s, dzt_s, da_s,
):
    step = pl.program_id(0)
    gain2 = vec_ref[2:3, :]

    @pl.when(step == 0)
    def _():
        dsent = dsent_ref[...]
        gproj_ref[...] = mm(enc_ref[...].T, dsent).astype(BF16)
        dy = mm_t(dsent, proj_ref[...])
        dx2_ref[...] = dy
        dz = dy.astype(BF16)
        dz_s[...] = dz
        dzt_s[...] = dz.T
        xhat, rstd = normalise(x2_ref[...])
        a2t_s[...] = (xhat * gain2 + vec_ref[3:4, :]).astype(BF16).T
        da_s[...] = jnp.zeros_like(da_s)

    dh = mm_t(dz_s[...], wd_ref[...])
    du = (gp_ref[...].astype(F32) * dh).astype(BF16)
    down_grad = mm(dzt_s[...], h_ref[...]).astype(BF16)
    up_grad = mm(a2t_s[...], du).astype(BF16)
    da_s[...] += mm_t(du, wu_ref[...])
    first = core_ref[0] == 0
    keep_ref[...] = jnp.where(first, up_grad, down_grad)
    give_ref[...] = jnp.where(first, down_grad, up_grad)

    @pl.when(step == pl.num_programs(0) - 1)
    def _():
        da = da_s[...]
        xhat, rstd = normalise(x2_ref[...])
        gvec_ref[...] = jnp.zeros_like(gvec_ref)
        gvec_ref[2:3, :] = jnp.sum(da * xhat, axis=0, keepdims=True)
        gvec_ref[3:4, :] = jnp.sum(da, axis=0, keepdims=True)
        dx2_ref[...] += norm_back(da, xhat, rstd, gain2)


def enc_attend_back_kernel(
    core_ref, dx2_ref, o_ref, qkv_ref, p_ref, x_ref, vec_ref, wqkv_ref, wo_ref, gproj_ref, gvec2_ref,
    keep_ref, give_ref, dvis_ref,
    gvec_ref, do_s, dqkv_s, gqkv_s, go_s,
):
    clips, slots, width = x_ref.shape
    m_rows = clips * slots
    head_dim, head_masks = enc_heads(width)
    count = len(head_masks)
    scale = head_dim ** (-0.5)
    gain1, shift1 = vec_ref[0:1, :], vec_ref[1:2, :]
    dy2 = dx2_ref[...].astype(BF16)
    go_s[...] = mm(o_ref[...].T, dy2).astype(BF16)
    do_s[...] = mm_t(dy2, wo_ref[...]).astype(BF16)

    def fold(t):
        out = t[:, 0:slots, :]
        for h in range(1, count):
            out = jnp.where(head_masks[h][None], t[:, h * slots : (h + 1) * slots, :], out)
        return out.reshape(m_rows, LANES).astype(BF16)

    for g in range(width // LANES):
        cols = lambda part: slice(part * width + g * LANES, part * width + (g + 1) * LANES)
        q3 = qkv_ref[:, cols(0)].reshape(clips, slots, LANES)
        k3 = enc_spread(qkv_ref[:, cols(1)].reshape(clips, slots, LANES), head_masks)
        v3 = enc_spread(qkv_ref[:, cols(2)].reshape(clips, slots, LANES), head_masks)
        do3 = do_s[:, cols(0)].reshape(clips, slots, LANES)
        span = count * slots
        p3 = p_ref[:, g * span : (g + 1) * span].reshape(clips, slots, span)
        dp = bmm_t(do3, v3)
        parts = []
        for h in range(count):
            hs = slice(h * slots, (h + 1) * slots)
            ph = p3[:, :, hs].astype(F32)
            dph = dp[:, :, hs]
            mean = jnp.sum(ph * dph, axis=-1, keepdims=True)
            parts.append((ph * (dph - mean) * scale).astype(BF16))
        draw3 = jnp.concatenate(parts, axis=2)
        dqkv_s[:, cols(0)] = bmm(draw3, k3).reshape(m_rows, LANES).astype(BF16)
        dqkv_s[:, cols(1)] = fold(bmm_l(draw3, q3))
        dqkv_s[:, cols(2)] = fold(bmm_l(p3, do3))

    x = x_ref[...].reshape(m_rows, width).astype(F32)
    xhat, rstd = normalise(x)
    a1t = (xhat * gain1 + shift1).astype(BF16).T
    gqkv_s[...] = mm(a1t, dqkv_s[...]).astype(BF16)
    da = mm_t(dqkv_s[...], wqkv_ref[...])
    gvec_ref[...] = gvec2_ref[...]
    gvec_ref[0:1, :] = jnp.sum(da * xhat, axis=0, keepdims=True)
    gvec_ref[1:2, :] = jnp.sum(da, axis=0, keepdims=True)
    dx = dx2_ref[...] + norm_back(da, xhat, rstd, gain1)
    dvis_ref[...] = dx.reshape(clips, slots, width).astype(BF16)
    half = keep_ref.shape[1]
    tail = 3 * width - half
    sent = gproj_ref.shape[1]

    def fill(first, second):
        first[...] = gqkv_s[:, :half]
        second[:, :tail] = gqkv_s[:, half:]
        second[:, tail : tail + width] = go_s[...]
        second[:, tail + width : tail + width + sent] = gproj_ref[...]
        end = tail + width + sent
        second[:, end : end + LANES] = columns_of_vectors(gvec_ref[...])
        second[:, end + LANES :] = jnp.zeros((width, half - end - LANES), BF16)

    by_core(core_ref, fill, keep_ref, give_ref)


FEED_CHUNK = 512


def whole_call(kernel, args, outs, scratch, name, flops, steps=1):
    arrays, specs = [], []

    def block(shape, at):
        if callable(at):
            return pl.BlockSpec(shape, at)
        index = (0,) * (len(shape) - 1) + (at,)
        return pl.BlockSpec(shape, lambda i: index, pipeline_mode=pl.Buffered(1))

    for arg in args:
        array, shape, at = arg if isinstance(arg, tuple) else (arg, arg.shape, 0)
        arrays.append(array)
        specs.append(pl.BlockSpec(memory_space=pltpu.SMEM) if len(shape) == 1 else block(shape, at))
    out_specs, shapes = [], []
    for out in outs:
        shape, dtype, part, at = out if len(out) == 4 else out + (out[0], 0)
        out_specs.append(block(part, at))
        shapes.append(jax.ShapeDtypeStruct(shape, dtype))
    return pl.pallas_call(
        kernel,
        grid=(steps,),
        in_specs=specs,
        out_specs=out_specs,
        out_shape=shapes,
        scratch_shapes=[pltpu.VMEM(s, d) for s, d in scratch],
        compiler_params=pltpu.CompilerParams(
            dimension_semantics=("arbitrary",), vmem_limit_bytes=VMEM_BYTES
        ),
        cost_estimate=pl.CostEstimate(flops=flops, bytes_accessed=16 << 20, transcendentals=0),
        name=name,
    )(*arrays)


def enc_blocks(pack, width, ff, sent):
    up = 4 * width // FEED_CHUNK
    return (
        (pack, (width, 3 * width), 0),
        (pack, (width, width), 3),
        (pack, (width, FEED_CHUNK), lambda i: (0, up + i)),
        (pack, (width, sent), (4 * width + ff) // sent),
        (pack, (width, LANES), (4 * width + ff + sent) // LANES),
    )


def enc_attend(x, mask, blocks):
    clips, slots, width = x.shape
    m = clips * slots
    outs = [
        ((m, 3 * width), BF16),
        ((m, HEADS_ENC * slots), BF16),
        ((m, width), BF16),
        ((m, width), F32),
        ((8, width), F32),
    ]
    qkv, out, _, _, small = blocks
    return whole_call(enc_attend_kernel, (x, mask, small, qkv, out), outs, [], "enc_attend", 10**10)


def enc_feed(x2, vecs, blocks, wd):
    m, width = x2.shape
    ff, chunk = wd.shape[0], FEED_CHUNK
    _, _, up, proj, _ = blocks
    across, down = lambda i: (0, i), lambda i: (i, 0)
    kept = ((m, ff), BF16, (m, chunk), across)
    outs = [((m, proj[1][1]), BF16), ((m, width), BF16), kept, kept]
    scratch = [((m, width), BF16), ((m, width), F32)]
    args = (x2, vecs, up, (wd, (chunk, width), down), proj)
    return whole_call(enc_feed_kernel, args, outs, scratch, "enc_feed", 14 * 10**9, ff // chunk)


def enc_feed_back(core, dsent, enc, h, gp, x2, vecs, blocks, wd):
    m, width = x2.shape
    ff, chunk = wd.shape[0], FEED_CHUNK
    _, _, up, proj, _ = blocks
    across, down = lambda i: (0, i), lambda i: (i, 0)
    half = ((width, ff), BF16, (width, chunk), across)
    outs = [(proj[1], BF16), half, half, ((m, width), F32), ((8, width), F32)]
    scratch = [((width, m), BF16), ((m, width), BF16), ((width, m), BF16), ((m, width), F32)]
    args = (core, dsent, enc, proj, (h, (m, chunk), across), (gp, (m, chunk), across), x2, vecs, up)
    args += ((wd, (chunk, width), down),)
    return whole_call(
        enc_feed_back_kernel, args, outs, scratch, "enc_feed_back", 18 * 10**9, ff // chunk
    )


def attend_half(width, sent):
    blocks = (4 * width + sent + LANES) // LANES
    return (blocks + 1) // 2 * LANES


def enc_attend_back(core, dx2, o, qkv, p, x, vecs, blocks, gproj, gvec):
    m, width = dx2.shape
    w_qkv, w_out, _, _, _ = blocks
    half = (width, attend_half(width, gproj.shape[1]))
    outs = [(half, BF16), (half, BF16), (x.shape, BF16)]
    scratch = [
        ((8, width), F32),
        ((m, width), BF16),
        ((m, 3 * width), BF16),
        ((width, 3 * width), BF16),
        ((width, width), BF16),
    ]
    args = (core, dx2, o, qkv, p, x, vecs, w_qkv, w_out, gproj, gvec)
    return whole_call(enc_attend_back_kernel, args, outs, scratch, "enc_attend_back", 14 * 10**9)


def unpack_kernel(sections, pieces, talls, smalls, packed_ref, *out_refs):
    chips, _, unit, _ = packed_ref.shape

    def read(place, start, size):
        at, part = place
        first, width, count = sections[at]
        blocks = [
            packed_ref[:, part, :, first + k * width + start : first + k * width + start + size]
            for k in range(count)
        ]
        block = blocks[0] if count == 1 else jnp.concatenate(blocks, axis=1)
        return block.reshape(chips * unit * count, size).astype(F32)

    for out, to, place, start, size in pieces:
        out_refs[out][:, to : to + size] = read(place, start, size)
    chunk = 512
    for out, place, start, size in talls:
        for c in range(size // chunk):
            rows = slice(c * chunk, (c + 1) * chunk)
            out_refs[out][rows, :] = read(place, start + c * chunk, chunk).T
    for out, place, start in smalls:
        out_refs[out][...] = read(place, start, LANES).T[0:8, :]


def even_units(packed, sections):
    parts = []
    for first, width, count in sections:
        chips, two, unit, _ = packed.shape
        part = packed[..., first : first + width * count].reshape(chips, two, unit, count, width)
        part = part.transpose(1, 0, 3, 2, 4).reshape(two, 16, count, chips * unit // 16, width)
        parts.append(part.transpose(1, 0, 3, 2, 4).reshape(16, two, chips * unit // 16, count * width))
    return jnp.concatenate(parts, axis=-1)


def unpack_sums(packed, sections, outs, pieces, talls, smalls):
    if packed.shape[2] % 16:
        packed = even_units(packed, sections)
    chips, _, unit, wide = packed.shape
    group = 8
    specs, shapes = [], []
    for at, width, turned in outs:
        step = group * unit * sections[at][2]
        height = chips * unit * sections[at][2]
        if turned:
            specs.append(pl.BlockSpec((turned, step), lambda i: (0, i)))
            shapes.append(jax.ShapeDtypeStruct((turned, height), F32))
        else:
            specs.append(pl.BlockSpec((step, width), lambda i: (i, 0)))
            shapes.append(jax.ShapeDtypeStruct((height, width), F32))
    return pl.pallas_call(
        functools.partial(unpack_kernel, sections, pieces, talls, smalls),
        grid=(chips // group,),
        in_specs=[pl.BlockSpec((group, 2, unit, wide), lambda i: (i, 0, 0, 0))],
        out_specs=specs,
        out_shape=shapes,
        compiler_params=pltpu.CompilerParams(vmem_limit_bytes=VMEM_BYTES),
        cost_estimate=pl.CostEstimate(
            flops=0, bytes_accessed=12 * chips * unit * wide, transcendentals=0
        ),
        name="unpack_sums",
    )(packed)


AXES = ("clip", "band")


def partner_pairs(total, mask):
    return [(i, i ^ mask) for i in range(total)]


def add_low(*parts):
    return sum(part.astype(F32) for part in parts).astype(BF16)


class RunningSum:
    def __init__(self, keep, give, total):
        bits = total.bit_length() - 1
        self.total = total
        self.cut = keep.shape[1] // 256 * 128
        rows = keep.shape[0] // (total // 2)
        self.shape = (2,) * (bits - 1) + (rows, keep.shape[1])
        self.keep = [keep]
        self.got = [lax.ppermute(give, AXES, partner_pairs(total, 1))]
        self.left = [list(range(bits - 1, 0, -1))]
        self.plan = [[[2], [1]], [[1], [2]]]
        rest = list(range(3, bits))
        while rest:
            self.plan.append([rest[:2]])
            rest = rest[2:]

    def settle(self):
        each = len(self.got) // len(self.keep)
        self.held = [
            add_low(keep, *self.got[i * each : (i + 1) * each]) for i, keep in enumerate(self.keep)
        ]
        if self.shape:
            self.held, self.shape = [self.held[0].reshape(self.shape)], None

    def offers(self):
        self.settle()
        me = lax.axis_index(AXES)
        groups = self.plan[0]
        if len(groups) > len(self.held):
            (held,), (left,) = self.held, self.left
            self.held = [held[..., : self.cut], held[..., self.cut :]]
            self.left = [list(left), list(left)]
        if len(groups) < len(self.held):
            self.held = [jnp.concatenate(self.held, axis=-1)]
            self.left = self.left[:1]
        self.keep, gives, self.masks = [], [], []
        for held, left, group in zip(self.held, self.left, groups):
            low, ways = group[0], 1 << len(group)
            place = left.index(group[-1])
            mine = (me >> low) & (ways - 1)
            shape = held.shape
            held = held.reshape(shape[:place] + (ways,) + shape[place + len(group) :])
            self.keep.append(lax.dynamic_index_in_dim(held, mine, place, keepdims=False))
            for k in range(1, ways):
                gives.append(lax.dynamic_index_in_dim(held, mine ^ k, place, keepdims=False))
                self.masks.append(k << low)
            for bit in group:
                left.remove(bit)
        return gives

    def deliver(self, gives):
        self.got = [
            lax.ppermute(give, AXES, partner_pairs(self.total, mask))
            for give, mask in zip(gives, self.masks)
        ]
        self.plan = self.plan[1:]

    def finish(self):
        while self.plan:
            self.deliver(self.offers())
        self.settle()
        return jnp.concatenate(self.held, axis=-1)


class RunningGather:
    def __init__(self, shard, total):
        bits = total.bit_length() - 1
        self.total = total
        self.cut = (shard.shape[1] + LANES) // 256 * 128
        self.shape = shard.shape
        rest, self.plan = list(range(3, bits)), []
        while rest:
            self.plan.append([rest[:2]])
            rest = rest[2:]
        self.plan += [[[1], [2]], [[2], [1]], [[0]]]
        self.held, self.have = [shard], [[]]

    def offers(self):
        groups = self.plan[0]
        if len(groups) > len(self.held):
            (held,), (have,) = self.held, self.have
            self.held = [held[..., : self.cut], held[..., self.cut :]]
            self.have = [list(have), list(have)]
        if len(groups) < len(self.held):
            self.held = [jnp.concatenate(self.held, axis=-1)]
            self.have = self.have[:1]
        gives, self.masks = [], []
        for held, group in zip(self.held, groups):
            for k in range(1, 1 << len(group)):
                gives.append(held)
                self.masks.append(k << group[0])
        return gives

    def deliver(self, gives):
        me = lax.axis_index(AXES)
        got = [
            lax.ppermute(give, AXES, partner_pairs(self.total, mask))
            for give, mask in zip(gives, self.masks)
        ]
        each = len(got) // len(self.held)
        for i, group in enumerate(self.plan[0]):
            parts = [self.held[i]] + got[i * each : (i + 1) * each]
            for b, bit in enumerate(group):
                flip = ((me >> bit) & 1) == 1
                parts = [jnp.where(flip, parts[k ^ (1 << b)], part) for k, part in enumerate(parts)]
            self.have[i] = sorted(self.have[i] + group, reverse=True)
            at = self.have[i].index(group[-1])
            held = jnp.stack(parts, axis=at)
            self.held[i] = held.reshape(held.shape[:at] + (2,) * len(group) + held.shape[at + 1 :])
        self.plan = self.plan[1:]

    def finish(self):
        while self.plan:
            self.deliver(self.offers())
        return self.held[0].reshape((self.total,) + self.shape)


def together(*groups):
    return lax.optimization_barrier(groups)


def gather_rows(shard):
    return lax.all_gather(shard, AXES, axis=0, tiled=True)


def columns_of(vectors):
    block = jnp.stack(vectors, axis=1)
    return jnp.pad(block, ((0, 0), (0, LANES - len(vectors))))


def blocks_beside(tall, rows):
    return [tall[i : i + rows] for i in range(0, tall.shape[0], rows)]


def blocks_below(beside, total, width):
    rows = beside.shape[0] // total
    count = beside.shape[1] // width
    parts = [beside[:, i * width : (i + 1) * width].reshape(total, rows, width) for i in range(count)]
    return jnp.concatenate(parts, axis=1)


def swap_band(array, bit):
    return lax.ppermute(array, "band", [(i, i ^ bit) for i in range(4)])


def owners_to_bands(array):
    band = lax.axis_index("band")
    half, side = band // 2, band % 2
    own = lax.dynamic_index_in_dim(array, half, 0, keepdims=False)
    got = swap_band(lax.dynamic_index_in_dim(array, 1 - half, 0, keepdims=False), 2)
    pair = jnp.stack([jnp.where(half == 0, own, got), jnp.where(half == 0, got, own)])
    other = swap_band(pair, 1)
    return jnp.stack([jnp.where(side == 0, pair, other), jnp.where(side == 0, other, pair)], axis=1)


def join_bands(array):
    side = lax.axis_index("band") % 2
    own = lax.dynamic_index_in_dim(array, side, 1, keepdims=False)
    return own + swap_band(lax.dynamic_index_in_dim(array, 1 - side, 1, keepdims=False), 1)


def bands_to_owners(pair):
    half = lax.axis_index("band") // 2
    own = lax.dynamic_index_in_dim(pair, half, 0, keepdims=False)
    got = swap_band(lax.dynamic_index_in_dim(pair, 1 - half, 0, keepdims=False), 2)
    return jnp.stack([jnp.where(half == 0, own, got), jnp.where(half == 0, got, own)])


def position_table(places):
    half_width = D_DEC // 2
    omega_vec = jnp.exp(
        jnp.arange(half_width, dtype=F32) * (-math.log(10000.0) / half_width)
    )
    angles = places.astype(F32)[..., None] * omega_vec
    return jnp.concatenate([jnp.sin(angles), jnp.cos(angles)], axis=-1)


def shards(
    visible,
    keep_index,
    visible_count,
    enc_gain1,
    enc_shift1,
    enc_qkv,
    enc_out,
    enc_gain2,
    enc_shift2,
    enc_up,
    enc_down,
    proj,
    mask_token,
    dec_gain1,
    dec_shift1,
    dec_qkv,
    dec_out,
    dec_gain2,
    dec_shift2,
    dec_up,
    dec_down,
    cotangent,
):
    total = lax.axis_size(AXES)
    enc_wide, dec_wide = enc_out.shape[1], dec_out.shape[1]
    enc_ff, dec_ff = enc_up.shape[1], dec_up.shape[1]
    core = (lax.axis_index(AXES) % 2).reshape(1)
    enc_small = columns_of([enc_gain1, enc_shift1, enc_gain2, enc_shift2])
    enc_pack = gather_rows(jnp.concatenate([enc_qkv, enc_out, enc_up, proj, enc_small], axis=1))
    down_run = RunningGather(enc_down, total)
    while len(down_run.plan) > 3:
        down_run.deliver(down_run.offers())

    clip_count, slot_total, _ = visible.shape
    half_clips = clip_count // 2
    band_height = FREQ // 2
    slot_ids = jnp.arange(slot_total)
    valid_rows = slot_ids[None, :] < visible_count[:, None]
    valid_mask = valid_rows.astype(F32)[:, None, :]
    cell_number = jnp.where(valid_rows, keep_index, -1).reshape(2, half_clips, slot_total)
    cell_number = owners_to_bands(cell_number).reshape(-1, slot_total)

    dec_small = columns_of([dec_gain1, dec_shift1, dec_gain2, dec_shift2, mask_token])
    dec_tall = blocks_beside(dec_down, dec_out.shape[0])
    dec_pack = jnp.concatenate([dec_qkv, dec_out, dec_up] + dec_tall + [dec_small], axis=1)
    dec_run = RunningGather(dec_pack, total)
    cell_number, gives, dec_gives = together(cell_number, down_run.offers(), dec_run.offers())
    down_run.deliver(gives)
    dec_run.deliver(dec_gives)
    while len(dec_run.plan) > 3:
        dec_run.deliver(dec_run.offers())
    down_run.deliver(down_run.offers())
    gives, dec_gives = together(down_run.offers(), dec_run.offers())
    down_run.deliver(gives)
    dec_run.deliver(dec_gives)
    whole_down = down_run.finish().reshape(-1, enc_wide)
    enc_pack, whole_down, gives = together(enc_pack, whole_down, dec_run.offers())
    dec_run.deliver(gives)

    band_pick = lax.axis_index("band") % 2
    rolled_time = (cell_number // FREQ + TIME - SHIFT) % TIME
    rolled_freq = (cell_number % FREQ + FREQ - SHIFT) % FREQ
    here = (cell_number >= 0) & (rolled_freq // band_height == band_pick)
    arrived_index = jnp.where(here, rolled_time * band_height + rolled_freq % band_height, -1)

    blocks = enc_blocks(enc_pack, enc_wide, enc_ff, dec_wide)
    qkv, probs, mixed, middle, vecs = enc_attend(visible, valid_mask, blocks)
    sent_rows, encoded, hidden, slope = enc_feed(middle, vecs, blocks, whole_down)
    sent_rows, gives = together(sent_rows, dec_run.offers())
    dec_run.deliver(gives)
    dec_pack = dec_run.finish().reshape(-1, dec_pack.shape[1])
    dec_end = 4 * dec_wide + dec_ff
    dec_whole_down = blocks_below(dec_pack[:, dec_end : dec_end + dec_ff], total, dec_wide)
    dec_whole_down = dec_whole_down.reshape(-1, dec_wide)
    arrived_rows = owners_to_bands(sent_rows.reshape(2, half_clips, slot_total, dec_wide))
    half_total = 4 * half_clips

    cell_count = TIME * band_height
    places = jnp.arange(cell_count)
    cell_freq = band_pick * band_height + places % band_height
    patch_number = (places // band_height + SHIFT) % TIME * FREQ + (cell_freq + SHIFT) % FREQ
    span = D_DEC // HEADS_DEC
    query = places[:, None]
    key = query // span * span + jnp.arange(LANES)[None, :] % span

    def label(cell):
        late = cell // band_height >= TIME - SHIFT
        high = band_pick * band_height + cell % band_height >= FREQ - SHIFT
        return late.astype(jnp.int32) * 2 + high.astype(jnp.int32)

    cells_in = WINDOW * WINDOW
    allowed = (query // cells_in == key // cells_in) & (label(query) == label(key))
    decoded, returning, keep, give = decoder_block(
        core,
        arrived_rows.reshape(half_total, slot_total, dec_wide),
        arrived_index,
        cotangent.reshape(half_total, cell_count, dec_wide),
        position_table(patch_number),
        allowed.astype(F32),
        dec_pack,
        dec_whole_down,
    )
    decoded_out = decoded.reshape(cotangent.shape)

    returning = join_bands(returning.reshape(2, 2, half_clips, slot_total, dec_wide))
    returning, keep, give = together(returning, keep, give)
    dec_run = RunningSum(keep, give, total)
    grad_sent = bands_to_owners(returning).reshape(-1, dec_wide)
    grad_sent, gives = together(grad_sent, dec_run.offers())
    dec_run.deliver(gives)
    g_proj, keep, give, grad_middle, g_vec = enc_feed_back(
        core, grad_sent, encoded, hidden, slope, middle, vecs, blocks, whole_down
    )
    keep, give, grad_middle, gives = together(keep, give, grad_middle, dec_run.offers())
    dec_run.deliver(gives)
    feed_run = RunningSum(keep, give, total)
    keep, give, grad_visible = enc_attend_back(
        core, grad_middle, mixed, qkv, probs, visible, vecs, blocks, g_proj, g_vec
    )
    keep, give, dec_run.got, feed_run.got = together(keep, give, dec_run.got, feed_run.got)
    attend_run = RunningSum(keep, give, total)
    feed_gives, dec_run.got, attend_run.got = together(
        feed_run.offers(), dec_run.got, attend_run.got
    )
    feed_run.deliver(feed_gives)
    dec_run.deliver(dec_run.offers())
    dec_shard, feed_gives = together(dec_run.finish(), feed_run.offers())
    feed_run.deliver(feed_gives)
    feed_gives, gives = together(feed_run.offers(), attend_run.offers())
    feed_run.deliver(feed_gives)
    attend_run.deliver(gives)
    feed_shard = feed_run.finish()
    feed_shard, gives = together(feed_shard, attend_run.offers())
    unit = dec_shard.shape[0] // 2
    dec_units = [dec_shard[k * unit : (k + 1) * unit] for k in range(2)]
    feed_units = [feed_shard[k * unit : (k + 1) * unit] for k in range(3)]
    most_sum = gather_rows(jnp.concatenate(dec_units + feed_units, axis=1))
    attend_run.deliver(gives)
    attend_shard = attend_run.finish()
    attend_sum = RunningGather(attend_shard, total).finish()

    half = attend_shard.shape[1]
    tail = 3 * enc_wide - half
    e_qkv, e_out, e_proj, enc_vecs = unpack_sums(
        attend_sum.reshape((total // 2, 2) + attend_shard.shape),
        ((0, half, 1),),
        ((0, 3 * enc_wide, 0), (0, enc_wide, 0), (0, dec_wide, 0), (0, 0, 8)),
        (
            (0, 0, (0, 0), 0, half),
            (0, half, (0, 1), 0, tail),
            (1, 0, (0, 1), tail, enc_wide),
            (2, 0, (0, 1), tail + enc_wide, dec_wide),
        ),
        (),
        ((3, (0, 1), tail + enc_wide + dec_wide),),
    )
    half = dec_ff // 2
    dec_half = dec_shard.shape[1]
    d_qkv, d_out, d_up, d_down, dec_vecs, e_up, e_down = unpack_sums(
        most_sum.reshape(total // 2, 2, unit, most_sum.shape[1]),
        ((0, dec_half, 2), (2 * dec_half, enc_ff, 3)),
        (
            (0, 3 * dec_wide, 0),
            (0, dec_wide, 0),
            (0, dec_ff, 0),
            (0, 0, dec_ff),
            (0, 0, 8),
            (1, enc_ff, 0),
            (1, 0, enc_ff),
        ),
        (
            (0, 0, (0, 0), 0, 3 * dec_wide),
            (1, 0, (0, 0), 3 * dec_wide, dec_wide),
            (2, 0, (0, 0), 4 * dec_wide, half),
            (2, half, (0, 1), 0, half),
            (5, 0, (1, 0), 0, enc_ff),
        ),
        ((3, (0, 1), half, dec_ff), (6, (1, 1), 0, enc_ff)),
        ((4, (0, 0), 4 * dec_wide + half),),
    )
    return (
        decoded_out,
        grad_visible,
        enc_vecs[0],
        enc_vecs[1],
        e_qkv,
        e_out,
        enc_vecs[2],
        enc_vecs[3],
        e_up,
        e_down,
        e_proj,
        dec_vecs[4],
        dec_vecs[0],
        dec_vecs[1],
        d_qkv,
        d_out,
        dec_vecs[2],
        dec_vecs[3],
        d_up,
        d_down,
    )


def solution(mesh):
    return jax.shard_map(
        shards,
        mesh=mesh,
        in_specs=(
            P(("clip", "band"), None, None),
            P(("clip", "band"), None),
            P(("clip", "band")),
            P(("clip", "band")),
            P(("clip", "band")),
            P(("clip", "band"), None),
            P(("clip", "band"), None),
            P(("clip", "band")),
            P(("clip", "band")),
            P(("clip", "band"), None),
            P(("clip", "band"), None),
            P(("clip", "band"), None),
            P(("clip", "band")),
            P(("clip", "band")),
            P(("clip", "band")),
            P(("clip", "band"), None),
            P(("clip", "band"), None),
            P(("clip", "band")),
            P(("clip", "band")),
            P(("clip", "band"), None),
            P(("clip", "band"), None),
            P(("clip", "band"), None, None, None, None),
        ),
        out_specs=(
            P(("clip", "band"), None, None, None, None),
            P(("clip", "band"), None, None),
            P(),
            P(),
            P(),
            P(),
            P(),
            P(),
            P(),
            P(),
            P(),
            P(),
            P(),
            P(),
            P(),
            P(),
            P(),
            P(),
            P(),
            P(),
        ),
        check_vma=False,
    )
```

```python
import functools
import math

import jax
import jax.numpy as jnp
from jax import lax
from jax.experimental import pallas as pl
from jax.experimental.pallas import tpu as pltpu
from jax.sharding import PartitionSpec as P

HEADS_ENC = 12
D_DEC = 512
HEADS_DEC = 16
TIME = 64
FREQ = 8
WINDOW = 4
SHIFT = 2
norm_eps = 1e-06
neg_fill = -1e30
F32 = jnp.float32
BF16 = jnp.bfloat16
LANES = 128
VMEM_BYTES = 58 * 1024 * 1024


def mm(a, b):
    return lax.dot_general(a, b, (((1,), (0,)), ((), ())), preferred_element_type=F32)


def mm_t(a, b):
    return lax.dot_general(a, b, (((1,), (1,)), ((), ())), preferred_element_type=F32)


def bmm(a, b):
    return lax.dot_general(a, b, (((2,), (1,)), ((0,), (0,))), preferred_element_type=F32)


def bmm_t(a, b):
    return lax.dot_general(a, b, (((2,), (2,)), ((0,), (0,))), preferred_element_type=F32)


def bmm_l(a, b):
    return lax.dot_general(a, b, (((1,), (1,)), ((0,), (0,))), preferred_element_type=F32)


def normalise(x):
    centre = jnp.mean(x, axis=-1, keepdims=True)
    centred = x - centre
    rstd = lax.rsqrt(jnp.mean(centred * centred, axis=-1, keepdims=True) + norm_eps)
    return centred * rstd, rstd


def norm_back(da, xhat, rstd, gain):
    dag = da * gain
    return rstd * (
        dag
        - jnp.mean(dag, axis=-1, keepdims=True)
        - xhat * jnp.mean(dag * xhat, axis=-1, keepdims=True)
    )


def gelu_parts(u):
    size = jnp.abs(u) * 0.7071067811865476
    bell = jnp.exp(-0.5 * u * u)
    t = 1.0 / (1.0 + 0.3275911 * size)
    poly = 0.530702715
    poly = poly * t - 0.726576013
    poly = poly * t + 0.710706871
    poly = poly * t - 0.142248368
    poly = poly * t + 0.127414796
    tail = poly * t * bell
    cdf = jnp.where(u >= 0, 1.0 - tail, tail)
    return cdf, u * bell * 0.3989422804014327


def vectors_of(small_ref):
    return small_ref[...].astype(F32).T[0:8, :]


def columns_of_vectors(vectors):
    count, width = vectors.shape
    block = jnp.concatenate([vectors, jnp.zeros((LANES - count, width), F32)], axis=0)
    return block.T.astype(BF16)


def by_core(core_ref, fill, keep_ref, give_ref):
    @pl.when(core_ref[0] == 0)
    def _():
        fill(keep_ref, give_ref)

    @pl.when(core_ref[0] != 0)
    def _():
        fill(give_ref, keep_ref)


def segment_sum(x, ones):
    return mm(x.astype(BF16), ones)


def window_max(s):
    ahead = s
    behind = s
    for step in (1, 2, 4, 8):
        ahead = jnp.maximum(ahead, pltpu.roll(ahead, step, 1))
        behind = jnp.maximum(behind, pltpu.roll(behind, LANES - step, 1))
    return jnp.maximum(ahead, behind)


def decoder_kernel(
    core_ref, rows_ref, idx_ref, cot_ref, pos_ref, mask_ref, small_ref, wqkv_ref, wo_ref, wu_ref, wd_ref,
    out_ref, own_ref, other_ref, keep_ref, give_ref,
    acc_qkv, acc_o, acc_u, acc_d, gvec_ref, vec_ref,
    x_s, qkv_s, p_s, o_s, a2_s, a2t_s, dzt_s, da_s, y_s, dqkv_s,
):
    step = pl.program_id(0)
    last = pl.num_programs(0) - 1
    halves, cells, width = cot_ref.shape
    m_rows = halves * cells
    slots = rows_ref.shape[1]
    head_dim = width // HEADS_DEC
    heads_in = LANES // head_dim
    groups = width // LANES
    block = LANES // heads_in
    blocks = m_rows // block
    scale = head_dim ** (-0.5)
    ff = wu_ref.shape[1]
    chunk = 512

    @pl.when(step == 0)
    def _():
        acc_qkv[...] = jnp.zeros_like(acc_qkv)
        acc_o[...] = jnp.zeros_like(acc_o)
        acc_u[...] = jnp.zeros_like(acc_u)
        acc_d[...] = jnp.zeros_like(acc_d)
        gvec_ref[...] = jnp.zeros_like(gvec_ref)
        vec_ref[...] = vectors_of(small_ref)

    gain1, shift1 = vec_ref[0:1, :], vec_ref[1:2, :]
    gain2, shift2 = vec_ref[2:3, :], vec_ref[3:4, :]
    token = vec_ref[4:5, :]

    def place_of(h):
        cell = lax.broadcasted_iota(jnp.int32, (cells, slots), 0)
        return cell == idx_ref[h]

    unseen = []
    for h in range(halves):
        place = place_of(h)
        unseen_h = 1.0 - jnp.sum(place.astype(F32), axis=1, keepdims=True)
        unseen.append(unseen_h)
        x_s[h * cells : (h + 1) * cells, :] = (
            mm(place.astype(BF16), rows_ref[h]) + unseen_h * token + pos_ref[...]
        )
    xhat1, rstd1 = normalise(x_s[...])
    a1 = (xhat1 * gain1 + shift1).astype(BF16)
    qkv_s[...] = mm(a1, wqkv_ref[...]).astype(BF16)

    lane = lax.broadcasted_iota(jnp.int32, (1, LANES), 1)
    head_masks = [(lane // head_dim == h) for h in range(heads_in)]
    ones = (
        lax.broadcasted_iota(jnp.int32, (LANES, LANES), 0) // block
        == lax.broadcasted_iota(jnp.int32, (LANES, LANES), 1) // block
    ).astype(BF16)

    def spread(t):
        parts = [t * hm.astype(BF16)[None] for hm in head_masks]
        return jnp.concatenate(parts, axis=1)

    def fold(t):
        out = t[:, 0:block, :]
        for h in range(1, heads_in):
            out = jnp.where(head_masks[h][None], t[:, h * block : (h + 1) * block, :], out)
        return out

    def part(ref, base, g):
        return ref[:, base + g * LANES : base + (g + 1) * LANES].reshape(blocks, block, LANES)

    allowed = jnp.concatenate([mask_ref[...]] * halves, axis=0) > 0.5
    for g in range(groups):
        q3 = part(qkv_s, 0, g)
        k3 = spread(part(qkv_s, width, g))
        v3 = spread(part(qkv_s, 2 * width, g))
        s = bmm_t(q3, k3).reshape(m_rows, LANES) * scale
        s = jnp.where(allowed, s, neg_fill)
        e = jnp.where(allowed, jnp.exp(s - window_max(s)), 0.0)
        p = e / segment_sum(e, ones)
        p_s[:, g * LANES : (g + 1) * LANES] = p
        o = bmm(p.astype(BF16).reshape(blocks, block, LANES), v3)
        o_s[:, g * LANES : (g + 1) * LANES] = o.reshape(m_rows, LANES).astype(BF16)

    x2 = x_s[...] + mm(o_s[...], wo_ref[...])
    xhat2, rstd2 = normalise(x2)
    a2 = (xhat2 * gain2 + shift2).astype(BF16)
    a2_s[...] = a2
    a2t_s[...] = a2.T
    dz = cot_ref[...].reshape(m_rows, width)
    dzt_s[...] = dz.T
    y_s[...] = x2
    da_s[...] = jnp.zeros_like(da_s)

    for c in range(ff // chunk):
        at = slice(c * chunk, (c + 1) * chunk)
        u = mm(a2_s[...], wu_ref[:, at])
        dh = mm_t(cot_ref[...].reshape(m_rows, width), wd_ref[at, :])
        cdf, bump = gelu_parts(u)
        h = (u * cdf).astype(BF16)
        du = ((cdf + bump) * dh).astype(BF16)
        y_s[...] += mm(h, wd_ref[at, :])
        acc_d[:, at] += mm(dzt_s[...], h)
        acc_u[:, at] += mm(a2t_s[...], du)
        da_s[...] += mm_t(du, wu_ref[:, at])

    out_ref[...] = y_s[...].reshape(halves, cells, width).astype(BF16)
    da2 = da_s[...]
    gvec_ref[2:3, :] += jnp.sum(da2 * xhat2, axis=0, keepdims=True)
    gvec_ref[3:4, :] += jnp.sum(da2, axis=0, keepdims=True)
    dx2 = cot_ref[...].reshape(m_rows, width).astype(F32) + norm_back(da2, xhat2, rstd2, gain2)
    dy2 = dx2.astype(BF16)
    acc_o[...] += mm(o_s[...].T, dy2)
    do = mm_t(dy2, wo_ref[...]).astype(BF16)

    for g in range(groups):
        cols = slice(g * LANES, (g + 1) * LANES)
        q3 = part(qkv_s, 0, g)
        k3 = spread(part(qkv_s, width, g))
        v3 = spread(part(qkv_s, 2 * width, g))
        do3 = do[:, cols].reshape(blocks, block, LANES)
        p = p_s[:, cols]
        dp = bmm_t(do3, v3).reshape(m_rows, LANES)
        draw = (p * (dp - segment_sum(p * dp, ones)) * scale).astype(BF16)
        draw3 = draw.reshape(blocks, block, LANES)
        dq = bmm(draw3, k3).reshape(m_rows, LANES)
        dk = fold(bmm_l(draw3, q3)).reshape(m_rows, LANES)
        dv = fold(bmm_l(p.astype(BF16).reshape(blocks, block, LANES), do3)).reshape(m_rows, LANES)
        dqkv_s[:, g * LANES : (g + 1) * LANES] = dq.astype(BF16)
        dqkv_s[:, width + g * LANES : width + (g + 1) * LANES] = dk.astype(BF16)
        dqkv_s[:, 2 * width + g * LANES : 2 * width + (g + 1) * LANES] = dv.astype(BF16)

    xhat1, rstd1 = normalise(x_s[...])
    a1 = (xhat1 * gain1 + shift1).astype(BF16)
    dqkv = dqkv_s[...]
    acc_qkv[...] += mm(a1.T, dqkv)
    da1 = mm_t(dqkv, wqkv_ref[...])
    gvec_ref[0:1, :] += jnp.sum(da1 * xhat1, axis=0, keepdims=True)
    gvec_ref[1:2, :] += jnp.sum(da1, axis=0, keepdims=True)
    dx = dx2 + norm_back(da1, xhat1, rstd1, gain1)
    for h in range(halves):
        dx_h = dx[h * cells : (h + 1) * cells, :]
        gvec_ref[4:5, :] += jnp.sum(unseen[h] * dx_h, axis=0, keepdims=True)
        place = place_of(h).astype(F32).T.astype(BF16)
        back = mm(place, dx_h.astype(BF16)).astype(BF16)
        ours = core_ref[0] == lax.rem(step, 2)

        @pl.when(ours)
        def _(back=back, h=h):
            own_ref[h] = back

        @pl.when(jnp.logical_not(ours))
        def _(back=back, h=h):
            other_ref[h] = back

    @pl.when(step == last)
    def _():
        half = ff // 2

        def fill(first, second):
            first[:, : 3 * width] = acc_qkv[...].astype(BF16)
            first[:, 3 * width : 4 * width] = acc_o[...].astype(BF16)
            first[:, 4 * width : 4 * width + half] = acc_u[:, :half].astype(BF16)
            first[:, 4 * width + half :] = columns_of_vectors(gvec_ref[...])
            second[:, :half] = acc_u[:, half:].astype(BF16)
            second[:, half : half + ff] = acc_d[...].astype(BF16)
            second[:, half + ff :] = jnp.zeros((width, second.shape[1] - half - ff), BF16)

        by_core(core_ref, fill, keep_ref, give_ref)


def decoder_block(core, rows, idx, cot, pos, mask, pack, wd):
    n_half, slots, width = rows.shape
    cells = cot.shape[1]
    ff = wd.shape[0]
    halves = 2
    m_rows = halves * cells
    half_wide = 4 * width + ff // 2 + LANES
    vm = pltpu.VMEM
    flops = 6 * n_half * cells * (4 * width + 2 * ff) * width * 2

    def whole(*shape, at=0):
        index = (0,) * (len(shape) - 1) + (at,)
        return pl.BlockSpec(shape, lambda i: index, pipeline_mode=pl.Buffered(1))

    return pl.pallas_call(
        decoder_kernel,
        grid=(n_half // halves,),
        in_specs=[
            pl.BlockSpec(memory_space=pltpu.SMEM),
            pl.BlockSpec((halves, slots, width), lambda i: (i, 0, 0)),
            pl.BlockSpec((halves, 1, slots), lambda i: (i, 0, 0)),
            pl.BlockSpec((halves, cells, width), lambda i: (i, 0, 0)),
            whole(cells, width),
            whole(cells, LANES),
            whole(width, LANES, at=(4 * width + 2 * ff) // LANES),
            whole(width, 3 * width),
            whole(width, width, at=3),
            whole(width, ff, at=1),
            whole(ff, width),
        ],
        out_specs=[
            pl.BlockSpec((halves, cells, width), lambda i: (i, 0, 0)),
            pl.BlockSpec((halves, slots, width), lambda i: (i // 2, 0, 0)),
            pl.BlockSpec((halves, slots, width), lambda i: (i // 2, 0, 0)),
            whole(width, half_wide),
            whole(width, half_wide),
        ],
        out_shape=[
            jax.ShapeDtypeStruct((n_half, cells, width), BF16),
            jax.ShapeDtypeStruct((n_half // 2, slots, width), BF16),
            jax.ShapeDtypeStruct((n_half // 2, slots, width), BF16),
            jax.ShapeDtypeStruct((width, half_wide), BF16),
            jax.ShapeDtypeStruct((width, half_wide), BF16),
        ],
        scratch_shapes=[
            vm((width, 3 * width), F32),
            vm((width, width), F32),
            vm((width, ff), F32),
            vm((width, ff), F32),
            vm((8, width), F32),
            vm((8, width), F32),
            vm((m_rows, width), F32),
            vm((m_rows, 3 * width), BF16),
            vm((m_rows, width), F32),
            vm((m_rows, width), BF16),
            vm((m_rows, width), BF16),
            vm((width, m_rows), BF16),
            vm((width, m_rows), BF16),
            vm((m_rows, width), F32),
            vm((m_rows, width), F32),
            vm((m_rows, 3 * width), BF16),
        ],
        compiler_params=pltpu.CompilerParams(
            dimension_semantics=("arbitrary",), vmem_limit_bytes=VMEM_BYTES
        ),
        cost_estimate=pl.CostEstimate(flops=flops, bytes_accessed=40 << 20, transcendentals=0),
        name="decoder_block",
    )(
        core, rows, idx.reshape(n_half, 1, slots), cot, pos, mask,
        pack, pack, pack, pack, wd,
    )


def enc_spread(t, head_masks):
    return jnp.concatenate([t * hm.astype(BF16)[None] for hm in head_masks], axis=1)


def enc_heads(width):
    head_dim = width // HEADS_ENC
    lane = lax.broadcasted_iota(jnp.int32, (1, LANES), 1)
    return head_dim, [(lane // head_dim == h) for h in range(LANES // head_dim)]


def enc_attend_kernel(
    x_ref, mask_ref, small_ref, wqkv_ref, wo_ref, qkv_ref, p_ref, o_ref, x2_ref, vec_ref
):
    vec_ref[...] = vectors_of(small_ref)
    clips, slots, width = x_ref.shape
    m_rows = clips * slots
    head_dim, head_masks = enc_heads(width)
    scale = head_dim ** (-0.5)
    x = x_ref[...].reshape(m_rows, width).astype(F32)
    xhat, rstd = normalise(x)
    a1 = (xhat * vec_ref[0:1, :] + vec_ref[1:2, :]).astype(BF16)
    qkv_ref[...] = mm(a1, wqkv_ref[...]).astype(BF16)
    allowed = mask_ref[...] > 0.5
    for g in range(width // LANES):
        cols = lambda part: slice(part * width + g * LANES, part * width + (g + 1) * LANES)
        q3 = qkv_ref[:, cols(0)].reshape(clips, slots, LANES)
        k3 = enc_spread(qkv_ref[:, cols(1)].reshape(clips, slots, LANES), head_masks)
        v3 = enc_spread(qkv_ref[:, cols(2)].reshape(clips, slots, LANES), head_masks)
        s = bmm_t(q3, k3) * scale
        for h in range(len(head_masks)):
            sh = jnp.where(allowed, s[:, :, h * slots : (h + 1) * slots], neg_fill)
            e = jnp.exp(sh - jnp.max(sh, axis=-1, keepdims=True))
            e = e / jnp.sum(e, axis=-1, keepdims=True)
            at = (g * len(head_masks) + h) * slots
            p_ref[:, at : at + slots] = e.reshape(m_rows, slots).astype(BF16)
        span = len(head_masks) * slots
        p3 = p_ref[:, g * span : (g + 1) * span].reshape(clips, slots, span)
        o_ref[:, cols(0)] = bmm(p3, v3).reshape(m_rows, LANES).astype(BF16)
    x2_ref[...] = x_ref[...].reshape(m_rows, width).astype(F32) + mm(o_ref[...], wo_ref[...])


def enc_feed_kernel(
    half_ref, x2_ref, vec_ref, wu_ref, wd_ref, proj_ref,
    own_ref, other_ref, enc_ref, h_ref, gp_ref,
    a2_s, y_s,
):
    step = pl.program_id(0)

    @pl.when(step == 0)
    def _():
        xhat, rstd = normalise(x2_ref[...])
        a2_s[...] = (xhat * vec_ref[2:3, :] + vec_ref[3:4, :]).astype(BF16)
        y_s[...] = x2_ref[...]

    u = mm(a2_s[...], wu_ref[...])
    cdf, bump = gelu_parts(u)
    h = (u * cdf).astype(BF16)
    h_ref[...] = h
    gp_ref[...] = (cdf + bump).astype(BF16)
    y_s[...] += mm(h, wd_ref[...])

    @pl.when(step == pl.num_programs(0) - 1)
    def _():
        encoded = y_s[...].astype(BF16)
        enc_ref[...] = encoded
        sent = mm(encoded, proj_ref[...]).astype(BF16)
        rows = own_ref.shape[0]
        first = half_ref[0] == 0
        own_ref[...] = jnp.where(first, sent[:rows], sent[rows:])
        other_ref[...] = jnp.where(first, sent[rows:], sent[:rows])


def enc_feed_back_kernel(
    core_ref, dsent_ref, enc_ref, proj_ref, h_ref, gp_ref, x2_ref, vec_ref, wu_ref, wd_ref,
    gproj_ref, keep_ref, give_ref, dx2_ref, gvec_ref,
    a2t_s, dz_s, dzt_s, da_s,
):
    step = pl.program_id(0)
    gain2 = vec_ref[2:3, :]

    @pl.when(step == 0)
    def _():
        dsent = dsent_ref[...]
        gproj_ref[...] = mm(enc_ref[...].T, dsent).astype(BF16)
        dy = mm_t(dsent, proj_ref[...])
        dx2_ref[...] = dy
        dz = dy.astype(BF16)
        dz_s[...] = dz
        dzt_s[...] = dz.T
        xhat, rstd = normalise(x2_ref[...])
        a2t_s[...] = (xhat * gain2 + vec_ref[3:4, :]).astype(BF16).T
        da_s[...] = jnp.zeros_like(da_s)

    dh = mm_t(dz_s[...], wd_ref[...])
    du = (gp_ref[...].astype(F32) * dh).astype(BF16)
    down_grad = mm(dzt_s[...], h_ref[...]).astype(BF16)
    up_grad = mm(a2t_s[...], du).astype(BF16)
    da_s[...] += mm_t(du, wu_ref[...])
    first = core_ref[0] == 0
    keep_ref[...] = jnp.where(first, up_grad, down_grad)
    give_ref[...] = jnp.where(first, down_grad, up_grad)

    @pl.when(step == pl.num_programs(0) - 1)
    def _():
        da = da_s[...]
        xhat, rstd = normalise(x2_ref[...])
        gvec_ref[...] = jnp.zeros_like(gvec_ref)
        gvec_ref[2:3, :] = jnp.sum(da * xhat, axis=0, keepdims=True)
        gvec_ref[3:4, :] = jnp.sum(da, axis=0, keepdims=True)
        dx2_ref[...] += norm_back(da, xhat, rstd, gain2)


def enc_attend_back_kernel(
    core_ref, dx2_ref, o_ref, qkv_ref, p_ref, x_ref, vec_ref, wqkv_ref, wo_ref, gproj_ref, gvec2_ref,
    keep_ref, give_ref, dvis_ref,
    gvec_ref, do_s, dqkv_s, gqkv_s, go_s,
):
    clips, slots, width = x_ref.shape
    m_rows = clips * slots
    head_dim, head_masks = enc_heads(width)
    count = len(head_masks)
    scale = head_dim ** (-0.5)
    gain1, shift1 = vec_ref[0:1, :], vec_ref[1:2, :]
    dy2 = dx2_ref[...].astype(BF16)
    go_s[...] = mm(o_ref[...].T, dy2).astype(BF16)
    do_s[...] = mm_t(dy2, wo_ref[...]).astype(BF16)

    def fold(t):
        out = t[:, 0:slots, :]
        for h in range(1, count):
            out = jnp.where(head_masks[h][None], t[:, h * slots : (h + 1) * slots, :], out)
        return out.reshape(m_rows, LANES).astype(BF16)

    for g in range(width // LANES):
        cols = lambda part: slice(part * width + g * LANES, part * width + (g + 1) * LANES)
        q3 = qkv_ref[:, cols(0)].reshape(clips, slots, LANES)
        k3 = enc_spread(qkv_ref[:, cols(1)].reshape(clips, slots, LANES), head_masks)
        v3 = enc_spread(qkv_ref[:, cols(2)].reshape(clips, slots, LANES), head_masks)
        do3 = do_s[:, cols(0)].reshape(clips, slots, LANES)
        span = count * slots
        p3 = p_ref[:, g * span : (g + 1) * span].reshape(clips, slots, span)
        dp = bmm_t(do3, v3)
        parts = []
        for h in range(count):
            hs = slice(h * slots, (h + 1) * slots)
            ph = p3[:, :, hs].astype(F32)
            dph = dp[:, :, hs]
            mean = jnp.sum(ph * dph, axis=-1, keepdims=True)
            parts.append((ph * (dph - mean) * scale).astype(BF16))
        draw3 = jnp.concatenate(parts, axis=2)
        dqkv_s[:, cols(0)] = bmm(draw3, k3).reshape(m_rows, LANES).astype(BF16)
        dqkv_s[:, cols(1)] = fold(bmm_l(draw3, q3))
        dqkv_s[:, cols(2)] = fold(bmm_l(p3, do3))

    x = x_ref[...].reshape(m_rows, width).astype(F32)
    xhat, rstd = normalise(x)
    a1t = (xhat * gain1 + shift1).astype(BF16).T
    gqkv_s[...] = mm(a1t, dqkv_s[...]).astype(BF16)
    da = mm_t(dqkv_s[...], wqkv_ref[...])
    gvec_ref[...] = gvec2_ref[...]
    gvec_ref[0:1, :] = jnp.sum(da * xhat, axis=0, keepdims=True)
    gvec_ref[1:2, :] = jnp.sum(da, axis=0, keepdims=True)
    dx = dx2_ref[...] + norm_back(da, xhat, rstd, gain1)
    dvis_ref[...] = dx.reshape(clips, slots, width).astype(BF16)
    half = keep_ref.shape[1]
    tail = 3 * width - half
    sent = gproj_ref.shape[1]

    def fill(first, second):
        first[...] = gqkv_s[:, :half]
        second[:, :tail] = gqkv_s[:, half:]
        second[:, tail : tail + width] = go_s[...]
        second[:, tail + width : tail + width + sent] = gproj_ref[...]
        end = tail + width + sent
        second[:, end : end + LANES] = columns_of_vectors(gvec_ref[...])
        second[:, end + LANES :] = jnp.zeros((width, half - end - LANES), BF16)

    by_core(core_ref, fill, keep_ref, give_ref)


FEED_CHUNK = 512


def whole_call(kernel, args, outs, scratch, name, flops, steps=1):
    arrays, specs = [], []

    def block(shape, at):
        if callable(at):
            return pl.BlockSpec(shape, at)
        index = (0,) * (len(shape) - 1) + (at,)
        return pl.BlockSpec(shape, lambda i: index, pipeline_mode=pl.Buffered(1))

    for arg in args:
        array, shape, at = arg if isinstance(arg, tuple) else (arg, arg.shape, 0)
        arrays.append(array)
        specs.append(pl.BlockSpec(memory_space=pltpu.SMEM) if len(shape) == 1 else block(shape, at))
    out_specs, shapes = [], []
    for out in outs:
        shape, dtype, part, at = out if len(out) == 4 else out + (out[0], 0)
        out_specs.append(block(part, at))
        shapes.append(jax.ShapeDtypeStruct(shape, dtype))
    return pl.pallas_call(
        kernel,
        grid=(steps,),
        in_specs=specs,
        out_specs=out_specs,
        out_shape=shapes,
        scratch_shapes=[pltpu.VMEM(s, d) for s, d in scratch],
        compiler_params=pltpu.CompilerParams(
            dimension_semantics=("arbitrary",), vmem_limit_bytes=VMEM_BYTES
        ),
        cost_estimate=pl.CostEstimate(flops=flops, bytes_accessed=16 << 20, transcendentals=0),
        name=name,
    )(*arrays)


def enc_blocks(pack, width, ff, sent):
    up = 4 * width // FEED_CHUNK
    return (
        (pack, (width, 3 * width), 0),
        (pack, (width, width), 3),
        (pack, (width, FEED_CHUNK), lambda i: (0, up + i)),
        (pack, (width, sent), (4 * width + ff) // sent),
        (pack, (width, LANES), (4 * width + ff + sent) // LANES),
    )


def enc_attend(x, mask, blocks):
    clips, slots, width = x.shape
    m = clips * slots
    outs = [
        ((m, 3 * width), BF16),
        ((m, HEADS_ENC * slots), BF16),
        ((m, width), BF16),
        ((m, width), F32),
        ((8, width), F32),
    ]
    qkv, out, _, _, small = blocks
    return whole_call(enc_attend_kernel, (x, mask, small, qkv, out), outs, [], "enc_attend", 10**10)


def enc_feed(half, x2, vecs, blocks, wd):
    m, width = x2.shape
    ff, chunk = wd.shape[0], FEED_CHUNK
    _, _, up, proj, _ = blocks
    across, down = lambda i: (0, i), lambda i: (i, 0)
    kept = ((m, ff), BF16, (m, chunk), across)
    sent = ((m // 2, proj[1][1]), BF16)
    outs = [sent, sent, ((m, width), BF16), kept, kept]
    scratch = [((m, width), BF16), ((m, width), F32)]
    args = (half, x2, vecs, up, (wd, (chunk, width), down), proj)
    return whole_call(enc_feed_kernel, args, outs, scratch, "enc_feed", 14 * 10**9, ff // chunk)


def enc_feed_back(core, dsent, enc, h, gp, x2, vecs, blocks, wd):
    m, width = x2.shape
    ff, chunk = wd.shape[0], FEED_CHUNK
    _, _, up, proj, _ = blocks
    across, down = lambda i: (0, i), lambda i: (i, 0)
    half = ((width, ff), BF16, (width, chunk), across)
    outs = [(proj[1], BF16), half, half, ((m, width), F32), ((8, width), F32)]
    scratch = [((width, m), BF16), ((m, width), BF16), ((width, m), BF16), ((m, width), F32)]
    args = (core, dsent, enc, proj, (h, (m, chunk), across), (gp, (m, chunk), across), x2, vecs, up)
    args += ((wd, (chunk, width), down),)
    return whole_call(
        enc_feed_back_kernel, args, outs, scratch, "enc_feed_back", 18 * 10**9, ff // chunk
    )


def attend_half(width, sent):
    blocks = (4 * width + sent + LANES) // LANES
    return (blocks + 1) // 2 * LANES


def enc_attend_back(core, dx2, o, qkv, p, x, vecs, blocks, gproj, gvec):
    m, width = dx2.shape
    w_qkv, w_out, _, _, _ = blocks
    half = (width, attend_half(width, gproj.shape[1]))
    outs = [(half, BF16), (half, BF16), (x.shape, BF16)]
    scratch = [
        ((8, width), F32),
        ((m, width), BF16),
        ((m, 3 * width), BF16),
        ((width, 3 * width), BF16),
        ((width, width), BF16),
    ]
    args = (core, dx2, o, qkv, p, x, vecs, w_qkv, w_out, gproj, gvec)
    return whole_call(enc_attend_back_kernel, args, outs, scratch, "enc_attend_back", 14 * 10**9)


def unpack_kernel(sections, pieces, talls, smalls, packed_ref, *out_refs):
    chips, _, unit, _ = packed_ref.shape

    def read(place, start, size):
        at, part = place
        first, width, count = sections[at]
        blocks = [
            packed_ref[:, part, :, first + k * width + start : first + k * width + start + size]
            for k in range(count)
        ]
        block = blocks[0] if count == 1 else jnp.concatenate(blocks, axis=1)
        return block.reshape(chips * unit * count, size).astype(F32)

    for out, to, place, start, size in pieces:
        out_refs[out][:, to : to + size] = read(place, start, size)
    chunk = 512
    for out, place, start, size in talls:
        for c in range(size // chunk):
            rows = slice(c * chunk, (c + 1) * chunk)
            out_refs[out][rows, :] = read(place, start + c * chunk, chunk).T
    for out, place, start in smalls:
        out_refs[out][...] = read(place, start, LANES).T[0:8, :]


def even_units(packed, sections):
    parts = []
    for first, width, count in sections:
        chips, two, unit, _ = packed.shape
        part = packed[..., first : first + width * count].reshape(chips, two, unit, count, width)
        part = part.transpose(1, 0, 3, 2, 4).reshape(two, 16, count, chips * unit // 16, width)
        parts.append(part.transpose(1, 0, 3, 2, 4).reshape(16, two, chips * unit // 16, count * width))
    return jnp.concatenate(parts, axis=-1)


def unpack_sums(packed, sections, outs, pieces, talls, smalls):
    if packed.shape[2] % 16:
        packed = even_units(packed, sections)
    chips, _, unit, wide = packed.shape
    group = 8
    specs, shapes = [], []
    for at, width, turned in outs:
        step = group * unit * sections[at][2]
        height = chips * unit * sections[at][2]
        if turned:
            specs.append(pl.BlockSpec((turned, step), lambda i: (0, i)))
            shapes.append(jax.ShapeDtypeStruct((turned, height), F32))
        else:
            specs.append(pl.BlockSpec((step, width), lambda i: (i, 0)))
            shapes.append(jax.ShapeDtypeStruct((height, width), F32))
    return pl.pallas_call(
        functools.partial(unpack_kernel, sections, pieces, talls, smalls),
        grid=(chips // group,),
        in_specs=[pl.BlockSpec((group, 2, unit, wide), lambda i: (i, 0, 0, 0))],
        out_specs=specs,
        out_shape=shapes,
        compiler_params=pltpu.CompilerParams(vmem_limit_bytes=VMEM_BYTES),
        cost_estimate=pl.CostEstimate(
            flops=0, bytes_accessed=12 * chips * unit * wide, transcendentals=0
        ),
        name="unpack_sums",
    )(packed)


AXES = ("clip", "band")


def partner_pairs(total, mask):
    return [(i, i ^ mask) for i in range(total)]


def add_low(*parts):
    return sum(part.astype(F32) for part in parts).astype(BF16)


class RunningSum:
    def __init__(self, keep, give, total):
        bits = total.bit_length() - 1
        self.total = total
        self.cut = keep.shape[1] // 256 * 128
        rows = keep.shape[0] // (total // 2)
        self.shape = (2,) * (bits - 1) + (rows, keep.shape[1])
        self.keep = [keep]
        self.got = [lax.ppermute(give, AXES, partner_pairs(total, 1))]
        self.left = [list(range(bits - 1, 0, -1))]
        self.plan = [[[2], [1]], [[1], [2]]]
        rest = list(range(3, bits))
        while rest:
            self.plan.append([rest[:2]])
            rest = rest[2:]

    def settle(self):
        each = len(self.got) // len(self.keep)
        self.held = [
            add_low(keep, *self.got[i * each : (i + 1) * each]) for i, keep in enumerate(self.keep)
        ]
        if self.shape:
            self.held, self.shape = [self.held[0].reshape(self.shape)], None

    def offers(self):
        self.settle()
        me = lax.axis_index(AXES)
        groups = self.plan[0]
        if len(groups) > len(self.held):
            (held,), (left,) = self.held, self.left
            self.held = [held[..., : self.cut], held[..., self.cut :]]
            self.left = [list(left), list(left)]
        if len(groups) < len(self.held):
            self.held = [jnp.concatenate(self.held, axis=-1)]
            self.left = self.left[:1]
        self.keep, gives, self.masks = [], [], []
        for held, left, group in zip(self.held, self.left, groups):
            low, ways = group[0], 1 << len(group)
            place = left.index(group[-1])
            mine = (me >> low) & (ways - 1)
            shape = held.shape
            held = held.reshape(shape[:place] + (ways,) + shape[place + len(group) :])
            self.keep.append(lax.dynamic_index_in_dim(held, mine, place, keepdims=False))
            for k in range(1, ways):
                gives.append(lax.dynamic_index_in_dim(held, mine ^ k, place, keepdims=False))
                self.masks.append(k << low)
            for bit in group:
                left.remove(bit)
        return gives

    def deliver(self, gives):
        self.got = [
            lax.ppermute(give, AXES, partner_pairs(self.total, mask))
            for give, mask in zip(gives, self.masks)
        ]
        self.plan = self.plan[1:]

    def finish(self):
        while self.plan:
            self.deliver(self.offers())
        self.settle()
        return jnp.concatenate(self.held, axis=-1)


class RunningGather:
    def __init__(self, shard, total):
        bits = total.bit_length() - 1
        self.total = total
        self.cut = (shard.shape[1] + LANES) // 256 * 128
        self.shape = shard.shape
        rest, self.plan = list(range(3, bits)), []
        while rest:
            self.plan.append([rest[:2]])
            rest = rest[2:]
        self.plan += [[[1], [2]], [[2], [1]], [[0]]]
        self.held, self.have = [shard], [[]]

    def offers(self):
        groups = self.plan[0]
        if len(groups) > len(self.held):
            (held,), (have,) = self.held, self.have
            self.held = [held[..., : self.cut], held[..., self.cut :]]
            self.have = [list(have), list(have)]
        if len(groups) < len(self.held):
            self.held = [jnp.concatenate(self.held, axis=-1)]
            self.have = self.have[:1]
        gives, self.masks = [], []
        for held, group in zip(self.held, groups):
            for k in range(1, 1 << len(group)):
                gives.append(held)
                self.masks.append(k << group[0])
        return gives

    def deliver(self, gives):
        me = lax.axis_index(AXES)
        got = [
            lax.ppermute(give, AXES, partner_pairs(self.total, mask))
            for give, mask in zip(gives, self.masks)
        ]
        each = len(got) // len(self.held)
        for i, group in enumerate(self.plan[0]):
            parts = [self.held[i]] + got[i * each : (i + 1) * each]
            for b, bit in enumerate(group):
                flip = ((me >> bit) & 1) == 1
                parts = [jnp.where(flip, parts[k ^ (1 << b)], part) for k, part in enumerate(parts)]
            self.have[i] = sorted(self.have[i] + group, reverse=True)
            at = self.have[i].index(group[-1])
            held = jnp.stack(parts, axis=at)
            self.held[i] = held.reshape(held.shape[:at] + (2,) * len(group) + held.shape[at + 1 :])
        self.plan = self.plan[1:]

    def finish(self):
        while self.plan:
            self.deliver(self.offers())
        return self.held[0].reshape((self.total,) + self.shape)


def together(*groups):
    return lax.optimization_barrier(groups)


def gather_rows(shard):
    return lax.all_gather(shard, AXES, axis=0, tiled=True)


def columns_of(vectors):
    block = jnp.stack(vectors, axis=1)
    return jnp.pad(block, ((0, 0), (0, LANES - len(vectors))))


def blocks_beside(tall, rows):
    return [tall[i : i + rows] for i in range(0, tall.shape[0], rows)]


def blocks_below(beside, total, width):
    rows = beside.shape[0] // total
    count = beside.shape[1] // width
    parts = [beside[:, i * width : (i + 1) * width].reshape(total, rows, width) for i in range(count)]
    return jnp.concatenate(parts, axis=1)


def swap_band(array, bit):
    return lax.ppermute(array, "band", [(i, i ^ bit) for i in range(4)])


def owners_to_bands(own, other):
    band = lax.axis_index("band")
    half, side = band // 2, band % 2
    got = swap_band(other, 2)
    pair = jnp.stack([jnp.where(half == 0, own, got), jnp.where(half == 0, got, own)])
    other = swap_band(pair, 1)
    return jnp.stack([jnp.where(side == 0, pair, other), jnp.where(side == 0, other, pair)], axis=1)


def bands_to_owners(pair):
    half = lax.axis_index("band") // 2
    own = lax.dynamic_index_in_dim(pair, half, 0, keepdims=False)
    got = swap_band(lax.dynamic_index_in_dim(pair, 1 - half, 0, keepdims=False), 2)
    return jnp.stack([jnp.where(half == 0, own, got), jnp.where(half == 0, got, own)])


def position_table(places):
    half_width = D_DEC // 2
    omega_vec = jnp.exp(
        jnp.arange(half_width, dtype=F32) * (-math.log(10000.0) / half_width)
    )
    angles = places.astype(F32)[..., None] * omega_vec
    return jnp.concatenate([jnp.sin(angles), jnp.cos(angles)], axis=-1)


def shards(
    visible,
    keep_index,
    visible_count,
    enc_gain1,
    enc_shift1,
    enc_qkv,
    enc_out,
    enc_gain2,
    enc_shift2,
    enc_up,
    enc_down,
    proj,
    mask_token,
    dec_gain1,
    dec_shift1,
    dec_qkv,
    dec_out,
    dec_gain2,
    dec_shift2,
    dec_up,
    dec_down,
    cotangent,
):
    total = lax.axis_size(AXES)
    enc_wide, dec_wide = enc_out.shape[1], dec_out.shape[1]
    enc_ff, dec_ff = enc_up.shape[1], dec_up.shape[1]
    core = (lax.axis_index(AXES) % 2).reshape(1)
    enc_small = columns_of([enc_gain1, enc_shift1, enc_gain2, enc_shift2])
    enc_pack = gather_rows(jnp.concatenate([enc_qkv, enc_out, enc_up, proj, enc_small], axis=1))
    down_run = RunningGather(enc_down, total)
    while len(down_run.plan) > 3:
        down_run.deliver(down_run.offers())

    clip_count, slot_total, _ = visible.shape
    half_clips = clip_count // 2
    band_height = FREQ // 2
    slot_ids = jnp.arange(slot_total)
    valid_rows = slot_ids[None, :] < visible_count[:, None]
    valid_mask = valid_rows.astype(F32)[:, None, :]
    cell_number = jnp.where(valid_rows, keep_index, -1).reshape(2, half_clips, slot_total)
    half = lax.axis_index("band") // 2
    own = lax.dynamic_index_in_dim(cell_number, half, 0, keepdims=False)
    other = lax.dynamic_index_in_dim(cell_number, 1 - half, 0, keepdims=False)
    cell_number = owners_to_bands(own, other).reshape(-1, slot_total)

    dec_small = columns_of([dec_gain1, dec_shift1, dec_gain2, dec_shift2, mask_token])
    dec_tall = blocks_beside(dec_down, dec_out.shape[0])
    dec_pack = jnp.concatenate([dec_qkv, dec_out, dec_up] + dec_tall + [dec_small], axis=1)
    dec_run = RunningGather(dec_pack, total)
    cell_number, gives, dec_gives = together(cell_number, down_run.offers(), dec_run.offers())
    down_run.deliver(gives)
    dec_run.deliver(dec_gives)
    while len(dec_run.plan) > 3:
        dec_run.deliver(dec_run.offers())
    down_run.deliver(down_run.offers())
    gives, dec_gives = together(down_run.offers(), dec_run.offers())
    down_run.deliver(gives)
    dec_run.deliver(dec_gives)
    whole_down = down_run.finish().reshape(-1, enc_wide)
    enc_pack, whole_down, gives = together(enc_pack, whole_down, dec_run.offers())
    dec_run.deliver(gives)

    band_pick = lax.axis_index("band") % 2
    rolled_time = (cell_number // FREQ + TIME - SHIFT) % TIME
    rolled_freq = (cell_number % FREQ + FREQ - SHIFT) % FREQ
    here = (cell_number >= 0) & (rolled_freq // band_height == band_pick)
    arrived_index = jnp.where(here, rolled_time * band_height + rolled_freq % band_height, -1)

    blocks = enc_blocks(enc_pack, enc_wide, enc_ff, dec_wide)
    qkv, probs, mixed, middle, vecs = enc_attend(visible, valid_mask, blocks)
    own, other, encoded, hidden, slope = enc_feed(
        half.reshape(1), middle, vecs, blocks, whole_down
    )
    own, other, gives = together(own, other, dec_run.offers())
    dec_run.deliver(gives)
    dec_pack = dec_run.finish().reshape(-1, dec_pack.shape[1])
    dec_end = 4 * dec_wide + dec_ff
    dec_whole_down = blocks_below(dec_pack[:, dec_end : dec_end + dec_ff], total, dec_wide)
    dec_whole_down = dec_whole_down.reshape(-1, dec_wide)
    parted = (half_clips, slot_total, dec_wide)
    arrived_rows = owners_to_bands(own.reshape(parted), other.reshape(parted))
    half_total = 4 * half_clips

    cell_count = TIME * band_height
    places = jnp.arange(cell_count)
    cell_freq = band_pick * band_height + places % band_height
    patch_number = (places // band_height + SHIFT) % TIME * FREQ + (cell_freq + SHIFT) % FREQ
    span = D_DEC // HEADS_DEC
    query = places[:, None]
    key = query // span * span + jnp.arange(LANES)[None, :] % span

    def label(cell):
        late = cell // band_height >= TIME - SHIFT
        high = band_pick * band_height + cell % band_height >= FREQ - SHIFT
        return late.astype(jnp.int32) * 2 + high.astype(jnp.int32)

    cells_in = WINDOW * WINDOW
    allowed = (query // cells_in == key // cells_in) & (label(query) == label(key))
    decoded, own, other, keep, give = decoder_block(
        core,
        arrived_rows.reshape(half_total, slot_total, dec_wide),
        arrived_index,
        cotangent.reshape(half_total, cell_count, dec_wide),
        position_table(patch_number),
        allowed.astype(F32),
        dec_pack,
        dec_whole_down,
    )
    decoded_out = decoded.reshape(cotangent.shape)

    returning = (own + swap_band(other, 1)).reshape(2, half_clips, slot_total, dec_wide)
    returning, keep, give = together(returning, keep, give)
    dec_run = RunningSum(keep, give, total)
    grad_sent = bands_to_owners(returning).reshape(-1, dec_wide)
    grad_sent, gives = together(grad_sent, dec_run.offers())
    dec_run.deliver(gives)
    g_proj, keep, give, grad_middle, g_vec = enc_feed_back(
        core, grad_sent, encoded, hidden, slope, middle, vecs, blocks, whole_down
    )
    keep, give, grad_middle, gives = together(keep, give, grad_middle, dec_run.offers())
    dec_run.deliver(gives)
    feed_run = RunningSum(keep, give, total)
    keep, give, grad_visible = enc_attend_back(
        core, grad_middle, mixed, qkv, probs, visible, vecs, blocks, g_proj, g_vec
    )
    keep, give, dec_run.got, feed_run.got = together(keep, give, dec_run.got, feed_run.got)
    attend_run = RunningSum(keep, give, total)
    feed_gives, dec_run.got, attend_run.got = together(
        feed_run.offers(), dec_run.got, attend_run.got
    )
    feed_run.deliver(feed_gives)
    dec_run.deliver(dec_run.offers())
    dec_shard, feed_gives = together(dec_run.finish(), feed_run.offers())
    feed_run.deliver(feed_gives)
    feed_gives, gives = together(feed_run.offers(), attend_run.offers())
    feed_run.deliver(feed_gives)
    attend_run.deliver(gives)
    feed_shard = feed_run.finish()
    feed_shard, gives = together(feed_shard, attend_run.offers())
    unit = dec_shard.shape[0] // 2
    dec_units = [dec_shard[k * unit : (k + 1) * unit] for k in range(2)]
    feed_units = [feed_shard[k * unit : (k + 1) * unit] for k in range(3)]
    most_sum = gather_rows(jnp.concatenate(dec_units + feed_units, axis=1))
    attend_run.deliver(gives)
    attend_shard = attend_run.finish()
    attend_sum = RunningGather(attend_shard, total).finish()

    half = attend_shard.shape[1]
    tail = 3 * enc_wide - half
    e_qkv, e_out, e_proj, enc_vecs = unpack_sums(
        attend_sum.reshape((total // 2, 2) + attend_shard.shape),
        ((0, half, 1),),
        ((0, 3 * enc_wide, 0), (0, enc_wide, 0), (0, dec_wide, 0), (0, 0, 8)),
        (
            (0, 0, (0, 0), 0, half),
            (0, half, (0, 1), 0, tail),
            (1, 0, (0, 1), tail, enc_wide),
            (2, 0, (0, 1), tail + enc_wide, dec_wide),
        ),
        (),
        ((3, (0, 1), tail + enc_wide + dec_wide),),
    )
    half = dec_ff // 2
    dec_half = dec_shard.shape[1]
    d_qkv, d_out, d_up, d_down, dec_vecs, e_up, e_down = unpack_sums(
        most_sum.reshape(total // 2, 2, unit, most_sum.shape[1]),
        ((0, dec_half, 2), (2 * dec_half, enc_ff, 3)),
        (
            (0, 3 * dec_wide, 0),
            (0, dec_wide, 0),
            (0, dec_ff, 0),
            (0, 0, dec_ff),
            (0, 0, 8),
            (1, enc_ff, 0),
            (1, 0, enc_ff),
        ),
        (
            (0, 0, (0, 0), 0, 3 * dec_wide),
            (1, 0, (0, 0), 3 * dec_wide, dec_wide),
            (2, 0, (0, 0), 4 * dec_wide, half),
            (2, half, (0, 1), 0, half),
            (5, 0, (1, 0), 0, enc_ff),
        ),
        ((3, (0, 1), half, dec_ff), (6, (1, 1), 0, enc_ff)),
        ((4, (0, 0), 4 * dec_wide + half),),
    )
    return (
        decoded_out,
        grad_visible,
        enc_vecs[0],
        enc_vecs[1],
        e_qkv,
        e_out,
        enc_vecs[2],
        enc_vecs[3],
        e_up,
        e_down,
        e_proj,
        dec_vecs[4],
        dec_vecs[0],
        dec_vecs[1],
        d_qkv,
        d_out,
        dec_vecs[2],
        dec_vecs[3],
        d_up,
        d_down,
    )


def solution(mesh):
    return jax.shard_map(
        shards,
        mesh=mesh,
        in_specs=(
            P(("clip", "band"), None, None),
            P(("clip", "band"), None),
            P(("clip", "band")),
            P(("clip", "band")),
            P(("clip", "band")),
            P(("clip", "band"), None),
            P(("clip", "band"), None),
            P(("clip", "band")),
            P(("clip", "band")),
            P(("clip", "band"), None),
            P(("clip", "band"), None),
            P(("clip", "band"), None),
            P(("clip", "band")),
            P(("clip", "band")),
            P(("clip", "band")),
            P(("clip", "band"), None),
            P(("clip", "band"), None),
            P(("clip", "band")),
            P(("clip", "band")),
            P(("clip", "band"), None),
            P(("clip", "band"), None),
            P(("clip", "band"), None, None, None, None),
        ),
        out_specs=(
            P(("clip", "band"), None, None, None, None),
            P(("clip", "band"), None, None),
            P(),
            P(),
            P(),
            P(),
            P(),
            P(),
            P(),
            P(),
            P(),
            P(),
            P(),
            P(),
            P(),
            P(),
            P(),
            P(),
            P(),
            P(),
        ),
        check_vma=False,
    )
```

```python
import functools
import math

import jax
import jax.numpy as jnp
from jax import lax
from jax.experimental import pallas as pl
from jax.experimental.pallas import tpu as pltpu
from jax.sharding import PartitionSpec as P

HEADS_ENC = 12
D_DEC = 512
HEADS_DEC = 16
TIME = 64
FREQ = 8
WINDOW = 4
SHIFT = 2
norm_eps = 1e-06
neg_fill = -1e30
F32 = jnp.float32
BF16 = jnp.bfloat16
LANES = 128
VMEM_BYTES = 58 * 1024 * 1024


def mm(a, b):
    return lax.dot_general(a, b, (((1,), (0,)), ((), ())), preferred_element_type=F32)


def mm_t(a, b):
    return lax.dot_general(a, b, (((1,), (1,)), ((), ())), preferred_element_type=F32)


def bmm(a, b):
    return lax.dot_general(a, b, (((2,), (1,)), ((0,), (0,))), preferred_element_type=F32)


def bmm_t(a, b):
    return lax.dot_general(a, b, (((2,), (2,)), ((0,), (0,))), preferred_element_type=F32)


def bmm_l(a, b):
    return lax.dot_general(a, b, (((1,), (1,)), ((0,), (0,))), preferred_element_type=F32)


def normalise(x):
    centre = jnp.mean(x, axis=-1, keepdims=True)
    centred = x - centre
    rstd = lax.rsqrt(jnp.mean(centred * centred, axis=-1, keepdims=True) + norm_eps)
    return centred * rstd, rstd


def norm_back(da, xhat, rstd, gain):
    dag = da * gain
    return rstd * (
        dag
        - jnp.mean(dag, axis=-1, keepdims=True)
        - xhat * jnp.mean(dag * xhat, axis=-1, keepdims=True)
    )


def gelu_parts(u):
    size = jnp.abs(u) * 0.7071067811865476
    bell = jnp.exp(-0.5 * u * u)
    t = 1.0 / (1.0 + 0.3275911 * size)
    poly = 0.530702715
    poly = poly * t - 0.726576013
    poly = poly * t + 0.710706871
    poly = poly * t - 0.142248368
    poly = poly * t + 0.127414796
    tail = poly * t * bell
    cdf = jnp.where(u >= 0, 1.0 - tail, tail)
    return cdf, u * bell * 0.3989422804014327


def vectors_of(small_ref):
    return small_ref[...].astype(F32).T[0:8, :]


def columns_of_vectors(vectors):
    count, width = vectors.shape
    block = jnp.concatenate([vectors, jnp.zeros((LANES - count, width), F32)], axis=0)
    return block.T.astype(BF16)


def by_core(core_ref, fill, keep_ref, give_ref):
    @pl.when(core_ref[0] == 0)
    def _():
        fill(keep_ref, give_ref)

    @pl.when(core_ref[0] != 0)
    def _():
        fill(give_ref, keep_ref)


def segment_sum(x, ones):
    return mm(x.astype(BF16), ones)


def window_max(s):
    ahead = s
    behind = s
    for step in (1, 2, 4, 8):
        ahead = jnp.maximum(ahead, pltpu.roll(ahead, step, 1))
        behind = jnp.maximum(behind, pltpu.roll(behind, LANES - step, 1))
    return jnp.maximum(ahead, behind)


def decoder_kernel(
    core_ref, rows_ref, idx_ref, cot_ref, pos_ref, mask_ref, small_ref, wqkv_ref, wo_ref, wu_ref, wd_ref,
    out_ref, own_ref, other_ref, keep_ref, give_ref,
    acc_qkv, acc_o, acc_u, acc_d, gvec_ref, vec_ref,
    x_s, qkv_s, p_s, o_s, a2_s, a2t_s, dzt_s, da_s, y_s, dqkv_s,
):
    step = pl.program_id(0)
    last = pl.num_programs(0) - 1
    halves, cells, width = cot_ref.shape
    m_rows = halves * cells
    slots = rows_ref.shape[1]
    head_dim = width // HEADS_DEC
    heads_in = LANES // head_dim
    groups = width // LANES
    block = LANES // heads_in
    blocks = m_rows // block
    scale = head_dim ** (-0.5)
    ff = wu_ref.shape[1]
    chunk = 1024

    @pl.when(step == 0)
    def _():
        acc_qkv[...] = jnp.zeros_like(acc_qkv)
        acc_o[...] = jnp.zeros_like(acc_o)
        acc_u[...] = jnp.zeros_like(acc_u)
        acc_d[...] = jnp.zeros_like(acc_d)
        gvec_ref[...] = jnp.zeros_like(gvec_ref)
        vec_ref[...] = vectors_of(small_ref)

    gain1, shift1 = vec_ref[0:1, :], vec_ref[1:2, :]
    gain2, shift2 = vec_ref[2:3, :], vec_ref[3:4, :]
    token = vec_ref[4:5, :]

    def place_of(h):
        cell = lax.broadcasted_iota(jnp.int32, (cells, slots), 0)
        return cell == idx_ref[h]

    unseen = []
    for h in range(halves):
        place = place_of(h)
        unseen_h = 1.0 - jnp.sum(place.astype(F32), axis=1, keepdims=True)
        unseen.append(unseen_h)
        x_s[h * cells : (h + 1) * cells, :] = (
            mm(place.astype(BF16), rows_ref[h]) + unseen_h * token + pos_ref[...]
        )
    xhat1, rstd1 = normalise(x_s[...])
    a1 = (xhat1 * gain1 + shift1).astype(BF16)
    qkv_s[...] = mm(a1, wqkv_ref[...]).astype(BF16)

    lane = lax.broadcasted_iota(jnp.int32, (1, LANES), 1)
    head_masks = [(lane // head_dim == h) for h in range(heads_in)]
    ones = (
        lax.broadcasted_iota(jnp.int32, (LANES, LANES), 0) // block
        == lax.broadcasted_iota(jnp.int32, (LANES, LANES), 1) // block
    ).astype(BF16)

    def spread(t):
        parts = [t * hm.astype(BF16)[None] for hm in head_masks]
        return jnp.concatenate(parts, axis=1)

    def fold(t):
        out = t[:, 0:block, :]
        for h in range(1, heads_in):
            out = jnp.where(head_masks[h][None], t[:, h * block : (h + 1) * block, :], out)
        return out

    def part(ref, base, g):
        return ref[:, base + g * LANES : base + (g + 1) * LANES].reshape(blocks, block, LANES)

    allowed = jnp.concatenate([mask_ref[...]] * halves, axis=0) > 0.5
    for g in range(groups):
        q3 = part(qkv_s, 0, g)
        k3 = spread(part(qkv_s, width, g))
        v3 = spread(part(qkv_s, 2 * width, g))
        s = bmm_t(q3, k3).reshape(m_rows, LANES) * scale
        s = jnp.where(allowed, s, neg_fill)
        e = jnp.where(allowed, jnp.exp(s - window_max(s)), 0.0)
        p = e / segment_sum(e, ones)
        p_s[:, g * LANES : (g + 1) * LANES] = p
        o = bmm(p.astype(BF16).reshape(blocks, block, LANES), v3)
        o_s[:, g * LANES : (g + 1) * LANES] = o.reshape(m_rows, LANES).astype(BF16)

    x2 = x_s[...] + mm(o_s[...], wo_ref[...])
    xhat2, rstd2 = normalise(x2)
    a2 = (xhat2 * gain2 + shift2).astype(BF16)
    a2_s[...] = a2
    a2t_s[...] = a2.T
    dz = cot_ref[...].reshape(m_rows, width)
    dzt_s[...] = dz.T
    y_s[...] = x2
    da_s[...] = jnp.zeros_like(da_s)

    for c in range(ff // chunk):
        at = slice(c * chunk, (c + 1) * chunk)
        u = mm(a2_s[...], wu_ref[:, at])
        dh = mm_t(cot_ref[...].reshape(m_rows, width), wd_ref[at, :])
        cdf, bump = gelu_parts(u)
        h = (u * cdf).astype(BF16)
        du = ((cdf + bump) * dh).astype(BF16)
        y_s[...] += mm(h, wd_ref[at, :])
        da_s[...] += mm_t(du, wu_ref[:, at])
        acc_d[:, at] += mm(dzt_s[...], h)
        acc_u[:, at] += mm(a2t_s[...], du)

    out_ref[...] = y_s[...].reshape(halves, cells, width).astype(BF16)
    da2 = da_s[...]
    gvec_ref[2:3, :] += jnp.sum(da2 * xhat2, axis=0, keepdims=True)
    gvec_ref[3:4, :] += jnp.sum(da2, axis=0, keepdims=True)
    dx2 = cot_ref[...].reshape(m_rows, width).astype(F32) + norm_back(da2, xhat2, rstd2, gain2)
    dy2 = dx2.astype(BF16)
    acc_o[...] += mm(o_s[...].T, dy2)
    do = mm_t(dy2, wo_ref[...]).astype(BF16)

    for g in range(groups):
        cols = slice(g * LANES, (g + 1) * LANES)
        q3 = part(qkv_s, 0, g)
        k3 = spread(part(qkv_s, width, g))
        v3 = spread(part(qkv_s, 2 * width, g))
        do3 = do[:, cols].reshape(blocks, block, LANES)
        p = p_s[:, cols]
        dp = bmm_t(do3, v3).reshape(m_rows, LANES)
        draw = (p * (dp - segment_sum(p * dp, ones)) * scale).astype(BF16)
        draw3 = draw.reshape(blocks, block, LANES)
        dq = bmm(draw3, k3).reshape(m_rows, LANES)
        dk = fold(bmm_l(draw3, q3)).reshape(m_rows, LANES)
        dv = fold(bmm_l(p.astype(BF16).reshape(blocks, block, LANES), do3)).reshape(m_rows, LANES)
        dqkv_s[:, g * LANES : (g + 1) * LANES] = dq.astype(BF16)
        dqkv_s[:, width + g * LANES : width + (g + 1) * LANES] = dk.astype(BF16)
        dqkv_s[:, 2 * width + g * LANES : 2 * width + (g + 1) * LANES] = dv.astype(BF16)

    xhat1, rstd1 = normalise(x_s[...])
    a1 = (xhat1 * gain1 + shift1).astype(BF16)
    dqkv = dqkv_s[...]
    acc_qkv[...] += mm(a1.T, dqkv)
    da1 = mm_t(dqkv, wqkv_ref[...])
    gvec_ref[0:1, :] += jnp.sum(da1 * xhat1, axis=0, keepdims=True)
    gvec_ref[1:2, :] += jnp.sum(da1, axis=0, keepdims=True)
    dx = dx2 + norm_back(da1, xhat1, rstd1, gain1)
    for h in range(halves):
        dx_h = dx[h * cells : (h + 1) * cells, :]
        gvec_ref[4:5, :] += jnp.sum(unseen[h] * dx_h, axis=0, keepdims=True)
        place = place_of(h).astype(F32).T.astype(BF16)
        back = mm(place, dx_h.astype(BF16)).astype(BF16)
        ours = core_ref[0] == lax.rem(step, 2)

        @pl.when(ours)
        def _(back=back, h=h):
            own_ref[h] = back

        @pl.when(jnp.logical_not(ours))
        def _(back=back, h=h):
            other_ref[h] = back

    @pl.when(step == last)
    def _():
        half = ff // 2

        def fill(first, second):
            first[:, : 3 * width] = acc_qkv[...].astype(BF16)
            first[:, 3 * width : 4 * width] = acc_o[...].astype(BF16)
            first[:, 4 * width : 4 * width + half] = acc_u[:, :half].astype(BF16)
            first[:, 4 * width + half :] = columns_of_vectors(gvec_ref[...])
            second[:, :half] = acc_u[:, half:].astype(BF16)
            second[:, half : half + ff] = acc_d[...].astype(BF16)
            second[:, half + ff :] = jnp.zeros((width, second.shape[1] - half - ff), BF16)

        by_core(core_ref, fill, keep_ref, give_ref)


def decoder_block(core, rows, idx, cot, pos, mask, pack, wd):
    n_half, slots, width = rows.shape
    cells = cot.shape[1]
    ff = wd.shape[0]
    halves = 2
    m_rows = halves * cells
    half_wide = 4 * width + ff // 2 + LANES
    vm = pltpu.VMEM
    flops = 6 * n_half * cells * (4 * width + 2 * ff) * width * 2

    def whole(*shape, at=0):
        index = (0,) * (len(shape) - 1) + (at,)
        return pl.BlockSpec(shape, lambda i: index, pipeline_mode=pl.Buffered(1))

    return pl.pallas_call(
        decoder_kernel,
        grid=(n_half // halves,),
        in_specs=[
            pl.BlockSpec(memory_space=pltpu.SMEM),
            pl.BlockSpec((halves, slots, width), lambda i: (i, 0, 0)),
            pl.BlockSpec((halves, 1, slots), lambda i: (i, 0, 0)),
            pl.BlockSpec((halves, cells, width), lambda i: (i, 0, 0)),
            whole(cells, width),
            whole(cells, LANES),
            whole(width, LANES, at=(4 * width + 2 * ff) // LANES),
            whole(width, 3 * width),
            whole(width, width, at=3),
            whole(width, ff, at=1),
            whole(ff, width),
        ],
        out_specs=[
            pl.BlockSpec((halves, cells, width), lambda i: (i, 0, 0)),
            pl.BlockSpec((halves, slots, width), lambda i: (i // 2, 0, 0)),
            pl.BlockSpec((halves, slots, width), lambda i: (i // 2, 0, 0)),
            whole(width, half_wide),
            whole(width, half_wide),
        ],
        out_shape=[
            jax.ShapeDtypeStruct((n_half, cells, width), BF16),
            jax.ShapeDtypeStruct((n_half // 2, slots, width), BF16),
            jax.ShapeDtypeStruct((n_half // 2, slots, width), BF16),
            jax.ShapeDtypeStruct((width, half_wide), BF16),
            jax.ShapeDtypeStruct((width, half_wide), BF16),
        ],
        scratch_shapes=[
            vm((width, 3 * width), F32),
            vm((width, width), F32),
            vm((width, ff), F32),
            vm((width, ff), F32),
            vm((8, width), F32),
            vm((8, width), F32),
            vm((m_rows, width), F32),
            vm((m_rows, 3 * width), BF16),
            vm((m_rows, width), F32),
            vm((m_rows, width), BF16),
            vm((m_rows, width), BF16),
            vm((width, m_rows), BF16),
            vm((width, m_rows), BF16),
            vm((m_rows, width), F32),
            vm((m_rows, width), F32),
            vm((m_rows, 3 * width), BF16),
        ],
        compiler_params=pltpu.CompilerParams(
            dimension_semantics=("arbitrary",), vmem_limit_bytes=VMEM_BYTES
        ),
        cost_estimate=pl.CostEstimate(flops=flops, bytes_accessed=40 << 20, transcendentals=0),
        name="decoder_block",
    )(
        core, rows, idx.reshape(n_half, 1, slots), cot, pos, mask,
        pack, pack, pack, pack, wd,
    )


def enc_spread(t, head_masks):
    return jnp.concatenate([t * hm.astype(BF16)[None] for hm in head_masks], axis=1)


def enc_heads(width):
    head_dim = width // HEADS_ENC
    lane = lax.broadcasted_iota(jnp.int32, (1, LANES), 1)
    return head_dim, [(lane // head_dim == h) for h in range(LANES // head_dim)]


def enc_attend_kernel(
    x_ref, mask_ref, small_ref, wqkv_ref, wo_ref, qkv_ref, p_ref, o_ref, x2_ref, vec_ref
):
    vec_ref[...] = vectors_of(small_ref)
    clips, slots, width = x_ref.shape
    m_rows = clips * slots
    head_dim, head_masks = enc_heads(width)
    scale = head_dim ** (-0.5)
    x = x_ref[...].reshape(m_rows, width).astype(F32)
    xhat, rstd = normalise(x)
    a1 = (xhat * vec_ref[0:1, :] + vec_ref[1:2, :]).astype(BF16)
    qkv_ref[...] = mm(a1, wqkv_ref[...]).astype(BF16)
    allowed = mask_ref[...] > 0.5
    for g in range(width // LANES):
        cols = lambda part: slice(part * width + g * LANES, part * width + (g + 1) * LANES)
        q3 = qkv_ref[:, cols(0)].reshape(clips, slots, LANES)
        k3 = enc_spread(qkv_ref[:, cols(1)].reshape(clips, slots, LANES), head_masks)
        v3 = enc_spread(qkv_ref[:, cols(2)].reshape(clips, slots, LANES), head_masks)
        s = bmm_t(q3, k3) * scale
        for h in range(len(head_masks)):
            sh = jnp.where(allowed, s[:, :, h * slots : (h + 1) * slots], neg_fill)
            e = jnp.exp(sh - jnp.max(sh, axis=-1, keepdims=True))
            e = e / jnp.sum(e, axis=-1, keepdims=True)
            at = (g * len(head_masks) + h) * slots
            p_ref[:, at : at + slots] = e.reshape(m_rows, slots).astype(BF16)
        span = len(head_masks) * slots
        p3 = p_ref[:, g * span : (g + 1) * span].reshape(clips, slots, span)
        o_ref[:, cols(0)] = bmm(p3, v3).reshape(m_rows, LANES).astype(BF16)
    x2_ref[...] = x_ref[...].reshape(m_rows, width).astype(F32) + mm(o_ref[...], wo_ref[...])


def enc_feed_kernel(
    half_ref, x2_ref, vec_ref, wu_ref, wd_ref, proj_ref,
    own_ref, other_ref, enc_ref, h_ref, gp_ref,
    a2_s, y_s,
):
    step = pl.program_id(0)

    @pl.when(step == 0)
    def _():
        xhat, rstd = normalise(x2_ref[...])
        a2_s[...] = (xhat * vec_ref[2:3, :] + vec_ref[3:4, :]).astype(BF16)
        y_s[...] = x2_ref[...]

    u = mm(a2_s[...], wu_ref[...])
    cdf, bump = gelu_parts(u)
    h = (u * cdf).astype(BF16)
    h_ref[...] = h
    gp_ref[...] = (cdf + bump).astype(BF16)
    y_s[...] += mm(h, wd_ref[...])

    @pl.when(step == pl.num_programs(0) - 1)
    def _():
        encoded = y_s[...].astype(BF16)
        enc_ref[...] = encoded
        sent = mm(encoded, proj_ref[...]).astype(BF16)
        rows = own_ref.shape[0]
        first = half_ref[0] == 0
        own_ref[...] = jnp.where(first, sent[:rows], sent[rows:])
        other_ref[...] = jnp.where(first, sent[rows:], sent[:rows])


def enc_feed_back_kernel(
    core_ref, dsent_ref, enc_ref, proj_ref, h_ref, gp_ref, x2_ref, vec_ref, wu_ref, wd_ref,
    gproj_ref, keep_ref, give_ref, dx2_ref, gvec_ref,
    a2t_s, dz_s, dzt_s, da_s,
):
    step = pl.program_id(0)
    gain2 = vec_ref[2:3, :]

    @pl.when(step == 0)
    def _():
        dsent = dsent_ref[...]
        gproj_ref[...] = mm(enc_ref[...].T, dsent).astype(BF16)
        dy = mm_t(dsent, proj_ref[...])
        dx2_ref[...] = dy
        dz = dy.astype(BF16)
        dz_s[...] = dz
        dzt_s[...] = dz.T
        xhat, rstd = normalise(x2_ref[...])
        a2t_s[...] = (xhat * gain2 + vec_ref[3:4, :]).astype(BF16).T
        da_s[...] = jnp.zeros_like(da_s)

    dh = mm_t(dz_s[...], wd_ref[...])
    du = (gp_ref[...].astype(F32) * dh).astype(BF16)
    down_grad = mm(dzt_s[...], h_ref[...]).astype(BF16)
    up_grad = mm(a2t_s[...], du).astype(BF16)
    da_s[...] += mm_t(du, wu_ref[...])
    first = core_ref[0] == 0
    keep_ref[...] = jnp.where(first, up_grad, down_grad)
    give_ref[...] = jnp.where(first, down_grad, up_grad)

    @pl.when(step == pl.num_programs(0) - 1)
    def _():
        da = da_s[...]
        xhat, rstd = normalise(x2_ref[...])
        gvec_ref[...] = jnp.zeros_like(gvec_ref)
        gvec_ref[2:3, :] = jnp.sum(da * xhat, axis=0, keepdims=True)
        gvec_ref[3:4, :] = jnp.sum(da, axis=0, keepdims=True)
        dx2_ref[...] += norm_back(da, xhat, rstd, gain2)


def enc_attend_back_kernel(
    core_ref, dx2_ref, o_ref, qkv_ref, p_ref, x_ref, vec_ref, wqkv_ref, wo_ref, gproj_ref, gvec2_ref,
    keep_ref, give_ref, dvis_ref,
    gvec_ref, do_s, dqkv_s, gqkv_s, go_s,
):
    clips, slots, width = x_ref.shape
    m_rows = clips * slots
    head_dim, head_masks = enc_heads(width)
    count = len(head_masks)
    scale = head_dim ** (-0.5)
    gain1, shift1 = vec_ref[0:1, :], vec_ref[1:2, :]
    dy2 = dx2_ref[...].astype(BF16)
    go_s[...] = mm(o_ref[...].T, dy2).astype(BF16)
    do_s[...] = mm_t(dy2, wo_ref[...]).astype(BF16)

    def fold(t):
        out = t[:, 0:slots, :]
        for h in range(1, count):
            out = jnp.where(head_masks[h][None], t[:, h * slots : (h + 1) * slots, :], out)
        return out.reshape(m_rows, LANES).astype(BF16)

    for g in range(width // LANES):
        cols = lambda part: slice(part * width + g * LANES, part * width + (g + 1) * LANES)
        q3 = qkv_ref[:, cols(0)].reshape(clips, slots, LANES)
        k3 = enc_spread(qkv_ref[:, cols(1)].reshape(clips, slots, LANES), head_masks)
        v3 = enc_spread(qkv_ref[:, cols(2)].reshape(clips, slots, LANES), head_masks)
        do3 = do_s[:, cols(0)].reshape(clips, slots, LANES)
        span = count * slots
        p3 = p_ref[:, g * span : (g + 1) * span].reshape(clips, slots, span)
        dp = bmm_t(do3, v3)
        parts = []
        for h in range(count):
            hs = slice(h * slots, (h + 1) * slots)
            ph = p3[:, :, hs].astype(F32)
            dph = dp[:, :, hs]
            mean = jnp.sum(ph * dph, axis=-1, keepdims=True)
            parts.append((ph * (dph - mean) * scale).astype(BF16))
        draw3 = jnp.concatenate(parts, axis=2)
        dqkv_s[:, cols(0)] = bmm(draw3, k3).reshape(m_rows, LANES).astype(BF16)
        dqkv_s[:, cols(1)] = fold(bmm_l(draw3, q3))
        dqkv_s[:, cols(2)] = fold(bmm_l(p3, do3))

    x = x_ref[...].reshape(m_rows, width).astype(F32)
    xhat, rstd = normalise(x)
    a1t = (xhat * gain1 + shift1).astype(BF16).T
    gqkv_s[...] = mm(a1t, dqkv_s[...]).astype(BF16)
    da = mm_t(dqkv_s[...], wqkv_ref[...])
    gvec_ref[...] = gvec2_ref[...]
    gvec_ref[0:1, :] = jnp.sum(da * xhat, axis=0, keepdims=True)
    gvec_ref[1:2, :] = jnp.sum(da, axis=0, keepdims=True)
    dx = dx2_ref[...] + norm_back(da, xhat, rstd, gain1)
    dvis_ref[...] = dx.reshape(clips, slots, width).astype(BF16)
    half = keep_ref.shape[1]
    tail = 3 * width - half
    sent = gproj_ref.shape[1]

    def fill(first, second):
        first[...] = gqkv_s[:, :half]
        second[:, :tail] = gqkv_s[:, half:]
        second[:, tail : tail + width] = go_s[...]
        second[:, tail + width : tail + width + sent] = gproj_ref[...]
        end = tail + width + sent
        second[:, end : end + LANES] = columns_of_vectors(gvec_ref[...])
        second[:, end + LANES :] = jnp.zeros((width, half - end - LANES), BF16)

    by_core(core_ref, fill, keep_ref, give_ref)


FEED_CHUNK = 768


def whole_call(kernel, args, outs, scratch, name, flops, steps=1):
    arrays, specs = [], []

    def block(shape, at):
        if callable(at):
            return pl.BlockSpec(shape, at)
        index = (0,) * (len(shape) - 1) + (at,)
        return pl.BlockSpec(shape, lambda i: index, pipeline_mode=pl.Buffered(1))

    for arg in args:
        array, shape, at = arg if isinstance(arg, tuple) else (arg, arg.shape, 0)
        arrays.append(array)
        specs.append(pl.BlockSpec(memory_space=pltpu.SMEM) if len(shape) == 1 else block(shape, at))
    out_specs, shapes = [], []
    for out in outs:
        shape, dtype, part, at = out if len(out) == 4 else out + (out[0], 0)
        out_specs.append(block(part, at))
        shapes.append(jax.ShapeDtypeStruct(shape, dtype))
    return pl.pallas_call(
        kernel,
        grid=(steps,),
        in_specs=specs,
        out_specs=out_specs,
        out_shape=shapes,
        scratch_shapes=[pltpu.VMEM(s, d) for s, d in scratch],
        compiler_params=pltpu.CompilerParams(
            dimension_semantics=("arbitrary",), vmem_limit_bytes=VMEM_BYTES
        ),
        cost_estimate=pl.CostEstimate(flops=flops, bytes_accessed=16 << 20, transcendentals=0),
        name=name,
    )(*arrays)


def enc_blocks(pack, width, ff, sent):
    up = 4 * width // FEED_CHUNK
    return (
        (pack, (width, 3 * width), 0),
        (pack, (width, width), 3),
        (pack, (width, FEED_CHUNK), lambda i: (0, up + i)),
        (pack, (width, sent), (4 * width + ff) // sent),
        (pack, (width, LANES), (4 * width + ff + sent) // LANES),
    )


def enc_attend(x, mask, blocks):
    clips, slots, width = x.shape
    m = clips * slots
    outs = [
        ((m, 3 * width), BF16),
        ((m, HEADS_ENC * slots), BF16),
        ((m, width), BF16),
        ((m, width), F32),
        ((8, width), F32),
    ]
    qkv, out, _, _, small = blocks
    return whole_call(enc_attend_kernel, (x, mask, small, qkv, out), outs, [], "enc_attend", 10**10)


def enc_feed(half, x2, vecs, blocks, wd):
    m, width = x2.shape
    ff, chunk = wd.shape[0], FEED_CHUNK
    _, _, up, proj, _ = blocks
    across, down = lambda i: (0, i), lambda i: (i, 0)
    kept = ((m, ff), BF16, (m, chunk), across)
    sent = ((m // 2, proj[1][1]), BF16)
    outs = [sent, sent, ((m, width), BF16), kept, kept]
    scratch = [((m, width), BF16), ((m, width), F32)]
    args = (half, x2, vecs, up, (wd, (chunk, width), down), proj)
    return whole_call(enc_feed_kernel, args, outs, scratch, "enc_feed", 14 * 10**9, ff // chunk)


def enc_feed_back(core, dsent, enc, h, gp, x2, vecs, blocks, wd):
    m, width = x2.shape
    ff, chunk = wd.shape[0], FEED_CHUNK
    _, _, up, proj, _ = blocks
    across, down = lambda i: (0, i), lambda i: (i, 0)
    half = ((width, ff), BF16, (width, chunk), across)
    outs = [(proj[1], BF16), half, half, ((m, width), F32), ((8, width), F32)]
    scratch = [((width, m), BF16), ((m, width), BF16), ((width, m), BF16), ((m, width), F32)]
    args = (core, dsent, enc, proj, (h, (m, chunk), across), (gp, (m, chunk), across), x2, vecs, up)
    args += ((wd, (chunk, width), down),)
    return whole_call(
        enc_feed_back_kernel, args, outs, scratch, "enc_feed_back", 18 * 10**9, ff // chunk
    )


def attend_half(width, sent):
    blocks = (4 * width + sent + LANES) // LANES
    return (blocks + 1) // 2 * LANES


def enc_attend_back(core, dx2, o, qkv, p, x, vecs, blocks, gproj, gvec):
    m, width = dx2.shape
    w_qkv, w_out, _, _, _ = blocks
    half = (width, attend_half(width, gproj.shape[1]))
    outs = [(half, BF16), (half, BF16), (x.shape, BF16)]
    scratch = [
        ((8, width), F32),
        ((m, width), BF16),
        ((m, 3 * width), BF16),
        ((width, 3 * width), BF16),
        ((width, width), BF16),
    ]
    args = (core, dx2, o, qkv, p, x, vecs, w_qkv, w_out, gproj, gvec)
    return whole_call(enc_attend_back_kernel, args, outs, scratch, "enc_attend_back", 14 * 10**9)


def unpack_kernel(sections, pieces, talls, smalls, packed_ref, *out_refs):
    chips, _, unit, _ = packed_ref.shape

    def read(place, start, size):
        at, part = place
        first, width, count = sections[at]
        blocks = [
            packed_ref[:, part, :, first + k * width + start : first + k * width + start + size]
            for k in range(count)
        ]
        block = blocks[0] if count == 1 else jnp.concatenate(blocks, axis=1)
        return block.reshape(chips * unit * count, size).astype(F32)

    for out, to, place, start, size in pieces:
        out_refs[out][:, to : to + size] = read(place, start, size)
    chunk = 512
    for out, place, start, size in talls:
        for c in range(size // chunk):
            rows = slice(c * chunk, (c + 1) * chunk)
            out_refs[out][rows, :] = read(place, start + c * chunk, chunk).T
    for out, place, start in smalls:
        out_refs[out][...] = read(place, start, LANES).T[0:8, :]


def even_units(packed, sections):
    parts = []
    for first, width, count in sections:
        chips, two, unit, _ = packed.shape
        part = packed[..., first : first + width * count].reshape(chips, two, unit, count, width)
        part = part.transpose(1, 0, 3, 2, 4).reshape(two, 16, count, chips * unit // 16, width)
        parts.append(part.transpose(1, 0, 3, 2, 4).reshape(16, two, chips * unit // 16, count * width))
    return jnp.concatenate(parts, axis=-1)


def unpack_sums(packed, sections, outs, pieces, talls, smalls):
    if packed.shape[2] % 16:
        packed = even_units(packed, sections)
    chips, _, unit, wide = packed.shape
    group = 8
    specs, shapes = [], []
    for at, width, turned in outs:
        step = group * unit * sections[at][2]
        height = chips * unit * sections[at][2]
        if turned:
            specs.append(pl.BlockSpec((turned, step), lambda i: (0, i)))
            shapes.append(jax.ShapeDtypeStruct((turned, height), F32))
        else:
            specs.append(pl.BlockSpec((step, width), lambda i: (i, 0)))
            shapes.append(jax.ShapeDtypeStruct((height, width), F32))
    return pl.pallas_call(
        functools.partial(unpack_kernel, sections, pieces, talls, smalls),
        grid=(chips // group,),
        in_specs=[pl.BlockSpec((group, 2, unit, wide), lambda i: (i, 0, 0, 0))],
        out_specs=specs,
        out_shape=shapes,
        compiler_params=pltpu.CompilerParams(vmem_limit_bytes=VMEM_BYTES),
        cost_estimate=pl.CostEstimate(
            flops=0, bytes_accessed=12 * chips * unit * wide, transcendentals=0
        ),
        name="unpack_sums",
    )(packed)


AXES = ("clip", "band")


def partner_pairs(total, mask):
    return [(i, i ^ mask) for i in range(total)]


def add_low(*parts):
    return sum(part.astype(F32) for part in parts).astype(BF16)


class RunningSum:
    def __init__(self, keep, give, total):
        bits = total.bit_length() - 1
        self.total = total
        self.cut = keep.shape[1] // 256 * 128
        rows = keep.shape[0] // (total // 2)
        self.shape = (2,) * (bits - 1) + (rows, keep.shape[1])
        self.keep = [keep]
        self.got = [lax.ppermute(give, AXES, partner_pairs(total, 1))]
        self.left = [list(range(bits - 1, 0, -1))]
        self.plan = [[[2], [1]], [[1], [2]]]
        rest = list(range(3, bits))
        while rest:
            self.plan.append([rest[:2]])
            rest = rest[2:]

    def settle(self):
        each = len(self.got) // len(self.keep)
        self.held = [
            add_low(keep, *self.got[i * each : (i + 1) * each]) for i, keep in enumerate(self.keep)
        ]
        if self.shape:
            self.held, self.shape = [self.held[0].reshape(self.shape)], None

    def offers(self):
        self.settle()
        me = lax.axis_index(AXES)
        groups = self.plan[0]
        if len(groups) > len(self.held):
            (held,), (left,) = self.held, self.left
            self.held = [held[..., : self.cut], held[..., self.cut :]]
            self.left = [list(left), list(left)]
        if len(groups) < len(self.held):
            self.held = [jnp.concatenate(self.held, axis=-1)]
            self.left = self.left[:1]
        self.keep, gives, self.masks = [], [], []
        for held, left, group in zip(self.held, self.left, groups):
            low, ways = group[0], 1 << len(group)
            place = left.index(group[-1])
            mine = (me >> low) & (ways - 1)
            shape = held.shape
            held = held.reshape(shape[:place] + (ways,) + shape[place + len(group) :])
            self.keep.append(lax.dynamic_index_in_dim(held, mine, place, keepdims=False))
            for k in range(1, ways):
                gives.append(lax.dynamic_index_in_dim(held, mine ^ k, place, keepdims=False))
                self.masks.append(k << low)
            for bit in group:
                left.remove(bit)
        return gives

    def deliver(self, gives):
        self.got = [
            lax.ppermute(give, AXES, partner_pairs(self.total, mask))
            for give, mask in zip(gives, self.masks)
        ]
        self.plan = self.plan[1:]

    def finish(self):
        while self.plan:
            self.deliver(self.offers())
        self.settle()
        return jnp.concatenate(self.held, axis=-1)


class RunningGather:
    def __init__(self, shard, total):
        bits = total.bit_length() - 1
        self.total = total
        self.cut = (shard.shape[1] + LANES) // 256 * 128
        self.shape = shard.shape
        rest, self.plan = list(range(3, bits)), []
        while rest:
            self.plan.append([rest[:2]])
            rest = rest[2:]
        self.plan += [[[1], [2]], [[2], [1]], [[0]]]
        self.held, self.have = [shard], [[]]

    def offers(self):
        groups = self.plan[0]
        if len(groups) > len(self.held):
            (held,), (have,) = self.held, self.have
            self.held = [held[..., : self.cut], held[..., self.cut :]]
            self.have = [list(have), list(have)]
        if len(groups) < len(self.held):
            self.held = [jnp.concatenate(self.held, axis=-1)]
            self.have = self.have[:1]
        gives, self.masks = [], []
        for held, group in zip(self.held, groups):
            for k in range(1, 1 << len(group)):
                gives.append(held)
                self.masks.append(k << group[0])
        return gives

    def deliver(self, gives):
        me = lax.axis_index(AXES)
        got = [
            lax.ppermute(give, AXES, partner_pairs(self.total, mask))
            for give, mask in zip(gives, self.masks)
        ]
        each = len(got) // len(self.held)
        for i, group in enumerate(self.plan[0]):
            parts = [self.held[i]] + got[i * each : (i + 1) * each]
            for b, bit in enumerate(group):
                flip = ((me >> bit) & 1) == 1
                parts = [jnp.where(flip, parts[k ^ (1 << b)], part) for k, part in enumerate(parts)]
            self.have[i] = sorted(self.have[i] + group, reverse=True)
            at = self.have[i].index(group[-1])
            held = jnp.stack(parts, axis=at)
            self.held[i] = held.reshape(held.shape[:at] + (2,) * len(group) + held.shape[at + 1 :])
        self.plan = self.plan[1:]

    def finish(self):
        while self.plan:
            self.deliver(self.offers())
        return self.held[0].reshape((self.total,) + self.shape)


def together(*groups):
    return lax.optimization_barrier(groups)


def gather_rows(shard):
    return lax.all_gather(shard, AXES, axis=0, tiled=True)


def columns_of(vectors):
    block = jnp.stack(vectors, axis=1)
    return jnp.pad(block, ((0, 0), (0, LANES - len(vectors))))


def blocks_beside(tall, rows):
    return [tall[i : i + rows] for i in range(0, tall.shape[0], rows)]


def blocks_below(beside, total, width):
    rows = beside.shape[0] // total
    count = beside.shape[1] // width
    parts = [beside[:, i * width : (i + 1) * width].reshape(total, rows, width) for i in range(count)]
    return jnp.concatenate(parts, axis=1)


def swap_band(array, bit):
    return lax.ppermute(array, "band", [(i, i ^ bit) for i in range(4)])


def owners_to_bands(own, other):
    band = lax.axis_index("band")
    half, side = band // 2, band % 2
    got = swap_band(other, 2)
    pair = jnp.stack([jnp.where(half == 0, own, got), jnp.where(half == 0, got, own)])
    other = swap_band(pair, 1)
    return jnp.stack([jnp.where(side == 0, pair, other), jnp.where(side == 0, other, pair)], axis=1)


def bands_to_owners(pair):
    half = lax.axis_index("band") // 2
    own = lax.dynamic_index_in_dim(pair, half, 0, keepdims=False)
    got = swap_band(lax.dynamic_index_in_dim(pair, 1 - half, 0, keepdims=False), 2)
    return jnp.stack([jnp.where(half == 0, own, got), jnp.where(half == 0, got, own)])


def position_table(places):
    half_width = D_DEC // 2
    omega_vec = jnp.exp(
        jnp.arange(half_width, dtype=F32) * (-math.log(10000.0) / half_width)
    )
    angles = places.astype(F32)[..., None] * omega_vec
    return jnp.concatenate([jnp.sin(angles), jnp.cos(angles)], axis=-1)


def shards(
    visible,
    keep_index,
    visible_count,
    enc_gain1,
    enc_shift1,
    enc_qkv,
    enc_out,
    enc_gain2,
    enc_shift2,
    enc_up,
    enc_down,
    proj,
    mask_token,
    dec_gain1,
    dec_shift1,
    dec_qkv,
    dec_out,
    dec_gain2,
    dec_shift2,
    dec_up,
    dec_down,
    cotangent,
):
    total = lax.axis_size(AXES)
    enc_wide, dec_wide = enc_out.shape[1], dec_out.shape[1]
    enc_ff, dec_ff = enc_up.shape[1], dec_up.shape[1]
    core = (lax.axis_index(AXES) % 2).reshape(1)
    enc_small = columns_of([enc_gain1, enc_shift1, enc_gain2, enc_shift2])
    enc_pack = gather_rows(jnp.concatenate([enc_qkv, enc_out, enc_up, proj, enc_small], axis=1))
    down_run = RunningGather(enc_down, total)
    while len(down_run.plan) > 3:
        down_run.deliver(down_run.offers())

    clip_count, slot_total, _ = visible.shape
    half_clips = clip_count // 2
    band_height = FREQ // 2
    slot_ids = jnp.arange(slot_total)
    valid_rows = slot_ids[None, :] < visible_count[:, None]
    valid_mask = valid_rows.astype(F32)[:, None, :]
    cell_number = jnp.where(valid_rows, keep_index, -1).reshape(2, half_clips, slot_total)
    half = lax.axis_index("band") // 2
    own = lax.dynamic_index_in_dim(cell_number, half, 0, keepdims=False)
    other = lax.dynamic_index_in_dim(cell_number, 1 - half, 0, keepdims=False)
    cell_number = owners_to_bands(own, other).reshape(-1, slot_total)

    dec_small = columns_of([dec_gain1, dec_shift1, dec_gain2, dec_shift2, mask_token])
    dec_tall = blocks_beside(dec_down, dec_out.shape[0])
    dec_pack = jnp.concatenate([dec_qkv, dec_out, dec_up] + dec_tall + [dec_small], axis=1)
    dec_run = RunningGather(dec_pack, total)
    cell_number, gives, dec_gives = together(cell_number, down_run.offers(), dec_run.offers())
    down_run.deliver(gives)
    dec_run.deliver(dec_gives)
    while len(dec_run.plan) > 3:
        dec_run.deliver(dec_run.offers())
    down_run.deliver(down_run.offers())
    gives, dec_gives = together(down_run.offers(), dec_run.offers())
    down_run.deliver(gives)
    dec_run.deliver(dec_gives)
    whole_down = down_run.finish().reshape(-1, enc_wide)
    enc_pack, whole_down, gives = together(enc_pack, whole_down, dec_run.offers())
    dec_run.deliver(gives)

    band_pick = lax.axis_index("band") % 2
    rolled_time = (cell_number // FREQ + TIME - SHIFT) % TIME
    rolled_freq = (cell_number % FREQ + FREQ - SHIFT) % FREQ
    here = (cell_number >= 0) & (rolled_freq // band_height == band_pick)
    arrived_index = jnp.where(here, rolled_time * band_height + rolled_freq % band_height, -1)

    blocks = enc_blocks(enc_pack, enc_wide, enc_ff, dec_wide)
    qkv, probs, mixed, middle, vecs = enc_attend(visible, valid_mask, blocks)
    own, other, encoded, hidden, slope = enc_feed(
        half.reshape(1), middle, vecs, blocks, whole_down
    )
    own, other, gives = together(own, other, dec_run.offers())
    dec_run.deliver(gives)
    dec_pack = dec_run.finish().reshape(-1, dec_pack.shape[1])
    dec_end = 4 * dec_wide + dec_ff
    dec_whole_down = blocks_below(dec_pack[:, dec_end : dec_end + dec_ff], total, dec_wide)
    dec_whole_down = dec_whole_down.reshape(-1, dec_wide)
    parted = (half_clips, slot_total, dec_wide)
    arrived_rows = owners_to_bands(own.reshape(parted), other.reshape(parted))
    half_total = 4 * half_clips

    cell_count = TIME * band_height
    places = jnp.arange(cell_count)
    cell_freq = band_pick * band_height + places % band_height
    patch_number = (places // band_height + SHIFT) % TIME * FREQ + (cell_freq + SHIFT) % FREQ
    span = D_DEC // HEADS_DEC
    query = places[:, None]
    key = query // span * span + jnp.arange(LANES)[None, :] % span

    def label(cell):
        late = cell // band_height >= TIME - SHIFT
        high = band_pick * band_height + cell % band_height >= FREQ - SHIFT
        return late.astype(jnp.int32) * 2 + high.astype(jnp.int32)

    cells_in = WINDOW * WINDOW
    allowed = (query // cells_in == key // cells_in) & (label(query) == label(key))
    decoded, own, other, keep, give = decoder_block(
        core,
        arrived_rows.reshape(half_total, slot_total, dec_wide),
        arrived_index,
        cotangent.reshape(half_total, cell_count, dec_wide),
        position_table(patch_number),
        allowed.astype(F32),
        dec_pack,
        dec_whole_down,
    )
    decoded_out = decoded.reshape(cotangent.shape)

    returning = (own + swap_band(other, 1)).reshape(2, half_clips, slot_total, dec_wide)
    returning, keep, give = together(returning, keep, give)
    dec_run = RunningSum(keep, give, total)
    grad_sent = bands_to_owners(returning).reshape(-1, dec_wide)
    grad_sent, gives = together(grad_sent, dec_run.offers())
    dec_run.deliver(gives)
    g_proj, keep, give, grad_middle, g_vec = enc_feed_back(
        core, grad_sent, encoded, hidden, slope, middle, vecs, blocks, whole_down
    )
    keep, give, grad_middle, gives = together(keep, give, grad_middle, dec_run.offers())
    dec_run.deliver(gives)
    feed_run = RunningSum(keep, give, total)
    keep, give, grad_visible = enc_attend_back(
        core, grad_middle, mixed, qkv, probs, visible, vecs, blocks, g_proj, g_vec
    )
    keep, give, dec_run.got, feed_run.got = together(keep, give, dec_run.got, feed_run.got)
    attend_run = RunningSum(keep, give, total)
    feed_gives, dec_run.got, attend_run.got = together(
        feed_run.offers(), dec_run.got, attend_run.got
    )
    feed_run.deliver(feed_gives)
    dec_run.deliver(dec_run.offers())
    dec_shard, feed_gives = together(dec_run.finish(), feed_run.offers())
    feed_run.deliver(feed_gives)
    feed_gives, gives = together(feed_run.offers(), attend_run.offers())
    feed_run.deliver(feed_gives)
    attend_run.deliver(gives)
    feed_shard = feed_run.finish()
    feed_shard, gives = together(feed_shard, attend_run.offers())
    unit = dec_shard.shape[0] // 2
    dec_units = [dec_shard[k * unit : (k + 1) * unit] for k in range(2)]
    feed_units = [feed_shard[k * unit : (k + 1) * unit] for k in range(3)]
    most_sum = gather_rows(jnp.concatenate(dec_units + feed_units, axis=1))
    attend_run.deliver(gives)
    attend_shard = attend_run.finish()
    attend_sum = RunningGather(attend_shard, total).finish()

    half = attend_shard.shape[1]
    tail = 3 * enc_wide - half
    e_qkv, e_out, e_proj, enc_vecs = unpack_sums(
        attend_sum.reshape((total // 2, 2) + attend_shard.shape),
        ((0, half, 1),),
        ((0, 3 * enc_wide, 0), (0, enc_wide, 0), (0, dec_wide, 0), (0, 0, 8)),
        (
            (0, 0, (0, 0), 0, half),
            (0, half, (0, 1), 0, tail),
            (1, 0, (0, 1), tail, enc_wide),
            (2, 0, (0, 1), tail + enc_wide, dec_wide),
        ),
        (),
        ((3, (0, 1), tail + enc_wide + dec_wide),),
    )
    half = dec_ff // 2
    dec_half = dec_shard.shape[1]
    d_qkv, d_out, d_up, d_down, dec_vecs, e_up, e_down = unpack_sums(
        most_sum.reshape(total // 2, 2, unit, most_sum.shape[1]),
        ((0, dec_half, 2), (2 * dec_half, enc_ff, 3)),
        (
            (0, 3 * dec_wide, 0),
            (0, dec_wide, 0),
            (0, dec_ff, 0),
            (0, 0, dec_ff),
            (0, 0, 8),
            (1, enc_ff, 0),
            (1, 0, enc_ff),
        ),
        (
            (0, 0, (0, 0), 0, 3 * dec_wide),
            (1, 0, (0, 0), 3 * dec_wide, dec_wide),
            (2, 0, (0, 0), 4 * dec_wide, half),
            (2, half, (0, 1), 0, half),
            (5, 0, (1, 0), 0, enc_ff),
        ),
        ((3, (0, 1), half, dec_ff), (6, (1, 1), 0, enc_ff)),
        ((4, (0, 0), 4 * dec_wide + half),),
    )
    return (
        decoded_out,
        grad_visible,
        enc_vecs[0],
        enc_vecs[1],
        e_qkv,
        e_out,
        enc_vecs[2],
        enc_vecs[3],
        e_up,
        e_down,
        e_proj,
        dec_vecs[4],
        dec_vecs[0],
        dec_vecs[1],
        d_qkv,
        d_out,
        dec_vecs[2],
        dec_vecs[3],
        d_up,
        d_down,
    )


def solution(mesh):
    return jax.shard_map(
        shards,
        mesh=mesh,
        in_specs=(
            P(("clip", "band"), None, None),
            P(("clip", "band"), None),
            P(("clip", "band")),
            P(("clip", "band")),
            P(("clip", "band")),
            P(("clip", "band"), None),
            P(("clip", "band"), None),
            P(("clip", "band")),
            P(("clip", "band")),
            P(("clip", "band"), None),
            P(("clip", "band"), None),
            P(("clip", "band"), None),
            P(("clip", "band")),
            P(("clip", "band")),
            P(("clip", "band")),
            P(("clip", "band"), None),
            P(("clip", "band"), None),
            P(("clip", "band")),
            P(("clip", "band")),
            P(("clip", "band"), None),
            P(("clip", "band"), None),
            P(("clip", "band"), None, None, None, None),
        ),
        out_specs=(
            P(("clip", "band"), None, None, None, None),
            P(("clip", "band"), None, None),
            P(),
            P(),
            P(),
            P(),
            P(),
            P(),
            P(),
            P(),
            P(),
            P(),
            P(),
            P(),
            P(),
            P(),
            P(),
            P(),
            P(),
            P(),
        ),
        check_vma=False,
    )
```
